256 devices in a mesh: lon: 64 (over x, z, y_hi), lat: 4 (over y_lo, core).
Axes of the slice: x: 4, y: 4 (y_hi: 2, y_lo: 2; y = y_hi * 2 + y_lo), z: 8, core: 2. Of those that a mesh axis runs over, the one named last changes fastest.
Arguments:
- features: bfloat16 [32, 8192, 256], P('lat', 'lon'), may hold values from -8 to 8
- conv_weight: bfloat16 [3, 3, 256, 256], replicated, may hold values from -0.125 to 0.125
- down_weight: bfloat16 [3, 3, 256, 256], replicated, may hold values from -0.125 to 0.125
- norm_gain: float32 [256], replicated, may hold values from 0.1 to 1.9
- norm_bias: float32 [256], replicated, may hold values from -3 to 3
- cotangent: bfloat16 [16, 4096, 256], P('lat', 'lon'), may hold values from -8 to 8
Outputs:
- output: bfloat16 [16, 4096, 256], P('lat', 'lon')
- input_grad: bfloat16 [32, 8192, 256], P('lat', 'lon')
- conv_grad: float32 [3, 3, 256, 256], replicated
- down_grad: float32 [3, 3, 256, 256], replicated
- gain_grad: float32 [256], replicated
- bias_grad: float32 [256], replicated
The draws below stay inside these ranges and needn't reach their ends.
All inputs are finite; a program needn't handle non-finite values.
Results may differ from the reference program's by a relative error of at most 0.015.
Values may be sent and summed in bfloat16 or wider, within the bound.
No kernel may reach another device: no remote copies, remote signals or barrier semaphores. Data moves between devices by JAX's collectives and lax.ppermute only.
A program may use at most 64 MiB of HBM per device.

```python
import math
import jax
import jax.numpy as jnp
from jax import lax

C = 256
GROUPS = 32
NLAT = 32
NLON = 8192
OLAT = 16
OLON = 4096


def rough_field(key, rows, cols, chans, tilt, lift, floor):
    key_base, key_rough, key_sign = jax.random.split(key, 3)
    base = jax.random.normal(key_base, (rows, cols, chans), jnp.float32)
    rough = jnp.exp(jax.random.uniform(key_rough, (rows, cols, chans), jnp.float32, math.log(0.5), math.log(1.5)))
    signs = jax.random.normal(key_sign, (chans,), jnp.float32)
    across = jnp.arange(cols, dtype=jnp.float32) / cols
    along = jnp.arange(rows, dtype=jnp.float32) / rows
    scale = (0.5 + across)[None, :, None] * (1.0 + tilt * along)[:, None, None]
    offset = lift * (floor + across)[None, :, None] * signs[None, None, :]
    return jnp.clip(base * rough * scale + offset, -8.0, 8.0)


def draw_features(key, part):
    key = jax.random.fold_in(key, 11)
    field = rough_field(key, NLAT, NLON, C, 0.0, 1.0, 0.5)
    return field.astype(jnp.bfloat16)


def draw_cotangent(key, part):
    key = jax.random.fold_in(key, 23)
    field = rough_field(key, OLAT, OLON, C, 0.0, 0.0, 0.5)
    return field.astype(jnp.bfloat16)


def scatter_about(key, extent, scale, reach, kind=jnp.bfloat16):
    return jnp.clip(scale * jax.random.normal(key, extent, jnp.float32), -reach, reach).astype(kind)


def setup_inputs(seed: int = 0) -> dict:
    streams_of = jax.random.split(jax.random.key(seed), 7)
    return {
        "features": draw_features(jax.random.fold_in(streams_of[6], 71), 0),
        "conv_weight": scatter_about(streams_of[1], (3, 3, C, C), (9 * C) ** -0.5, 0.125),
        "down_weight": scatter_about(streams_of[2], (3, 3, C, C), (9 * C) ** -0.5, 0.125),
        "norm_gain": jnp.clip(1.0 + 0.18 * jax.random.normal(streams_of[3], (C,), jnp.float32), 0.1, 1.9),
        "norm_bias": scatter_about(streams_of[4], (C,), 0.5, 3.0, jnp.float32),
        "cotangent": draw_cotangent(jax.random.fold_in(streams_of[6], 71), 0),
    }


EPS = 1e-05

def pad_rim(field):
    wrapped = jnp.concatenate([field[:, -1:], field, field[:, :1]], axis=1)
    zero_row = jnp.zeros((1,) + wrapped.shape[1:], wrapped.dtype)
    return jnp.concatenate([zero_row, wrapped, zero_row], axis=0)

def conv_taps(padded, weight, rows, cols, step):
    chans = padded.shape[2]
    total = jnp.zeros((rows * cols, weight.shape[3]), jnp.float32)
    for tap_a in range(3):
        for tap_b in range(3):
            piece = padded[tap_a:tap_a + step * rows:step, tap_b:tap_b + step * cols:step]
            piece = piece.reshape(rows * cols, chans)
            total = total + jnp.dot(piece, weight[tap_a, tap_b], preferred_element_type=jnp.float32)
    return total.reshape(rows, cols, -1)

def tap_grads(padded, grad, rows, cols, step):
    chans = padded.shape[2]
    flat_grad = grad.reshape(rows * cols, grad.shape[2])
    results = []
    for tap_a in range(3):
        for tap_b in range(3):
            piece = padded[tap_a:tap_a + step * rows:step, tap_b:tap_b + step * cols:step]
            piece = piece.reshape(rows * cols, chans)
            results.append(lax.dot_general(piece, flat_grad, (((0,), (0,)), ((), ())), preferred_element_type=jnp.float32))
    return jnp.stack(results).reshape(3, 3, chans, grad.shape[2])

def conv_data_grad(padded_grad, weight, rows, cols):
    chans = padded_grad.shape[2]
    total = jnp.zeros((rows * cols, weight.shape[2]), jnp.float32)
    for tap_a in range(3):
        for tap_b in range(3):
            piece = padded_grad[2 - tap_a:2 - tap_a + rows, 2 - tap_b:2 - tap_b + cols].reshape(rows * cols, chans)
            total = total + lax.dot_general(piece, weight[tap_a, tap_b], (((1,), (1,)), ((), ())), preferred_element_type=jnp.float32)
    return total.reshape(rows, cols, -1)

def down_back(grad, weight, rows, cols):
    flat_grad = grad.reshape(rows * cols, grad.shape[2])
    total = jnp.zeros((2 * rows + 1, 2 * cols + 1, weight.shape[2]), jnp.float32)
    for tap_a in range(3):
        for tap_b in range(3):
            term = lax.dot_general(flat_grad, weight[tap_a, tap_b], (((1,), (1,)), ((), ())), preferred_element_type=jnp.float32)
            term = term.reshape(rows, cols, -1)
            total = total + lax.pad(term, jnp.zeros((), term.dtype), ((tap_a, 2 - tap_a, 1), (tap_b, 2 - tap_b, 1), (0, 0, 0)))
    return total

def group_total(vector):
    return vector.reshape(GROUPS, -1).sum(axis=1)

def reference(features, conv_weight, down_weight, norm_gain, norm_bias, cotangent):
    width = C // GROUPS
    cells = NLAT * NLON
    count = cells * width
    framed = pad_rim(features)
    hidden = conv_taps(framed, conv_weight, NLAT, NLON, 1).astype(jnp.bfloat16)
    wide = hidden.astype(jnp.float32)
    mean = jnp.repeat(group_total(lax.optimization_barrier(jnp.sum(wide, axis=(0, 1)))) / count, width)
    centered = wide - mean
    var_g = group_total(lax.optimization_barrier(jnp.sum(centered * centered, axis=(0, 1)))) / count
    inverse = jnp.repeat(lax.rsqrt(var_g + EPS), width)
    normed = centered * inverse
    shifted = norm_gain * normed + norm_bias
    sigma = jax.nn.sigmoid(shifted)
    active = (shifted * sigma).astype(jnp.bfloat16)
    with_col = jnp.concatenate([active[:, -1:], active], axis=1)
    padded_act = jnp.concatenate([jnp.zeros((1,) + with_col.shape[1:], jnp.bfloat16), with_col], axis=0)
    output = conv_taps(padded_act, down_weight, OLAT, OLON, 2).astype(jnp.bfloat16)
    down_part = tap_grads(padded_act, cotangent, OLAT, OLON, 2)
    frame = down_back(cotangent, down_weight, OLAT, OLON)
    act_grad = frame[1:, 1:].at[:, NLON - 1].add(frame[1:, 0]).astype(jnp.bfloat16)
    pre = act_grad.astype(jnp.float32) * sigma * (1.0 + shifted * (1.0 - sigma))
    bias_sum = lax.optimization_barrier(jnp.sum(pre, axis=(0, 1)))
    gain_sum = lax.optimization_barrier(jnp.sum(pre * normed, axis=(0, 1)))
    first = jnp.repeat(group_total(norm_gain * bias_sum) / count, width)
    second = jnp.repeat(group_total(norm_gain * gain_sum) / count, width)
    hidden_grad = (inverse * (norm_gain * pre - first - normed * second)).astype(jnp.bfloat16)
    input_grad = conv_data_grad(pad_rim(hidden_grad), conv_weight, NLAT, NLON).astype(jnp.bfloat16)
    conv_part = tap_grads(framed, hidden_grad, NLAT, NLON, 1)
    factor = 1.0 / math.sqrt(cells)
    return (output, input_grad, conv_part * factor, down_part * factor, gain_sum * factor, bias_sum * factor)
```

```python
import functools
import math

import jax
import jax.numpy as jnp
from jax import lax
from jax.experimental import pallas as pl
from jax.experimental.pallas import tpu as pltpu
from jax.sharding import Mesh
from jax.sharding import PartitionSpec as P

EPS = 1e-05
WIDTH = 8
J = 80
LON = ("x", "z", "y_hi")
LAT = ("y_lo", "core")
PLANE = ("x", "y_hi", "y_lo")
ALL = LON + LAT
BF = jnp.bfloat16
F32 = jnp.float32


def call(body, outs, scratch=(), flops=0, smem=(), n_in=0):
    specs = [
        pl.BlockSpec(memory_space=pltpu.SMEM) if i in smem else pl.BlockSpec(memory_space=pltpu.VMEM)
        for i in range(n_in)
    ]
    return pl.pallas_call(
        body,
        out_shape=[jax.ShapeDtypeStruct(s, d) for s, d in outs],
        in_specs=specs,
        out_specs=[pl.BlockSpec(memory_space=pltpu.VMEM)] * len(outs),
        scratch_shapes=[pltpu.VMEM(s, d) for s, d in scratch],
        compiler_params=pltpu.CompilerParams(vmem_limit_bytes=40 * 1024 * 1024),
        cost_estimate=pl.CostEstimate(flops=flops, bytes_accessed=1 << 20, transcendentals=0),
    )


def dot(a, b):
    return jnp.dot(a, b, preferred_element_type=F32)


def dot_t(a, b):
    return lax.dot_general(a, b, (((1,), (1,)), ((), ())), preferred_element_type=F32)


def t_dot(a, b):
    return lax.dot_general(a, b, (((0,), (0,)), ((), ())), preferred_element_type=F32)


def exact(a, b):
    a8 = jnp.broadcast_to(a, (8, a.shape[1]))
    return jnp.dot(a8, b, preferred_element_type=F32, precision=lax.Precision.HIGHEST)[0:1]


def to_lanes(chans, shift):
    c = lax.broadcasted_iota(jnp.int32, (chans, 128), 0) // WIDTH
    l = lax.broadcasted_iota(jnp.int32, (chans, 128), 1)
    return (c + shift == l).astype(F32)


def from_lanes(chans, shift):
    c = lax.broadcasted_iota(jnp.int32, (128, chans), 1) // WIDTH
    l = lax.broadcasted_iota(jnp.int32, (128, chans), 0)
    return (c + shift == l).astype(F32)


def masks():
    j = lax.broadcasted_iota(jnp.int32, (J, 1), 0)
    odd = jnp.where((j >= 1) & (j <= 64), 1.0, 0.0)
    even = jnp.where(j <= 63, 1.0, 0.0)
    return odd, even


def pack_lon(feat, cot, east, west):
    rows, cols, _ = feat.shape
    half = cot.shape[0]
    east[0:rows] = feat[:, cols - 16 : cols]
    east[rows : rows + half] = cot[:, cot.shape[1] - 16 :]
    west[0:rows] = feat[:, 0:16]
    west[rows : rows + half] = cot[:, 0:16]


def pack_lat(feat, cot, west, east, south, north):
    rows, cols, _ = feat.shape
    half, pairs, _ = cot.shape
    for dest, top, mid in ((south, rows - 2, half - 1), (north, 0, 0)):
        for k in range(2):
            o = k * (cols + 32)
            dest[o : o + 16] = west[top + k]
            dest[o + 16 : o + 16 + cols] = feat[top + k]
            dest[o + 16 + cols : o + 32 + cols] = east[top + k]
        o = 2 * (cols + 32)
        dest[o : o + 16] = west[rows + mid]
        dest[o + 16 : o + 16 + pairs] = cot[mid]
        dest[o + 16 + pairs : o + 32 + pairs] = east[rows + mid]


def conv_kernel(devices, feat, west, east, north, south, w, x_out, hq_out, he_out, stat_out, f32s):
    rows, cols, chans = feat.shape
    wide = cols + 32
    f32s[:, :, wide : wide + 16] = jnp.zeros((rows + 4, 2, 16, 128), F32)
    for v in range(2):
        part = slice(v * 128, v * 128 + 128)
        for k in range(2):
            f32s[k, v, 0:wide] = north[k * wide : (k + 1) * wide, part].astype(F32)
            f32s[rows + 2 + k, v, 0:wide] = south[k * wide : (k + 1) * wide, part].astype(F32)
        f32s[2 : rows + 2, v, 0:16] = west[0:rows, :, part].astype(F32)
        f32s[2 : rows + 2, v, 16 : 16 + cols] = feat[:, :, part].astype(F32)
        f32s[2 : rows + 2, v, 16 + cols : wide] = east[0:rows, :, part].astype(F32)
        for r in range(rows + 4):
            for k in range(4):
                lane = k * chans + v * 128
                x_out[r, :, lane : lane + 128] = f32s[r, v, pl.ds(14 + k, J, stride=2), :].astype(BF)
    odd, even = masks()
    sums = jnp.zeros((1, chans), F32)
    for out, lo in ((hq_out, 0), (he_out, chans)):
        acc = None
        for a in range(3):
            lhs = x_out[a : a + rows + 2, :, lo : lo + 3 * chans].reshape((rows + 2) * J, 3 * chans)
            term = dot(lhs, w[a])
            acc = term if acc is None else acc + term
        out[...] = acc.astype(BF).reshape(rows + 2, J, chans)
    for out, mask in ((hq_out, odd), (he_out, even)):
        part = jnp.zeros((J, chans), F32)
        for r in range(1, rows + 1):
            part = part + out[r].astype(F32)
        sums = sums + jnp.sum(part * mask, axis=0, keepdims=True)
    lanes = to_lanes(chans, 0)
    means = exact(sums, lanes) / (rows * cols * WIDTH)
    mean = exact(means, from_lanes(chans, 0))
    squares = jnp.zeros((1, chans), F32)
    for out, mask in ((hq_out, odd), (he_out, even)):
        part = jnp.zeros((J, chans), F32)
        for r in range(1, rows + 1):
            d = out[r].astype(F32) - mean
            part = part + d * d
        squares = squares + jnp.sum(part * mask, axis=0, keepdims=True)
    stat = means + exact(squares, to_lanes(chans, 32))
    stat_out[...] = jnp.broadcast_to(stat[None], stat_out.shape)


def back_kernel(cot, west, east, north, south, dw, c_out, aq_out, ae_out, f32s):
    half, pairs, chans = cot.shape
    rows = west.shape[0] - half
    wide = pairs + 32
    base = north.shape[0] - wide
    f32s[0, 0:wide] = north[base : base + wide].astype(F32)
    f32s[half + 1, 0:wide] = south[base : base + wide].astype(F32)
    f32s[1 : half + 1, 0:16] = west[rows:].astype(F32)
    f32s[1 : half + 1, 16 : 16 + pairs] = cot[...].astype(F32)
    f32s[1 : half + 1, 16 + pairs : wide] = east[rows:].astype(F32)
    for s in range(half + 2):
        c_out[s, :, 0:chans] = f32s[s, 15 : 15 + J].astype(BF)
        c_out[s, :, chans : 2 * chans] = f32s[s, 16 : 16 + J].astype(BF)
    n = half + 1
    lo_l = c_out[0:n, :, 0:chans].reshape(n * J, chans)
    lo_r = c_out[0:n, :, chans:].reshape(n * J, chans)
    hi_l = c_out[1 : n + 1, :, 0:chans].reshape(n * J, chans)
    hi_r = c_out[1 : n + 1, :, chans:].reshape(n * J, chans)

    def put(out, k, value):
        value = value.astype(BF).reshape(n, J, chans)
        for i in range(n):
            out[2 * i + k] = value[i]

    put(ae_out, 1, dot_t(hi_r, dw[1, 1]))
    put(aq_out, 1, dot_t(hi_r, dw[1, 0]) + dot_t(hi_l, dw[1, 2]))
    put(ae_out, 0, dot_t(hi_r, dw[0, 1]) + dot_t(lo_r, dw[2, 1]))
    put(
        aq_out,
        0,
        dot_t(hi_r, dw[0, 0]) + dot_t(hi_l, dw[0, 2]) + dot_t(lo_r, dw[2, 0]) + dot_t(lo_l, dw[2, 2]),
    )


def act_kernel(cells, flags, stats, hq, he, aq, ae, gain, bias, t_out, pq_out, pe_out, coef_out, sum_out, f32s):
    devices = stats.shape[0]
    rows = hq.shape[0] - 2
    chans = hq.shape[2]
    local_n = float(cells // devices * WIDTH)
    count = float(cells * WIDTH)
    rec = stats[...]
    total = jnp.sum(rec, axis=0)
    centre = total / devices
    dev = rec - centre[None]
    spread = jnp.sum(dev * dev, axis=0)
    mean = exact(centre, from_lanes(chans, 0))
    var = (exact(total, from_lanes(chans, 32)) + local_n * exact(spread, from_lanes(chans, 0))) / count
    inverse = lax.rsqrt(var + EPS)
    coef_out[0:1] = mean
    coef_out[1:2] = inverse
    g = gain[...]
    b = bias[...]
    odd, even = masks()
    top = jnp.where(flags[0] == 1, 0.0, 1.0)
    bias_sum = jnp.zeros((1, chans), F32)
    gain_sum = jnp.zeros((1, chans), F32)
    for h, a, p_out, mask, is_q in ((hq, aq, pq_out, odd, True), (he, ae, pe_out, even, False)):
        acc_b = jnp.zeros((J, chans), F32)
        acc_g = jnp.zeros((J, chans), F32)
        for r in range(rows + 2):
            normed = (h[r].astype(F32) - mean) * inverse
            shifted = g * normed + b
            sigma = jax.nn.sigmoid(shifted)
            pre = a[r].astype(F32) * sigma * (1.0 + shifted * (1.0 - sigma))
            p_out[r] = pre
            if 1 <= r <= rows:
                acc_b = acc_b + pre
                acc_g = acc_g + pre * normed
            if r <= rows:
                active = shifted * sigma
                if r == 0:
                    active = active * top
                if is_q:
                    f32s[...] = active.astype(BF).astype(F32)
                    t_out[r, :, 0:chans] = active[0:64].astype(BF)
                    t_out[r, :, 2 * chans :] = f32s[1:65].astype(BF)
                else:
                    t_out[r, :, chans : 2 * chans] = active[0:64].astype(BF)
        bias_sum = bias_sum + jnp.sum(acc_b * mask, axis=0, keepdims=True)
        gain_sum = gain_sum + jnp.sum(acc_g * mask, axis=0, keepdims=True)
    payload = jnp.concatenate(
        [bias_sum[:, 0:128], bias_sum[:, 128:256], gain_sum[:, 0:128], gain_sum[:, 128:256]], axis=0
    )
    sum_out[...] = jnp.broadcast_to(payload[None], sum_out.shape)


def down_kernel(t, c, dw, out, grad):
    half = out.shape[0]
    pairs, chans = out.shape[1:]
    cot = c[1 : half + 1, 0:pairs, chans:].reshape(half * pairs, chans)
    acc = None
    for a in range(3):
        lhs = jnp.concatenate([t[2 * i + a] for i in range(half)], axis=0)
        term = dot(lhs, dw[a])
        acc = term if acc is None else acc + term
        grad[a] = t_dot(lhs, cot)
    out[...] = acc.astype(BF).reshape(out.shape)


def grad_kernel(cells, flags, sums, coef, hq, he, pq, pe, gain, x, h4_out, conv_out, vec_out, f32s, rq, re):
    rows = hq.shape[0] - 2
    chans = hq.shape[2]
    count = float(cells * WIDTH)
    total = jnp.sum(sums[...], axis=0)
    bias_sum = jnp.concatenate([total[0:1], total[1:2]], axis=1)
    gain_sum = jnp.concatenate([total[2:3], total[3:4]], axis=1)
    factor = 1.0 / math.sqrt(cells)
    vec_out[0:1] = gain_sum * factor
    vec_out[1:2] = bias_sum * factor
    g = gain[...]
    lanes, back = to_lanes(chans, 0), from_lanes(chans, 0)
    first = exact(exact(g * bias_sum, lanes), back) / count
    second = exact(exact(g * gain_sum, lanes), back) / count
    mean = coef[0:1]
    inverse = coef[1:2]
    top = jnp.where(flags[0] == 1, 0.0, 1.0)
    bottom = jnp.where(flags[1] == 1, 0.0, 1.0)
    odd, even = masks()
    zero = jnp.zeros((J, chans), BF)
    for h, p, r_out, mask, is_q in ((hq, pq, rq, odd, True), (he, pe, re, even, False)):
        for f in (0, 1):
            for a in (1, 2):
                if f - a + 1 <= 0:
                    r_out[f, :, a * chans : (a + 1) * chans] = zero
                    r_out[rows + 1 - f, :, (2 - a) * chans : (3 - a) * chans] = zero
        for r in range(rows + 2):
            normed = (h[r].astype(F32) - mean) * inverse
            value = inverse * (g * p[r] - first - normed * second)
            if r == 0:
                value = value * top
            if r == rows + 1:
                value = value * bottom
            rounded = value.astype(BF)
            if 1 <= r <= rows:
                inner = (value * mask).astype(BF)
                for a in range(3):
                    r_out[r + a - 1, :, a * chans : (a + 1) * chans] = inner
            f32s[...] = rounded.astype(F32)
            moved = f32s[1:65].astype(BF)
            lo = 3 if is_q else 2
            h4_out[r, :, lo * chans : (lo + 1) * chans] = rounded[0:64]
            lo = 1 if is_q else 0
            h4_out[r, :, lo * chans : (lo + 1) * chans] = moved
    m = (rows + 2) * J
    lhs = x[1 : rows + 3].reshape(m, 4 * chans)
    part = t_dot(lhs[:, 0 : 3 * chans], rq[...].reshape(m, 3 * chans))
    part = part + t_dot(lhs[:, chans : 4 * chans], re[...].reshape(m, 3 * chans))
    for a in range(3):
        conv_out[a] = part[:, a * chans : (a + 1) * chans]


def input_kernel(h4, w, out, f32s):
    rows, cols, chans = out.shape
    for k, lo in ((0, 1), (1, 0)):
        acc = None
        for a in range(3):
            for b in range(3):
                lane = (lo + b) * chans
                lhs = h4[2 - a : 2 - a + rows, :, lane : lane + chans].reshape(rows * (cols // 2), chans)
                term = dot_t(lhs, w[a, b])
                acc = term if acc is None else acc + term
        acc = acc.reshape(rows, cols // 2, chans)
        for r in range(rows):
            for v in range(2):
                f32s[r, v, pl.ds(k, cols // 2, stride=2), :] = acc[r, :, v * 128 : v * 128 + 128]
    for v in range(2):
        out[:, :, v * 128 : v * 128 + 128] = f32s[:, v].astype(BF)


def passed(value, axes, step, wrap):
    n = lax.axis_size(axes)
    pairs = [(i, (i + step) % n) for i in range(n) if wrap or 0 <= i + step < n]
    return lax.ppermute(value, axes, pairs)


def local(features, conv_weight, down_weight, norm_gain, norm_bias, cotangent):
    rows, cols, chans = features.shape
    half, pairs, _ = cotangent.shape
    devices = lax.axis_size(ALL)
    lats = lax.axis_size(LAT)
    cells = rows * cols * devices
    lat = lax.axis_index(LAT)
    flags = jnp.stack([lat == 0, lat == lats - 1]).astype(jnp.int32)
    gain = norm_gain.reshape(1, chans)
    bias = norm_bias.reshape(1, chans)
    w3 = conv_weight.reshape(3, 3 * chans, chans)
    dw3 = down_weight.reshape(3, 3 * chans, chans)

    with jax.named_scope("halo"):
        slab = (rows + half, 16, chans)
        to_east, to_west = call(pack_lon, [(slab, BF)] * 2, n_in=2)(features, cotangent)
        west = passed(to_east, LON, 1, True)
        east = passed(to_west, LON, -1, True)
        strip = (2 * (cols + 32) + pairs + 32, chans)
        to_south, to_north = call(pack_lat, [(strip, BF)] * 2, n_in=4)(features, cotangent, west, east)
        north = passed(to_south, LAT, 1, False)
        south = passed(to_north, LAT, -1, False)

    plane = (rows + 2, J, chans)
    with jax.named_scope("conv"):
        x, hq, he, stat = call(
            functools.partial(conv_kernel, devices),
            [((rows + 4, J, 4 * chans), BF), (plane, BF), (plane, BF), ((devices, 1, 128), F32)],
            [((rows + 4, 2, cols + 48, 128), F32)],
            flops=2 * 1600 * 2304 * 256,
            n_in=6,
        )(features, west, east, north, south, w3)
        stats = lax.all_to_all(stat, ALL, 0, 0, tiled=True)
    with jax.named_scope("back"):
        c2, aq, ae = call(
            back_kernel,
            [((half + 2, J, 2 * chans), BF), (plane, BF), (plane, BF)],
            [((half + 2, pairs + 32, chans), F32)],
            flops=2 * 400 * 2304 * 256,
            n_in=6,
        )(cotangent, west, east, north, south, down_weight)
    with jax.named_scope("act"):
        t, pq, pe, coef, sums = call(
            functools.partial(act_kernel, cells),
            [
                ((rows + 1, pairs, 3 * chans), BF),
                (plane, F32),
                (plane, F32),
                ((2, chans), F32),
                ((devices, 4, 128), F32),
            ],
            [((J, chans), F32)],
            flops=1600 * 256 * 20,
            smem=(0,),
            n_in=8,
        )(flags, stats, hq, he, aq, ae, gain, bias)
        sums = lax.all_to_all(sums, ALL, 0, 0, tiled=True)
    with jax.named_scope("down"):
        output, down_part = call(
            down_kernel,
            [((half, pairs, chans), BF), ((3, 3 * chans, chans), F32)],
            flops=4 * 256 * 2304 * 256,
            n_in=3,
        )(t, c2, dw3)
    with jax.named_scope("grad"):
        h4, conv_part, vec = call(
            functools.partial(grad_kernel, cells),
            [((rows + 2, pairs, 4 * chans), BF), ((3, 3 * chans, chans), F32), ((2, chans), F32)],
            [((J, chans), F32), ((rows + 2, J, 3 * chans), BF), ((rows + 2, J, 3 * chans), BF)],
            flops=2 * 1600 * 2304 * 256,
            smem=(0,),
            n_in=9,
        )(flags, sums, coef, hq, he, pq, pe, gain, x)
    with jax.named_scope("total"):
        total_rows = 9 * chans
        core = lax.axis_index("core")
        conv_flat = conv_part.reshape(total_rows, chans)
        down_flat = down_part.reshape(total_rows, chans)
        mine = jnp.where(core == 0, conv_flat, down_flat)
        theirs = jnp.where(core == 0, down_flat, conv_flat)
        pair = [(0, 1), (1, 0)]
        other = lax.ppermute(theirs.astype(BF), "core", pair)
        mine = (mine + other.astype(F32)).astype(BF)
        chips = lax.axis_size(PLANE)
        depth = lax.axis_size("z")
        share = total_rows // chips
        got = lax.all_to_all(mine.reshape(chips, share, chans), PLANE, 0, 0, tiled=True)
        piece = jnp.sum(got.astype(F32), axis=0).astype(BF)
        got = lax.all_to_all(jnp.broadcast_to(piece[None], (depth, share, chans)), "z", 0, 0, tiled=True)
        piece = (jnp.sum(got.astype(F32), axis=0) * (1.0 / math.sqrt(cells))).astype(BF)
        whole = lax.all_to_all(jnp.broadcast_to(piece[None], (chips, share, chans)), PLANE, 0, 0, tiled=True)
        other = lax.ppermute(whole, "core", pair)
        whole = whole.reshape(3, 3, chans, chans)
        other = other.reshape(3, 3, chans, chans)
        conv_grad = jnp.where(core == 0, whole, other).astype(F32)
        down_grad = jnp.where(core == 0, other, whole).astype(F32)
    with jax.named_scope("input"):
        (input_grad,) = call(
            input_kernel,
            [((rows, cols, chans), BF)],
            [((rows, 2, cols, 128), F32)],
            flops=2 * 1024 * 2304 * 256,
            n_in=2,
        )(h4, conv_weight)
    return output, input_grad, conv_grad, down_grad, vec[0], vec[1]


SIZES = {64: (4, 8, 2), 2: (1, 2, 1), 4: (2, 2, 1)}


def solution(mesh):
    lon, lat = mesh.devices.shape
    fine = Mesh(mesh.devices.reshape(SIZES[lon] + (lat // 2, 2)), ALL)
    band = P(LAT, LON, None)
    return jax.shard_map(
        local,
        mesh=fine,
        in_specs=(band, P(), P(), P(), P(), band),
        out_specs=(band, band, P(), P(), P(), P()),
        check_vma=False,
    )
```

```python
import functools
import math

import jax
import jax.numpy as jnp
from jax import lax
from jax.experimental import pallas as pl
from jax.experimental.pallas import tpu as pltpu
from jax.sharding import Mesh
from jax.sharding import PartitionSpec as P

EPS = 1e-05
WIDTH = 8
J = 80
LON = ("x", "z", "y_hi")
LAT = ("y_lo", "core")
PLANE = ("x", "y_hi", "y_lo")
ALL = LON + LAT
CHIPS = ("x", "z", "y_hi", "y_lo")
BF = jnp.bfloat16
F32 = jnp.float32


def call(body, outs, scratch=(), flops=0, smem=(), hbm=(), n_in=0, sems=0):
    spaces = [pltpu.SMEM if i in smem else pltpu.HBM if i in hbm else pltpu.VMEM for i in range(n_in)]
    out_spaces = [pltpu.HBM if len(o) > 2 else pltpu.VMEM for o in outs]
    return pl.pallas_call(
        body,
        out_shape=[pltpu.HBM(o[0], o[1]) if len(o) > 2 else jax.ShapeDtypeStruct(o[0], o[1]) for o in outs],
        in_specs=[pl.BlockSpec(memory_space=m) for m in spaces],
        out_specs=[pl.BlockSpec(memory_space=m) for m in out_spaces],
        scratch_shapes=[pltpu.VMEM(s, d) for s, d in scratch]
        + ([pltpu.SemaphoreType.DMA((sems,))] if sems else []),
        compiler_params=pltpu.CompilerParams(vmem_limit_bytes=24 * 1024 * 1024),
        cost_estimate=pl.CostEstimate(flops=flops, bytes_accessed=1 << 20, transcendentals=0),
    )


def pinned(value):
    return pltpu.with_memory_space_constraint(value, pltpu.HBM)


def dot(a, b):
    return jnp.dot(a, b, preferred_element_type=F32)


def dot_t(a, b):
    return lax.dot_general(a, b, (((1,), (1,)), ((), ())), preferred_element_type=F32)


def t_dot(a, b):
    return lax.dot_general(a, b, (((0,), (0,)), ((), ())), preferred_element_type=F32)


def exact(a, b):
    a8 = jnp.broadcast_to(a, (8, a.shape[1]))
    return jnp.dot(a8, b, preferred_element_type=F32, precision=lax.Precision.HIGHEST)[0:1]


def to_lanes(chans):
    c = lax.broadcasted_iota(jnp.int32, (chans, 128), 0) // WIDTH
    l = lax.broadcasted_iota(jnp.int32, (chans, 128), 1)
    return (c == l).astype(F32)


def from_lanes(chans):
    c = lax.broadcasted_iota(jnp.int32, (128, chans), 1) // WIDTH
    l = lax.broadcasted_iota(jnp.int32, (128, chans), 0)
    return (c == l).astype(F32)


def masks():
    j = lax.broadcasted_iota(jnp.int32, (J, 1), 0)
    odd = jnp.where((j >= 1) & (j <= 64), 1.0, 0.0)
    even = jnp.where(j <= 63, 1.0, 0.0)
    return odd, even


def pack_lon(feat, cot, east, west, sems):
    rows, cols, _ = feat.shape
    half, pairs, _ = cot.shape
    copies = [
        pltpu.make_async_copy(feat.at[:, cols - 16 : cols], east.at[0:rows], sems.at[0]),
        pltpu.make_async_copy(cot.at[:, pairs - 16 : pairs], east.at[rows : rows + half], sems.at[1]),
        pltpu.make_async_copy(feat.at[:, 0:16], west.at[0:rows], sems.at[2]),
        pltpu.make_async_copy(cot.at[:, 0:16], west.at[rows : rows + half], sems.at[3]),
    ]
    for copy in copies:
        copy.start()
    for copy in copies:
        copy.wait()


def pack_lat(feat, cot, west, east, south, north, sems):
    rows, cols, _ = feat.shape
    half, pairs, _ = cot.shape
    copies = []
    ends = ((south, rows - 2, half - 1), (north, 0, 0))
    for dest, top, mid in ends:
        parts = [(feat.at[top + k], k * (cols + 32) + 16, cols) for k in range(2)]
        parts.append((cot.at[mid], 2 * (cols + 32) + 16, pairs))
        for src, o, n in parts:
            copies.append(pltpu.make_async_copy(src, dest.at[o : o + n], sems.at[len(copies)]))
            copies[-1].start()
    for dest, top, mid in ends:
        for row, o, n in (
            (top, 0, cols),
            (top + 1, cols + 32, cols),
            (rows + mid, 2 * (cols + 32), pairs),
        ):
            dest[o : o + 16] = west[row]
            dest[o + 16 + n : o + 32 + n] = east[row]
    for copy in copies:
        copy.wait()


def conv_kernel(
    feat_hbm, west, east, north, south, w_hbm, x_hbm, h_hbm, hq_out, he_out, stat_out, f32s, x_out, feat, w, sems
):
    rows, cols, chans = feat.shape
    load_f = pltpu.make_async_copy(feat_hbm, feat, sems.at[1])
    load_f.start()
    load_w = pltpu.make_async_copy(w_hbm, w, sems.at[2])
    load_w.start()
    wide = cols + 32
    f32s[:, :, wide : wide + 16] = jnp.zeros((rows + 4, 2, 16, 128), F32)
    load_f.wait()
    for v in range(2):
        part = slice(v * 128, v * 128 + 128)
        for k in range(2):
            f32s[k, v, 0:wide] = north[k * wide : (k + 1) * wide, part].astype(F32)
            f32s[rows + 2 + k, v, 0:wide] = south[k * wide : (k + 1) * wide, part].astype(F32)
        f32s[2 : rows + 2, v, 0:16] = west[0:rows, :, part].astype(F32)
        f32s[2 : rows + 2, v, 16 : 16 + cols] = feat[:, :, part].astype(F32)
        f32s[2 : rows + 2, v, 16 + cols : wide] = east[0:rows, :, part].astype(F32)
        for r in range(rows + 4):
            for k in range(4):
                lane = k * chans + v * 128
                x_out[r, :, lane : lane + 128] = f32s[r, v, pl.ds(14 + k, J, stride=2), :].astype(BF)
    keep = pltpu.make_async_copy(x_out, x_hbm, sems.at[0])
    keep.start()
    load_w.wait()
    copies = [keep]
    odd, even = masks()
    sums = jnp.zeros((1, chans), F32)
    for out, lo in ((hq_out, 0), (he_out, chans)):
        acc = None
        for a in range(3):
            lhs = x_out[a : a + rows + 2, :, lo : lo + 3 * chans].reshape((rows + 2) * J, 3 * chans)
            term = dot(lhs, w[a])
            acc = term if acc is None else acc + term
        out[...] = acc.astype(BF).reshape(rows + 2, J, chans)
        k = lo // chans
        copies.append(pltpu.make_async_copy(out, h_hbm.at[k], sems.at[3 + k]))
        copies[-1].start()
    for out, mask in ((hq_out, odd), (he_out, even)):
        part = jnp.zeros((J, chans), F32)
        for r in range(1, rows + 1):
            part = part + out[r].astype(F32)
        sums = sums + jnp.sum(part * mask, axis=0, keepdims=True)
    lanes = to_lanes(chans)
    means = exact(sums, lanes) / (rows * cols * WIDTH)
    mean = exact(means, from_lanes(chans))
    squares = jnp.zeros((1, chans), F32)
    for out, mask in ((hq_out, odd), (he_out, even)):
        part = jnp.zeros((J, chans), F32)
        for r in range(1, rows + 1):
            d = out[r].astype(F32) - mean
            part = part + d * d
        squares = squares + jnp.sum(part * mask, axis=0, keepdims=True)
    stat_out[...] = jnp.concatenate([means, exact(squares, lanes)], axis=0)
    for copy in copies:
        copy.wait()


def pair_stats(local_n, stat, other, out):
    mine, theirs = stat[...], other[...]
    gap = mine[0:1] - theirs[0:1]
    mean = 0.5 * (mine[0:1] + theirs[0:1])
    squares = mine[1:2] + theirs[1:2] + (0.5 * local_n) * gap * gap
    both = jnp.concatenate([mean, squares], axis=0)
    out[...] = jnp.broadcast_to(both[None], out.shape)


def pair_sums(mine, other, out):
    both = mine[...] + other[...]
    out[...] = jnp.broadcast_to(both[None], out.shape)


def back_kernel(cot, west, east, north, south, dw, c_out, aq_out, ae_out, f32s):
    half, pairs, chans = cot.shape
    rows = west.shape[0] - half
    wide = pairs + 32
    base = north.shape[0] - wide
    f32s[0, 0:wide] = north[base : base + wide].astype(F32)
    f32s[half + 1, 0:wide] = south[base : base + wide].astype(F32)
    f32s[1 : half + 1, 0:16] = west[rows:].astype(F32)
    f32s[1 : half + 1, 16 : 16 + pairs] = cot[...].astype(F32)
    f32s[1 : half + 1, 16 + pairs : wide] = east[rows:].astype(F32)
    for s in range(half + 2):
        c_out[s, :, 0:chans] = f32s[s, 15 : 15 + J].astype(BF)
        c_out[s, :, chans : 2 * chans] = f32s[s, 16 : 16 + J].astype(BF)
    n = half + 1
    lo_l = c_out[0:n, :, 0:chans].reshape(n * J, chans)
    lo_r = c_out[0:n, :, chans:].reshape(n * J, chans)
    hi_l = c_out[1 : n + 1, :, 0:chans].reshape(n * J, chans)
    hi_r = c_out[1 : n + 1, :, chans:].reshape(n * J, chans)

    def put(out, k, value):
        value = value.astype(BF).reshape(n, J, chans)
        for i in range(n):
            out[2 * i + k] = value[i]

    put(ae_out, 1, dot_t(hi_r, dw[1, 1]))
    put(aq_out, 1, dot_t(hi_r, dw[1, 0]) + dot_t(hi_l, dw[1, 2]))
    put(ae_out, 0, dot_t(hi_r, dw[0, 1]) + dot_t(lo_r, dw[2, 1]))
    put(
        aq_out,
        0,
        dot_t(hi_r, dw[0, 0]) + dot_t(hi_l, dw[0, 2]) + dot_t(lo_r, dw[2, 0]) + dot_t(lo_l, dw[2, 2]),
    )


def act_kernel(cells, flags, stats, hq, he, aq, ae, gain, bias, t_hbm, p_hbm, coef_out, sum_out, f32s, t_out, p_out, sems):
    chips = stats.shape[0]
    rows = hq.shape[0] - 2
    chans = hq.shape[2]
    chip_n = float(cells // chips * WIDTH)
    count = float(cells * WIDTH)
    rec = stats[...]
    total = jnp.sum(rec, axis=0)
    centre = total[0:1] / chips
    dev = rec[:, 0, :] - centre
    spread = jnp.sum(dev * dev, axis=0, keepdims=True)
    back = from_lanes(chans)
    mean = exact(centre, back)
    var = exact((total[1:2] + chip_n * spread) / count, back)
    inverse = lax.rsqrt(var + EPS)
    coef_out[0:1] = mean
    coef_out[1:2] = inverse
    g = gain[...]
    b = bias[...]
    odd, even = masks()
    top = jnp.where(flags[0] == 1, 0.0, 1.0)
    bias_sum = jnp.zeros((1, chans), F32)
    gain_sum = jnp.zeros((1, chans), F32)
    copies = []
    for k, (h, a, mask) in enumerate(((hq, aq, odd), (he, ae, even))):
        is_q = k == 0
        acc_b = jnp.zeros((J, chans), F32)
        acc_g = jnp.zeros((J, chans), F32)
        for r in range(rows + 2):
            normed = (h[r].astype(F32) - mean) * inverse
            shifted = g * normed + b
            sigma = jax.nn.sigmoid(shifted)
            pre = a[r].astype(F32) * sigma * (1.0 + shifted * (1.0 - sigma))
            p_out[k, r] = pre
            copies.append(pltpu.make_async_copy(p_out.at[k, r], p_hbm.at[k, r], sems.at[len(copies)]))
            copies[-1].start()
            if 1 <= r <= rows:
                acc_b = acc_b + pre
                acc_g = acc_g + pre * normed
            if r <= rows:
                active = shifted * sigma
                if r == 0:
                    active = active * top
                if is_q:
                    f32s[...] = active.astype(BF).astype(F32)
                    t_out[r, :, 0:chans] = active[0:64].astype(BF)
                    t_out[r, :, 2 * chans :] = f32s[1:65].astype(BF)
                else:
                    t_out[r, :, chans : 2 * chans] = active[0:64].astype(BF)
                    copies.append(pltpu.make_async_copy(t_out.at[r], t_hbm.at[r], sems.at[len(copies)]))
                    copies[-1].start()
        bias_sum = bias_sum + jnp.sum(acc_b * mask, axis=0, keepdims=True)
        gain_sum = gain_sum + jnp.sum(acc_g * mask, axis=0, keepdims=True)
    sum_out[...] = jnp.concatenate(
        [bias_sum[:, 0:128], bias_sum[:, 128:256], gain_sum[:, 0:128], gain_sum[:, 128:256]], axis=0
    )
    for copy in copies:
        copy.wait()


def down_kernel(t, c, dw, out, grad):
    half = out.shape[0]
    pairs, chans = out.shape[1:]
    cot = c[1 : half + 1, 0:pairs, chans:].reshape(half * pairs, chans)
    acc = None
    for a in range(3):
        lhs = jnp.concatenate([t[2 * i + a] for i in range(half)], axis=0)
        term = dot(lhs, dw[a])
        acc = term if acc is None else acc + term
        grad[a * 3 * chans : (a + 1) * 3 * chans] = t_dot(lhs, cot)
    out[...] = acc.astype(BF).reshape(out.shape)


def grad_kernel(
    cells, flags, sums, coef, gain, h_hbm, p_hbm, x_hbm, h4_hbm, conv_out, vec_out, f32s, rq, re, h_in, p_in, x, h4_out, sems
):
    rows = p_in.shape[1] - 2
    chans = p_in.shape[3]
    loads = []
    for k in range(2):
        loads.append(pltpu.make_async_copy(h_hbm.at[k], h_in.at[k], sems.at[len(loads)]))
        loads[-1].start()
        for r in range(rows + 2):
            loads.append(pltpu.make_async_copy(p_hbm.at[k, r], p_in.at[k, r], sems.at[len(loads)]))
            loads[-1].start()
    load_x = pltpu.make_async_copy(x_hbm, x, sems.at[len(loads)])
    load_x.start()
    first_out = len(loads) + 1
    copies = []
    count = float(cells * WIDTH)
    total = jnp.sum(sums[...], axis=0)
    bias_sum = jnp.concatenate([total[0:1], total[1:2]], axis=1)
    gain_sum = jnp.concatenate([total[2:3], total[3:4]], axis=1)
    factor = 1.0 / math.sqrt(cells)
    vec_out[0:1] = gain_sum * factor
    vec_out[1:2] = bias_sum * factor
    g = gain[...]
    lanes, back = to_lanes(chans), from_lanes(chans)
    first = exact(exact(g * bias_sum, lanes), back) / count
    second = exact(exact(g * gain_sum, lanes), back) / count
    mean = coef[0:1]
    inverse = coef[1:2]
    top = jnp.where(flags[0] == 1, 0.0, 1.0)
    bottom = jnp.where(flags[1] == 1, 0.0, 1.0)
    odd, even = masks()
    zero = jnp.zeros((J, chans), BF)
    for k, (r_out, mask) in enumerate(((rq, odd), (re, even))):
        is_q = k == 0
        loads[k * (rows + 3)].wait()
        for f in (0, 1):
            for a in (1, 2):
                if f - a + 1 <= 0:
                    r_out[f, :, a * chans : (a + 1) * chans] = zero
                    r_out[rows + 1 - f, :, (2 - a) * chans : (3 - a) * chans] = zero
        for r in range(rows + 2):
            loads[k * (rows + 3) + 1 + r].wait()
            normed = (h_in[k, r].astype(F32) - mean) * inverse
            value = inverse * (g * p_in[k, r] - first - normed * second)
            if r == 0:
                value = value * top
            if r == rows + 1:
                value = value * bottom
            rounded = value.astype(BF)
            if 1 <= r <= rows:
                inner = (value * mask).astype(BF)
                for a in range(3):
                    r_out[r + a - 1, :, a * chans : (a + 1) * chans] = inner
            f32s[...] = rounded.astype(F32)
            moved = f32s[1:65].astype(BF)
            lo = 3 if is_q else 2
            h4_out[r, :, lo * chans : (lo + 1) * chans] = rounded[0:64]
            lo = 1 if is_q else 0
            h4_out[r, :, lo * chans : (lo + 1) * chans] = moved
            if not is_q:
                copies.append(pltpu.make_async_copy(h4_out.at[r], h4_hbm.at[r], sems.at[first_out + r]))
                copies[-1].start()
    m = (rows + 2) * J
    load_x.wait()
    lhs = x[1 : rows + 3].reshape(m, 4 * chans)
    part = t_dot(lhs[:, 0 : 3 * chans], rq[...].reshape(m, 3 * chans))
    part = part + t_dot(lhs[:, chans : 4 * chans], re[...].reshape(m, 3 * chans))
    for a in range(3):
        conv_out[a * 3 * chans : (a + 1) * 3 * chans] = part[:, a * chans : (a + 1) * chans]
    for copy in copies:
        copy.wait()


def input_kernel(h4, w, out, f32s):
    rows, cols, chans = out.shape
    for k, lo in ((0, 1), (1, 0)):
        acc = None
        for a in range(3):
            for b in range(3):
                lane = (lo + b) * chans
                lhs = h4[2 - a : 2 - a + rows, :, lane : lane + chans].reshape(rows * (cols // 2), chans)
                term = dot_t(lhs, w[a, b])
                acc = term if acc is None else acc + term
        acc = acc.reshape(rows, cols // 2, chans)
        for r in range(rows):
            for v in range(2):
                f32s[r, v, pl.ds(k, cols // 2, stride=2), :] = acc[r, :, v * 128 : v * 128 + 128]
    for v in range(2):
        out[:, :, v * 128 : v * 128 + 128] = f32s[:, v].astype(BF)


def passed(value, axes, step, wrap):
    n = lax.axis_size(axes)
    pairs = [(i, (i + step) % n) for i in range(n) if wrap or 0 <= i + step < n]
    return lax.ppermute(value, axes, pairs)


def unpack_kernel(flags, whole, other, conv, down, f32s, sems):
    n = whole.shape[0]
    step = n // 4
    for core, one, two in ((0, whole, other), (1, other, whole)):

        @pl.when(flags[2] == core)
        def _():
            copies = []
            for k, (src, dst) in enumerate(((one, conv), (two, down))):
                for q in range(4):
                    part = slice(q * step, (q + 1) * step)
                    f32s[k, part] = src[part].astype(F32)
                    copies.append(pltpu.make_async_copy(f32s.at[k, part], dst.at[part], sems.at[k * 4 + q]))
                    copies[-1].start()
            for copy in copies:
                copy.wait()


def core_swap(value):
    return lax.ppermute(value, "core", [(0, 1), (1, 0)])


def local(features, conv_weight, down_weight, norm_gain, norm_bias, cotangent):
    rows, cols, chans = features.shape
    half, pairs, _ = cotangent.shape
    devices = lax.axis_size(ALL)
    lats = lax.axis_size(LAT)
    cells = rows * cols * devices
    factor = 1.0 / math.sqrt(cells)
    lat = lax.axis_index(LAT)
    flags = jnp.stack([lat == 0, lat == lats - 1, lax.axis_index("core") == 1]).astype(jnp.int32)
    gain = norm_gain.reshape(1, chans)
    bias = norm_bias.reshape(1, chans)
    w3 = conv_weight.reshape(3, 3 * chans, chans)
    dw3 = down_weight.reshape(3, 3 * chans, chans)
    all_rows = 9 * chans

    with jax.named_scope("halo"):
        slab = (rows + half, 16, chans)
        to_east, to_west = call(pack_lon, [(slab, BF)] * 2, n_in=2, hbm=(0, 1), sems=4)(
            pinned(features), pinned(cotangent)
        )
        west = passed(to_east, LON, 1, True)
        east = passed(to_west, LON, -1, True)
        strip = (2 * (cols + 32) + pairs + 32, chans)
        to_south, to_north = call(pack_lat, [(strip, BF)] * 2, n_in=4, hbm=(0, 1), sems=6)(
            pinned(features), pinned(cotangent), west, east
        )
        north = passed(to_south, LAT, 1, False)
        south = passed(to_north, LAT, -1, False)

    plane = (rows + 2, J, chans)
    x_shape = (rows + 4, J, 4 * chans)
    with jax.named_scope("conv"):
        x, h, hq, he, stat = call(
            conv_kernel,
            [(x_shape, BF, True), ((2,) + plane, BF, True), (plane, BF), (plane, BF), ((2, 128), F32)],
            [((rows + 4, 2, cols + 48, 128), F32), (x_shape, BF), ((rows, cols, chans), BF), (w3.shape, BF)],
            flops=2 * 1600 * 2304 * 256,
            n_in=6,
            hbm=(0, 5),
            sems=5,
        )(pinned(features), west, east, north, south, pinned(w3))
        chips = lax.axis_size(CHIPS)
        local_n = float(rows * cols * WIDTH)
        (wide,) = call(functools.partial(pair_stats, local_n), [((chips, 2, 128), F32)], n_in=2)(stat, core_swap(stat))
        stats = lax.all_to_all(wide, CHIPS, 0, 0, tiled=True)
    with jax.named_scope("back"):
        c2, aq, ae = call(
            back_kernel,
            [((half + 2, J, 2 * chans), BF), (plane, BF), (plane, BF)],
            [((half + 2, pairs + 32, chans), F32)],
            flops=2 * 400 * 2304 * 256,
            n_in=6,
        )(cotangent, west, east, north, south, down_weight)
    t_shape = (rows + 1, pairs, 3 * chans)
    with jax.named_scope("act"):
        t, p, coef, sums = call(
            functools.partial(act_kernel, cells),
            [(t_shape, BF, True), ((2,) + plane, F32, True), ((2, chans), F32), ((4, 128), F32)],
            [((J, chans), F32), (t_shape, BF), ((2,) + plane, F32)],
            flops=1600 * 256 * 20,
            smem=(0,),
            n_in=8,
            sems=3 * rows + 5,
        )(flags, stats, hq, he, aq, ae, gain, bias)
        (wide,) = call(pair_sums, [((chips, 4, 128), F32)], n_in=2)(sums, core_swap(sums))
        sums = lax.all_to_all(wide, CHIPS, 0, 0, tiled=True)
    with jax.named_scope("down"):
        output, down_part = call(
            down_kernel,
            [((half, pairs, chans), BF), ((all_rows, chans), F32)],
            flops=4 * 256 * 2304 * 256,
            n_in=3,
        )(t, c2, dw3)
    h4_shape = (rows + 2, pairs, 4 * chans)
    with jax.named_scope("grad"):
        h4, conv_part, vec = call(
            functools.partial(grad_kernel, cells),
            [(h4_shape, BF, True), ((all_rows, chans), F32), ((2, chans), F32)],
            [
                ((J, chans), F32),
                ((rows + 2, J, 3 * chans), BF),
                ((rows + 2, J, 3 * chans), BF),
                ((2,) + plane, BF),
                ((2,) + plane, F32),
                (x_shape, BF),
                (h4_shape, BF),
            ],
            flops=2 * 1600 * 2304 * 256,
            smem=(0,),
            hbm=(4, 5, 6),
            n_in=7,
            sems=3 * (rows + 2) + 3,
        )(flags, sums, coef, gain, pinned(h), pinned(p), pinned(x))
    with jax.named_scope("input"):
        (input_grad,) = call(
            input_kernel,
            [((rows, cols, chans), BF)],
            [((rows, 2, cols, 128), F32)],
            flops=2 * 1024 * 2304 * 256,
            n_in=2,
        )(h4, conv_weight)
    with jax.named_scope("total"):
        first = lax.axis_index("core") == 0
        other = core_swap(jnp.where(first, down_part, conv_part).astype(BF))
        mine = (jnp.where(first, conv_part, down_part) + other.astype(F32)).astype(BF)
        chips = lax.axis_size(PLANE)
        depth = lax.axis_size("z")
        share = all_rows // chips
        got = lax.all_to_all(mine.reshape(chips, share, chans), PLANE, 0, 0, tiled=True)
        got, input_grad = lax.optimization_barrier((got, input_grad))
        piece = jnp.sum(got.astype(F32), axis=0).astype(BF)
        got = lax.all_to_all(jnp.broadcast_to(piece[None], (depth, share, chans)), "z", 0, 0, tiled=True)
        piece = (jnp.sum(got.astype(F32), axis=0) * factor).astype(BF)
        whole = lax.all_to_all(jnp.broadcast_to(piece[None], (chips, share, chans)), PLANE, 0, 0, tiled=True)
        whole = whole.reshape(all_rows, chans)
        flat = ((all_rows, chans), F32, True)
        conv_grad, down_grad = call(
            unpack_kernel, [flat, flat], [((2, all_rows, chans), F32)], smem=(0,), n_in=3, sems=8
        )(flags, whole, core_swap(whole))
    shape = (3, 3, chans, chans)
    return output, input_grad, conv_grad.reshape(shape), down_grad.reshape(shape), vec[0], vec[1]


SIZES = {64: (4, 8, 2), 2: (1, 2, 1), 4: (2, 2, 1)}


def solution(mesh):
    lon, lat = mesh.devices.shape
    fine = Mesh(mesh.devices.reshape(SIZES[lon] + (lat // 2, 2)), ALL)
    band = P(LAT, LON, None)
    return jax.shard_map(
        local,
        mesh=fine,
        in_specs=(band, P(), P(), P(), P(), band),
        out_specs=(band, band, P(), P(), P(), P()),
        check_vma=False,
    )
```

```python
import functools
import math

import jax
import jax.numpy as jnp
from jax import lax
from jax.experimental import pallas as pl
from jax.experimental.pallas import tpu as pltpu
from jax.sharding import Mesh
from jax.sharding import PartitionSpec as P

EPS = 1e-05
WIDTH = 8
J = 80
LON = ("x", "z_hi", "z_lo", "y_hi")
LAT = ("y_lo", "core")
NEAR = ("x", "z_lo", "y_hi", "y_lo")
FEW = ("x", "core")
REST = ("z_hi", "z_lo", "y_hi", "y_lo")
ALL = LON + LAT
BF = jnp.bfloat16
F32 = jnp.float32


def call(body, outs, scratch=(), flops=0, smem=(), hbm=(), n_in=0, sems=0):
    spaces = [pltpu.SMEM if i in smem else pltpu.HBM if i in hbm else pltpu.VMEM for i in range(n_in)]
    out_spaces = [pltpu.HBM if len(o) > 2 else pltpu.VMEM for o in outs]
    return pl.pallas_call(
        body,
        out_shape=[pltpu.HBM(o[0], o[1]) if len(o) > 2 else jax.ShapeDtypeStruct(o[0], o[1]) for o in outs],
        in_specs=[pl.BlockSpec(memory_space=m) for m in spaces],
        out_specs=[pl.BlockSpec(memory_space=m) for m in out_spaces],
        scratch_shapes=[pltpu.VMEM(s, d) for s, d in scratch]
        + ([pltpu.SemaphoreType.DMA((sems,))] if sems else []),
        compiler_params=pltpu.CompilerParams(vmem_limit_bytes=24 * 1024 * 1024),
        cost_estimate=pl.CostEstimate(flops=flops, bytes_accessed=1 << 20, transcendentals=0),
    )


def pinned(value):
    return pltpu.with_memory_space_constraint(value, pltpu.HBM)


def dot(a, b):
    return jnp.dot(a, b, preferred_element_type=F32)


def dot_t(a, b):
    return lax.dot_general(a, b, (((1,), (1,)), ((), ())), preferred_element_type=F32)


def t_dot(a, b):
    return lax.dot_general(a, b, (((0,), (0,)), ((), ())), preferred_element_type=F32)


def exact(a, b):
    a8 = jnp.broadcast_to(a, (8, a.shape[1]))
    return jnp.dot(a8, b, preferred_element_type=F32, precision=lax.Precision.HIGHEST)[0:1]


def to_lanes(chans):
    c = lax.broadcasted_iota(jnp.int32, (chans, 128), 0) // WIDTH
    l = lax.broadcasted_iota(jnp.int32, (chans, 128), 1)
    return (c == l).astype(F32)


def from_lanes(chans):
    c = lax.broadcasted_iota(jnp.int32, (128, chans), 1) // WIDTH
    l = lax.broadcasted_iota(jnp.int32, (128, chans), 0)
    return (c == l).astype(F32)


def masks():
    j = lax.broadcasted_iota(jnp.int32, (J, 1), 0)
    odd = jnp.where((j >= 1) & (j <= 64), 1.0, 0.0)
    even = jnp.where(j <= 63, 1.0, 0.0)
    return odd, even


def pack_lon(feat_hbm, cot_hbm, east, west, feat, cot, f32s, sems):
    rows, cols, chans = feat_hbm.shape
    half, pairs, _ = cot_hbm.shape
    copies = []
    for k, (lo_f, lo_c) in enumerate(((cols - 16, pairs - 16), (0, 0))):
        copies.append(pltpu.make_async_copy(feat_hbm.at[:, lo_f : lo_f + 16], feat.at[k], sems.at[2 * k]))
        copies.append(pltpu.make_async_copy(cot_hbm.at[:, lo_c : lo_c + 16], cot.at[k], sems.at[2 * k + 1]))
    for copy in copies:
        copy.start()
    f32s[...] = jnp.zeros(f32s.shape, F32)
    for copy in copies:
        copy.wait()
    for k, (out, at_f, at_c) in enumerate(((east, 14, 15), (west, 0, 0))):
        for r in range(rows):
            f32s[2 * r : 2 * r + 2] = feat[k, r].astype(F32)[at_f : at_f + 2]
        for i in range(half):
            f32s[2 * rows + i : 2 * rows + i + 1] = cot[k, i].astype(F32)[at_c : at_c + 1]
        out[...] = f32s[...].astype(BF)


def pack_lat(feat, cot, west, east, south, north, w32, e32, corner, sems):
    rows, cols, _ = feat.shape
    half, pairs, _ = cot.shape
    copies = []
    ends = ((south, rows - 2, half - 1), (north, 0, 0))
    for dest, top, mid in ends:
        parts = [(feat.at[top + k], k * cols, cols) for k in range(2)]
        parts.append((cot.at[mid], 2 * cols, pairs))
        for src, o, n in parts:
            copies.append(pltpu.make_async_copy(src, dest.at[o : o + n], sems.at[len(copies)]))
            copies[-1].start()
    w32[...] = west[...].astype(F32)
    e32[...] = east[...].astype(F32)
    corner[...] = jnp.zeros(corner.shape, F32)
    o = 2 * cols + pairs
    for dest, top, mid in ends:
        corner[0:4] = w32[2 * top : 2 * top + 4]
        corner[4:8] = e32[2 * top : 2 * top + 4]
        corner[8:9] = w32[2 * rows + mid : 2 * rows + mid + 1]
        corner[9:10] = e32[2 * rows + mid : 2 * rows + mid + 1]
        dest[o : o + 16] = corner[...].astype(BF)
    for copy in copies:
        copy.wait()


def conv_kernel(
    feat_hbm, west, east, north, south, w_hbm, x_hbm, h_hbm, hq_out, he_out, stat_out, f32s, edge, x_out, feat, w, sems
):
    rows, cols, chans = feat.shape
    load_f = pltpu.make_async_copy(feat_hbm, feat, sems.at[1])
    load_f.start()
    load_w = pltpu.make_async_copy(w_hbm, w, sems.at[2])
    load_w.start()
    f32s[:, :, 16 + cols : 56 + cols] = jnp.zeros((rows + 4, 2, 40, 128), F32)
    pairs = cols // 2
    for v in range(2):
        part = slice(v * 128, v * 128 + 128)
        for k, side in enumerate((west, east)):
            edge[k, v] = side[:, part].astype(F32)
        for k, side in enumerate((north, south)):
            edge[2 + k, v, 0:16] = side[2 * cols + pairs : 2 * cols + pairs + 16, part].astype(F32)
            for q in range(2):
                row = q + k * (rows + 2)
                f32s[row, v, 16 : 16 + cols] = side[q * cols : (q + 1) * cols, part].astype(F32)
                f32s[row, v, 14:16] = edge[2 + k, v, 2 * q : 2 * q + 2]
                f32s[row, v, 16 + cols : 18 + cols] = edge[2 + k, v, 4 + 2 * q : 6 + 2 * q]
        for r in range(rows):
            f32s[2 + r, v, 14:16] = edge[0, v, 2 * r : 2 * r + 2]
            f32s[2 + r, v, 16 + cols : 18 + cols] = edge[1, v, 2 * r : 2 * r + 2]
    load_f.wait()
    for v in range(2):
        part = slice(v * 128, v * 128 + 128)
        f32s[2 : rows + 2, v, 16 : 16 + cols] = feat[:, :, part].astype(F32)
        for r in range(rows + 4):
            for k in range(4):
                lane = k * chans + v * 128
                x_out[r, :, lane : lane + 128] = f32s[r, v, pl.ds(14 + k, J, stride=2), :].astype(BF)
    keep = pltpu.make_async_copy(x_out, x_hbm, sems.at[0])
    keep.start()
    load_w.wait()
    copies = [keep]
    odd, even = masks()
    sums = jnp.zeros((1, chans), F32)
    for out, lo in ((hq_out, 0), (he_out, chans)):
        acc = None
        for a in range(3):
            lhs = x_out[a : a + rows + 2, :, lo : lo + 3 * chans].reshape((rows + 2) * J, 3 * chans)
            term = dot(lhs, w[a])
            acc = term if acc is None else acc + term
        out[...] = acc.astype(BF).reshape(rows + 2, J, chans)
        k = lo // chans
        copies.append(pltpu.make_async_copy(out, h_hbm.at[k], sems.at[3 + k]))
        copies[-1].start()
    for out, mask in ((hq_out, odd), (he_out, even)):
        part = jnp.zeros((J, chans), F32)
        for r in range(1, rows + 1):
            part = part + out[r].astype(F32)
        sums = sums + jnp.sum(part * mask, axis=0, keepdims=True)
    lanes = to_lanes(chans)
    means = exact(sums, lanes) / (rows * cols * WIDTH)
    mean = exact(means, from_lanes(chans))
    squares = jnp.zeros((1, chans), F32)
    for out, mask in ((hq_out, odd), (he_out, even)):
        part = jnp.zeros((J, chans), F32)
        for r in range(1, rows + 1):
            d = out[r].astype(F32) - mean
            part = part + d * d
        squares = squares + jnp.sum(part * mask, axis=0, keepdims=True)
    stat = jnp.concatenate([means, exact(squares, lanes)], axis=0)
    stat_out[...] = jnp.broadcast_to(stat[None], stat_out.shape)
    for copy in copies:
        copy.wait()


def merged_stats(local_n, rec, out):
    means = rec[:, 0, :]
    mean = jnp.sum(means, axis=0, keepdims=True) / rec.shape[0]
    gap = means - mean
    squares = jnp.sum(rec[:, 1, :] + local_n * gap * gap, axis=0, keepdims=True)
    both = jnp.concatenate([mean, squares], axis=0)
    out[...] = jnp.broadcast_to(both[None], out.shape)


def merged_sums(rec, out):
    out[...] = jnp.broadcast_to(jnp.sum(rec[...], axis=0)[None], out.shape)


def back_kernel(cot, west, east, north, south, dw, c_out, aq_out, ae_out, f32s, edge):
    half, pairs, chans = cot.shape
    rows = 2 * half
    cols = 2 * pairs
    f32s[:, 16 + pairs :] = jnp.zeros((half + 2, 16, chans), F32)
    for k, side in enumerate((west, east)):
        edge[k] = side[...].astype(F32)
    for k, side in enumerate((north, south)):
        row = k * (half + 1)
        f32s[row, 16 : 16 + pairs] = side[2 * cols : 2 * cols + pairs].astype(F32)
        edge[2 + k, 0:16] = side[2 * cols + pairs : 2 * cols + pairs + 16].astype(F32)
        f32s[row, 15:16] = edge[2 + k, 8:9]
        f32s[row, 16 + pairs : 17 + pairs] = edge[2 + k, 9:10]
    f32s[1 : half + 1, 16 : 16 + pairs] = cot[...].astype(F32)
    for i in range(half):
        f32s[1 + i, 15:16] = edge[0, 2 * rows + i : 2 * rows + i + 1]
        f32s[1 + i, 16 + pairs : 17 + pairs] = edge[1, 2 * rows + i : 2 * rows + i + 1]
    for s in range(half + 2):
        c_out[s, :, 0:chans] = f32s[s, 15 : 15 + J].astype(BF)
        c_out[s, :, chans : 2 * chans] = f32s[s, 16 : 16 + J].astype(BF)
    n = half + 1
    lo_l = c_out[0:n, :, 0:chans].reshape(n * J, chans)
    lo_r = c_out[0:n, :, chans:].reshape(n * J, chans)
    hi_l = c_out[1 : n + 1, :, 0:chans].reshape(n * J, chans)
    hi_r = c_out[1 : n + 1, :, chans:].reshape(n * J, chans)

    def put(out, k, value):
        value = value.astype(BF).reshape(n, J, chans)
        for i in range(n):
            out[2 * i + k] = value[i]

    put(ae_out, 1, dot_t(hi_r, dw[1, 1]))
    put(aq_out, 1, dot_t(hi_r, dw[1, 0]) + dot_t(hi_l, dw[1, 2]))
    put(ae_out, 0, dot_t(hi_r, dw[0, 1]) + dot_t(lo_r, dw[2, 1]))
    put(
        aq_out,
        0,
        dot_t(hi_r, dw[0, 0]) + dot_t(hi_l, dw[0, 2]) + dot_t(lo_r, dw[2, 0]) + dot_t(lo_l, dw[2, 2]),
    )


def act_kernel(cells, flags, stats, hq, he, aq, ae, gain, bias, t_hbm, p_hbm, coef_out, sum_out, f32s, t_out, p_out, sems):
    parts = stats.shape[0]
    rows = hq.shape[0] - 2
    chans = hq.shape[2]
    part_n = float(cells // parts * WIDTH)
    count = float(cells * WIDTH)
    rec = stats[...]
    total = jnp.sum(rec, axis=0)
    centre = total[0:1] / parts
    dev = rec[:, 0, :] - centre
    spread = jnp.sum(dev * dev, axis=0, keepdims=True)
    back = from_lanes(chans)
    mean = exact(centre, back)
    var = exact((total[1:2] + part_n * spread) / count, back)
    inverse = lax.rsqrt(var + EPS)
    coef_out[0:1] = mean
    coef_out[1:2] = inverse
    g = gain[...]
    b = bias[...]
    odd, even = masks()
    top = jnp.where(flags[0] == 1, 0.0, 1.0)
    bias_sum = jnp.zeros((1, chans), F32)
    gain_sum = jnp.zeros((1, chans), F32)
    copies = []
    for k, (h, a, mask) in enumerate(((hq, aq, odd), (he, ae, even))):
        is_q = k == 0
        acc_b = jnp.zeros((J, chans), F32)
        acc_g = jnp.zeros((J, chans), F32)
        for r in range(rows + 2):
            normed = (h[r].astype(F32) - mean) * inverse
            shifted = g * normed + b
            sigma = jax.nn.sigmoid(shifted)
            pre = a[r].astype(F32) * sigma * (1.0 + shifted * (1.0 - sigma))
            p_out[k, r] = pre
            copies.append(pltpu.make_async_copy(p_out.at[k, r], p_hbm.at[k, r], sems.at[len(copies)]))
            copies[-1].start()
            if 1 <= r <= rows:
                acc_b = acc_b + pre
                acc_g = acc_g + pre * normed
            if r <= rows:
                active = shifted * sigma
                if r == 0:
                    active = active * top
                if is_q:
                    f32s[...] = active.astype(BF).astype(F32)
                    t_out[r, :, 0:chans] = active[0:64].astype(BF)
                    t_out[r, :, 2 * chans :] = f32s[1:65].astype(BF)
                else:
                    t_out[r, :, chans : 2 * chans] = active[0:64].astype(BF)
                    copies.append(pltpu.make_async_copy(t_out.at[r], t_hbm.at[r], sems.at[len(copies)]))
                    copies[-1].start()
        bias_sum = bias_sum + jnp.sum(acc_b * mask, axis=0, keepdims=True)
        gain_sum = gain_sum + jnp.sum(acc_g * mask, axis=0, keepdims=True)
    payload = jnp.concatenate(
        [bias_sum[:, 0:128], bias_sum[:, 128:256], gain_sum[:, 0:128], gain_sum[:, 128:256]], axis=0
    )
    sum_out[...] = jnp.broadcast_to(payload[None], sum_out.shape)
    for copy in copies:
        copy.wait()


def down_kernel(t, c, dw, out, grad):
    half = out.shape[0]
    pairs, chans = out.shape[1:]
    cot = c[1 : half + 1, 0:pairs, chans:].reshape(half * pairs, chans)
    acc = None
    for a in range(3):
        lhs = jnp.concatenate([t[2 * i + a] for i in range(half)], axis=0)
        term = dot(lhs, dw[a])
        acc = term if acc is None else acc + term
        grad[a * 3 * chans : (a + 1) * 3 * chans] = t_dot(lhs, cot)
    out[...] = acc.astype(BF).reshape(out.shape)


def grad_kernel(
    cells, flags, sums, coef, gain, h_hbm, p_hbm, x_hbm, h4_hbm, conv_out, vec_out, f32s, rq, re, h_in, p_in, x, h4_out, sems
):
    rows = p_in.shape[1] - 2
    chans = p_in.shape[3]
    loads = []
    for k in range(2):
        loads.append(pltpu.make_async_copy(h_hbm.at[k], h_in.at[k], sems.at[len(loads)]))
        loads[-1].start()
        for r in range(rows + 2):
            loads.append(pltpu.make_async_copy(p_hbm.at[k, r], p_in.at[k, r], sems.at[len(loads)]))
            loads[-1].start()
    load_x = pltpu.make_async_copy(x_hbm, x, sems.at[len(loads)])
    load_x.start()
    first_out = len(loads) + 1
    copies = []
    count = float(cells * WIDTH)
    total = jnp.sum(sums[...], axis=0)
    bias_sum = jnp.concatenate([total[0:1], total[1:2]], axis=1)
    gain_sum = jnp.concatenate([total[2:3], total[3:4]], axis=1)
    factor = 1.0 / math.sqrt(cells)
    vec_out[0:1] = gain_sum * factor
    vec_out[1:2] = bias_sum * factor
    g = gain[...]
    lanes, back = to_lanes(chans), from_lanes(chans)
    first = exact(exact(g * bias_sum, lanes), back) / count
    second = exact(exact(g * gain_sum, lanes), back) / count
    mean = coef[0:1]
    inverse = coef[1:2]
    top = jnp.where(flags[0] == 1, 0.0, 1.0)
    bottom = jnp.where(flags[1] == 1, 0.0, 1.0)
    odd, even = masks()
    zero = jnp.zeros((J, chans), BF)
    for k, (r_out, mask) in enumerate(((rq, odd), (re, even))):
        is_q = k == 0
        loads[k * (rows + 3)].wait()
        for f in (0, 1):
            for a in (1, 2):
                if f - a + 1 <= 0:
                    r_out[f, :, a * chans : (a + 1) * chans] = zero
                    r_out[rows + 1 - f, :, (2 - a) * chans : (3 - a) * chans] = zero
        for r in range(rows + 2):
            loads[k * (rows + 3) + 1 + r].wait()
            normed = (h_in[k, r].astype(F32) - mean) * inverse
            value = inverse * (g * p_in[k, r] - first - normed * second)
            if r == 0:
                value = value * top
            if r == rows + 1:
                value = value * bottom
            rounded = value.astype(BF)
            if 1 <= r <= rows:
                inner = (value * mask).astype(BF)
                for a in range(3):
                    r_out[r + a - 1, :, a * chans : (a + 1) * chans] = inner
            f32s[...] = rounded.astype(F32)
            moved = f32s[1:65].astype(BF)
            lo = 3 if is_q else 2
            h4_out[r, :, lo * chans : (lo + 1) * chans] = rounded[0:64]
            lo = 1 if is_q else 0
            h4_out[r, :, lo * chans : (lo + 1) * chans] = moved
            if not is_q:
                copies.append(pltpu.make_async_copy(h4_out.at[r], h4_hbm.at[r], sems.at[first_out + r]))
                copies[-1].start()
    m = (rows + 2) * J
    load_x.wait()
    lhs = x[1 : rows + 3].reshape(m, 4 * chans)
    part = t_dot(lhs[:, 0 : 3 * chans], rq[...].reshape(m, 3 * chans))
    part = part + t_dot(lhs[:, chans : 4 * chans], re[...].reshape(m, 3 * chans))
    for a in range(3):
        conv_out[a * 3 * chans : (a + 1) * 3 * chans] = part[:, a * chans : (a + 1) * chans]
    for copy in copies:
        copy.wait()


def input_kernel(h4, w, out, f32s):
    rows, cols, chans = out.shape
    for k, lo in ((0, 1), (1, 0)):
        acc = None
        for a in range(3):
            for b in range(3):
                lane = (lo + b) * chans
                lhs = h4[2 - a : 2 - a + rows, :, lane : lane + chans].reshape(rows * (cols // 2), chans)
                term = dot_t(lhs, w[a, b])
                acc = term if acc is None else acc + term
        acc = acc.reshape(rows, cols // 2, chans)
        for r in range(rows):
            for v in range(2):
                f32s[r, v, pl.ds(k, cols // 2, stride=2), :] = acc[r, :, v * 128 : v * 128 + 128]
    for v in range(2):
        out[:, :, v * 128 : v * 128 + 128] = f32s[:, v, 0:cols].astype(BF)


def passed(value, axes, step, wrap):
    n = lax.axis_size(axes)
    pairs = [(i, (i + step) % n) for i in range(n) if wrap or 0 <= i + step < n]
    return lax.ppermute(value, axes, pairs)


def unpack_kernel(flags, whole, other, conv, down, f32s, sems):
    n = whole.shape[0]
    step = n // 4
    for core, one, two in ((0, whole, other), (1, other, whole)):

        @pl.when(flags[2] == core)
        def _():
            copies = []
            for k, (src, dst) in enumerate(((one, conv), (two, down))):
                for q in range(4):
                    part = slice(q * step, (q + 1) * step)
                    f32s[k, part] = src[part].astype(F32)
                    copies.append(pltpu.make_async_copy(f32s.at[k, part], dst.at[part], sems.at[k * 4 + q]))
                    copies[-1].start()
            for copy in copies:
                copy.wait()


def core_swap(value):
    return lax.ppermute(value, "core", [(0, 1), (1, 0)])


def local(features, conv_weight, down_weight, norm_gain, norm_bias, cotangent):
    rows, cols, chans = features.shape
    half, pairs, _ = cotangent.shape
    devices = lax.axis_size(ALL)
    lats = lax.axis_size(LAT)
    cells = rows * cols * devices
    factor = 1.0 / math.sqrt(cells)
    lat = lax.axis_index(LAT)
    flags = jnp.stack([lat == 0, lat == lats - 1, lax.axis_index("core") == 1]).astype(jnp.int32)
    gain = norm_gain.reshape(1, chans)
    bias = norm_bias.reshape(1, chans)
    w3 = conv_weight.reshape(3, 3 * chans, chans)
    dw3 = down_weight.reshape(3, 3 * chans, chans)
    all_rows = 9 * chans
    few = lax.axis_size(FEW)
    rest = lax.axis_size(REST)

    with jax.named_scope("halo"):
        slab = (2 * rows + 16, chans)
        to_east, to_west = call(
            pack_lon,
            [(slab, BF)] * 2,
            [((2, rows, 16, chans), BF), ((2, half, 16, chans), BF), (slab, F32)],
            n_in=2,
            hbm=(0, 1),
            sems=4,
        )(pinned(features), pinned(cotangent))
        west = passed(to_east, LON, 1, True)
        east = passed(to_west, LON, -1, True)
        strip = (2 * cols + pairs + 16, chans)
        to_south, to_north = call(
            pack_lat,
            [(strip, BF)] * 2,
            [(slab, F32), (slab, F32), ((16, chans), F32)],
            n_in=4,
            hbm=(0, 1),
            sems=6,
        )(pinned(features), pinned(cotangent), west, east)
        north = passed(to_south, LAT, 1, False)
        south = passed(to_north, LAT, -1, False)

    plane = (rows + 2, J, chans)
    x_shape = (rows + 4, J, 4 * chans)
    with jax.named_scope("conv"):
        x, h, hq, he, stat = call(
            conv_kernel,
            [(x_shape, BF, True), ((2,) + plane, BF, True), (plane, BF), (plane, BF), ((few, 2, 128), F32)],
            [((rows + 4, 2, cols + 56, 128), F32), ((4, 2) + (slab[0], 128), F32), (x_shape, BF), ((rows, cols, chans), BF), (w3.shape, BF)],
            flops=2 * 1600 * 2304 * 256,
            n_in=6,
            hbm=(0, 5),
            sems=5,
        )(pinned(features), west, east, north, south, pinned(w3))
        local_n = float(rows * cols * WIDTH)
        stat = lax.all_to_all(stat, FEW, 0, 0, tiled=True)
        (stat,) = call(functools.partial(merged_stats, local_n), [((rest, 2, 128), F32)], n_in=1)(stat)
        stats = lax.all_to_all(stat, REST, 0, 0, tiled=True)
    with jax.named_scope("back"):
        c2, aq, ae = call(
            back_kernel,
            [((half + 2, J, 2 * chans), BF), (plane, BF), (plane, BF)],
            [((half + 2, pairs + 32, chans), F32), ((4,) + slab, F32)],
            flops=2 * 400 * 2304 * 256,
            n_in=6,
        )(cotangent, west, east, north, south, down_weight)
    t_shape = (rows + 1, pairs, 3 * chans)
    with jax.named_scope("act"):
        t, p, coef, sums = call(
            functools.partial(act_kernel, cells),
            [(t_shape, BF, True), ((2,) + plane, F32, True), ((2, chans), F32), ((few, 4, 128), F32)],
            [((J, chans), F32), (t_shape, BF), ((2,) + plane, F32)],
            flops=1600 * 256 * 20,
            smem=(0,),
            n_in=8,
            sems=3 * rows + 5,
        )(flags, stats, hq, he, aq, ae, gain, bias)
        sums = lax.all_to_all(sums, FEW, 0, 0, tiled=True)
        (sums,) = call(merged_sums, [((rest, 4, 128), F32)], n_in=1)(sums)
        sums = lax.all_to_all(sums, REST, 0, 0, tiled=True)
    with jax.named_scope("down"):
        output, down_part = call(
            down_kernel,
            [((half, pairs, chans), BF), ((all_rows, chans), F32)],
            flops=4 * 256 * 2304 * 256,
            n_in=3,
        )(t, c2, dw3)
    h4_shape = (rows + 2, pairs, 4 * chans)
    with jax.named_scope("grad"):
        h4, conv_part, vec = call(
            functools.partial(grad_kernel, cells),
            [(h4_shape, BF, True), ((all_rows, chans), F32), ((2, chans), F32)],
            [
                ((J, chans), F32),
                ((rows + 2, J, 3 * chans), BF),
                ((rows + 2, J, 3 * chans), BF),
                ((2,) + plane, BF),
                ((2,) + plane, F32),
                (x_shape, BF),
                (h4_shape, BF),
            ],
            flops=2 * 1600 * 2304 * 256,
            smem=(0,),
            hbm=(4, 5, 6),
            n_in=7,
            sems=3 * (rows + 2) + 3,
        )(flags, sums, coef, gain, pinned(h), pinned(p), pinned(x))
    with jax.named_scope("input"):
        (input_grad,) = call(
            input_kernel,
            [((rows, cols, chans), BF)],
            [((rows, 2, cols + 8, 128), F32)],
            flops=2 * 1024 * 2304 * 256,
            n_in=2,
        )(h4, conv_weight)
    with jax.named_scope("total"):
        first = lax.axis_index("core") == 0
        other = core_swap(jnp.where(first, down_part, conv_part).astype(BF))
        mine = (jnp.where(first, conv_part, down_part) + other.astype(F32)).astype(BF)
        chips = lax.axis_size(NEAR)
        depth = lax.axis_size("z_hi")
        share = all_rows // chips
        got = lax.all_to_all(mine.reshape(chips, share, chans), NEAR, 0, 0, tiled=True)
        got, input_grad = lax.optimization_barrier((got, input_grad))
        piece = jnp.sum(got.astype(F32), axis=0).astype(BF)
        got = lax.all_to_all(jnp.broadcast_to(piece[None], (depth, share, chans)), "z_hi", 0, 0, tiled=True)
        piece = (jnp.sum(got.astype(F32), axis=0) * factor).astype(BF)
        whole = lax.all_to_all(jnp.broadcast_to(piece[None], (chips, share, chans)), NEAR, 0, 0, tiled=True)
        whole = whole.reshape(all_rows, chans)
        flat = ((all_rows, chans), F32, True)
        conv_grad, down_grad = call(
            unpack_kernel, [flat, flat], [((2, all_rows, chans), F32)], smem=(0,), n_in=3, sems=8
        )(flags, whole, core_swap(whole))
    shape = (3, 3, chans, chans)
    return output, input_grad, conv_grad.reshape(shape), down_grad.reshape(shape), vec[0], vec[1]


SIZES = {64: (4, 4, 2, 2), 2: (1, 1, 2, 1), 4: (2, 1, 2, 1), 8: (1, 2, 2, 2)}


def solution(mesh):
    lon, lat = mesh.devices.shape
    fine = Mesh(mesh.devices.reshape(SIZES[lon] + (lat // 2, 2)), ALL)
    band = P(LAT, LON, None)
    return jax.shard_map(
        local,
        mesh=fine,
        in_specs=(band, P(), P(), P(), P(), band),
        out_specs=(band, band, P(), P(), P(), P()),
        check_vma=False,
    )
```

```python
import functools
import math

import jax
import jax.numpy as jnp
from jax import lax
from jax.experimental import pallas as pl
from jax.experimental.pallas import tpu as pltpu
from jax.sharding import Mesh
from jax.sharding import PartitionSpec as P

EPS = 1e-05
WIDTH = 8
J = 80
LON = ("x", "z_hi", "z_lo", "y_hi")
LAT = ("y_lo", "core")
NEAR = ("x", "z_lo", "y_hi", "y_lo")
FEW = ("x", "core")
REST = ("z_hi", "z_lo", "y_hi", "y_lo")
ALL = LON + LAT
BF = jnp.bfloat16
F32 = jnp.float32


def call(body, outs, scratch=(), flops=0, smem=(), hbm=(), n_in=0, sems=0, aliases=None):
    spaces = [pltpu.SMEM if i in smem else pltpu.HBM if i in hbm else pltpu.VMEM for i in range(n_in)]
    out_spaces = [pltpu.HBM if len(o) > 2 else pltpu.VMEM for o in outs]
    return pl.pallas_call(
        body,
        out_shape=[pltpu.HBM(o[0], o[1]) if len(o) > 2 else jax.ShapeDtypeStruct(o[0], o[1]) for o in outs],
        in_specs=[pl.BlockSpec(memory_space=m) for m in spaces],
        out_specs=[pl.BlockSpec(memory_space=m) for m in out_spaces],
        scratch_shapes=[pltpu.VMEM(s, d) for s, d in scratch]
        + ([pltpu.SemaphoreType.DMA((sems,))] if sems else []),
        input_output_aliases=aliases or {},
        compiler_params=pltpu.CompilerParams(vmem_limit_bytes=24 * 1024 * 1024),
        cost_estimate=pl.CostEstimate(flops=flops, bytes_accessed=1 << 20, transcendentals=0),
    )


def pinned(value):
    return pltpu.with_memory_space_constraint(value, pltpu.HBM)


def dot(a, b):
    return jnp.dot(a, b, preferred_element_type=F32)


def dot_t(a, b):
    return lax.dot_general(a, b, (((1,), (1,)), ((), ())), preferred_element_type=F32)


def t_dot(a, b):
    return lax.dot_general(a, b, (((0,), (0,)), ((), ())), preferred_element_type=F32)


def exact(a, b):
    a8 = jnp.broadcast_to(a, (8, a.shape[1]))
    return jnp.dot(a8, b, preferred_element_type=F32, precision=lax.Precision.HIGHEST)[0:1]


def to_lanes(chans):
    c = lax.broadcasted_iota(jnp.int32, (chans, 128), 0) // WIDTH
    l = lax.broadcasted_iota(jnp.int32, (chans, 128), 1)
    return (c == l).astype(F32)


def from_lanes(chans):
    c = lax.broadcasted_iota(jnp.int32, (128, chans), 1) // WIDTH
    l = lax.broadcasted_iota(jnp.int32, (128, chans), 0)
    return (c == l).astype(F32)


def masks():
    j = lax.broadcasted_iota(jnp.int32, (J, 1), 0)
    odd = jnp.where((j >= 1) & (j <= 64), 1.0, 0.0)
    even = jnp.where(j <= 63, 1.0, 0.0)
    return odd, even


def pack_lon(feat_hbm, cot_hbm, east, west, feat, cot, f32s, sems):
    rows, cols, chans = feat_hbm.shape
    half, pairs, _ = cot_hbm.shape
    copies = []
    for k, (lo_f, lo_c) in enumerate(((cols - 16, pairs - 16), (0, 0))):
        copies.append(pltpu.make_async_copy(feat_hbm.at[:, lo_f : lo_f + 16], feat.at[k], sems.at[2 * k]))
        copies.append(pltpu.make_async_copy(cot_hbm.at[:, lo_c : lo_c + 16], cot.at[k], sems.at[2 * k + 1]))
    for copy in copies:
        copy.start()
    f32s[...] = jnp.zeros(f32s.shape, F32)
    for copy in copies:
        copy.wait()
    for k, (out, at_f, at_c) in enumerate(((east, 14, 15), (west, 0, 0))):
        for r in range(rows):
            f32s[2 * r : 2 * r + 2] = feat[k, r].astype(F32)[at_f : at_f + 2]
        for i in range(half):
            f32s[2 * rows + i : 2 * rows + i + 1] = cot[k, i].astype(F32)[at_c : at_c + 1]
        out[...] = f32s[...].astype(BF)


def pack_lat(flags, feat, cot, west, east, near, far, w32, e32, corner, sems):
    rows, cols, _ = feat.shape
    half, pairs, _ = cot.shape
    core = flags[2]
    copies = []
    for dest, last in ((near, 1 - core), (far, core)):
        top, mid = last * (rows - 2), last * (half - 1)
        parts = [(feat.at[top + k], k * cols, cols) for k in range(2)]
        parts.append((cot.at[mid], 2 * cols, pairs))
        for src, o, n in parts:
            copies.append(pltpu.make_async_copy(src, dest.at[o : o + n], sems.at[len(copies)]))
            copies[-1].start()
    w32[...] = west[...].astype(F32)
    e32[...] = east[...].astype(F32)
    corner[...] = jnp.zeros(corner.shape, F32)
    for k, (top, mid) in enumerate(((rows - 2, half - 1), (0, 0))):
        corner[k, 0:4] = w32[2 * top : 2 * top + 4]
        corner[k, 4:8] = e32[2 * top : 2 * top + 4]
        corner[k, 8:9] = w32[2 * rows + mid : 2 * rows + mid + 1]
        corner[k, 9:10] = e32[2 * rows + mid : 2 * rows + mid + 1]
    o = 2 * cols + pairs
    near[o : o + 16] = corner[core].astype(BF)
    far[o : o + 16] = corner[1 - core].astype(BF)
    for copy in copies:
        copy.wait()


def sides(flags, near, far):
    low = flags[2] == 0

    def north(lo, hi, part):
        return jnp.where(low, far[lo:hi, part].astype(F32), near[lo:hi, part].astype(F32))

    def south(lo, hi, part):
        return jnp.where(low, near[lo:hi, part].astype(F32), far[lo:hi, part].astype(F32))

    return north, south


def conv_kernel(
    flags, feat_hbm, west, east, near, far, w_hbm, x_hbm, h_hbm, hq_out, he_out, stat_out, f32s, edge, x_out, feat, w, sems
):
    rows, cols, chans = feat.shape
    load_f = pltpu.make_async_copy(feat_hbm, feat, sems.at[1])
    load_f.start()
    load_w = pltpu.make_async_copy(w_hbm, w, sems.at[2])
    load_w.start()
    f32s[:, :, 16 + cols : 56 + cols] = jnp.zeros((rows + 4, 2, 40, 128), F32)
    pairs = cols // 2
    for v in range(2):
        part = slice(v * 128, v * 128 + 128)
        for k, side in enumerate((west, east)):
            edge[k, v] = side[:, part].astype(F32)
        for k, side in enumerate(sides(flags, near, far)):
            edge[2 + k, v, 0:16] = side(2 * cols + pairs, 2 * cols + pairs + 16, part)
            for q in range(2):
                row = q + k * (rows + 2)
                f32s[row, v, 16 : 16 + cols] = side(q * cols, (q + 1) * cols, part)
                f32s[row, v, 14:16] = edge[2 + k, v, 2 * q : 2 * q + 2]
                f32s[row, v, 16 + cols : 18 + cols] = edge[2 + k, v, 4 + 2 * q : 6 + 2 * q]
        for r in range(rows):
            f32s[2 + r, v, 14:16] = edge[0, v, 2 * r : 2 * r + 2]
            f32s[2 + r, v, 16 + cols : 18 + cols] = edge[1, v, 2 * r : 2 * r + 2]
    load_f.wait()
    for v in range(2):
        part = slice(v * 128, v * 128 + 128)
        f32s[2 : rows + 2, v, 16 : 16 + cols] = feat[:, :, part].astype(F32)
        for r in range(rows + 4):
            for k in range(5):
                lane = k * chans + v * 128
                x_out[r, :, lane : lane + 128] = f32s[r, v, pl.ds(14 + k, J, stride=2), :].astype(BF)
    kept = x_out.at[1 : rows + 3, 0:pairs, chans : 5 * chans]
    keep = pltpu.make_async_copy(kept, x_hbm, sems.at[0])
    keep.start()
    load_w.wait()
    copies = [keep]
    odd, even = masks()
    sums = jnp.zeros((1, chans), F32)
    for out, lo in ((hq_out, 0), (he_out, chans)):
        acc = None
        for a in range(3):
            lhs = x_out[a : a + rows + 2, :, lo : lo + 3 * chans].reshape((rows + 2) * J, 3 * chans)
            term = dot(lhs, w[a])
            acc = term if acc is None else acc + term
        out[...] = acc.astype(BF).reshape(rows + 2, J, chans)
        k = lo // chans
        copies.append(pltpu.make_async_copy(out, h_hbm.at[k], sems.at[3 + k]))
        copies[-1].start()
    for out, mask in ((hq_out, odd), (he_out, even)):
        part = jnp.zeros((J, chans), F32)
        for r in range(1, rows + 1):
            part = part + out[r].astype(F32)
        sums = sums + jnp.sum(part * mask, axis=0, keepdims=True)
    lanes = to_lanes(chans)
    means = exact(sums, lanes) / (rows * cols * WIDTH)
    mean = exact(means, from_lanes(chans))
    squares = jnp.zeros((1, chans), F32)
    for out, mask in ((hq_out, odd), (he_out, even)):
        part = jnp.zeros((J, chans), F32)
        for r in range(1, rows + 1):
            d = out[r].astype(F32) - mean
            part = part + d * d
        squares = squares + jnp.sum(part * mask, axis=0, keepdims=True)
    stat = jnp.concatenate([means, exact(squares, lanes)], axis=0)
    stat_out[...] = jnp.broadcast_to(stat[None], stat_out.shape)
    for copy in copies:
        copy.wait()


def merged_stats(local_n, rec, out):
    means = rec[:, 0, :]
    mean = jnp.sum(means, axis=0, keepdims=True) / rec.shape[0]
    gap = means - mean
    squares = jnp.sum(rec[:, 1, :] + local_n * gap * gap, axis=0, keepdims=True)
    both = jnp.concatenate([mean, squares], axis=0)
    out[...] = jnp.broadcast_to(both[None], out.shape)


def merged_sums(rec, out):
    out[...] = jnp.broadcast_to(jnp.sum(rec[...], axis=0)[None], out.shape)


def back_kernel(flags, cot, west, east, near, far, dw, c_hbm, aq_out, ae_out, f32s, edge, c_out, sems):
    half, pairs, chans = cot.shape
    rows = 2 * half
    cols = 2 * pairs
    f32s[:, 16 + pairs :] = jnp.zeros((half + 2, 16, chans), F32)
    for k, side in enumerate((west, east)):
        edge[k] = side[...].astype(F32)
    every = slice(None)
    for k, side in enumerate(sides(flags, near, far)):
        row = k * (half + 1)
        f32s[row, 16 : 16 + pairs] = side(2 * cols, 2 * cols + pairs, every)
        edge[2 + k, 0:16] = side(2 * cols + pairs, 2 * cols + pairs + 16, every)
        f32s[row, 15:16] = edge[2 + k, 8:9]
        f32s[row, 16 + pairs : 17 + pairs] = edge[2 + k, 9:10]
    f32s[1 : half + 1, 16 : 16 + pairs] = cot[...].astype(F32)
    for i in range(half):
        f32s[1 + i, 15:16] = edge[0, 2 * rows + i : 2 * rows + i + 1]
        f32s[1 + i, 16 + pairs : 17 + pairs] = edge[1, 2 * rows + i : 2 * rows + i + 1]
    for s in range(half + 2):
        c_out[s, :, 0:chans] = f32s[s, 15 : 15 + J].astype(BF)
        c_out[s, :, chans : 2 * chans] = f32s[s, 16 : 16 + J].astype(BF)
    keep = pltpu.make_async_copy(c_out, c_hbm, sems.at[0])
    keep.start()
    n = half + 1
    lo_l = c_out[0:n, :, 0:chans].reshape(n * J, chans)
    lo_r = c_out[0:n, :, chans:].reshape(n * J, chans)
    hi_l = c_out[1 : n + 1, :, 0:chans].reshape(n * J, chans)
    hi_r = c_out[1 : n + 1, :, chans:].reshape(n * J, chans)

    def put(out, k, value):
        value = value.astype(BF).reshape(n, J, chans)
        for i in range(n):
            out[2 * i + k] = value[i]

    put(ae_out, 1, dot_t(hi_r, dw[1, 1]))
    put(aq_out, 1, dot_t(hi_r, dw[1, 0]) + dot_t(hi_l, dw[1, 2]))
    put(ae_out, 0, dot_t(hi_r, dw[0, 1]) + dot_t(lo_r, dw[2, 1]))
    put(
        aq_out,
        0,
        dot_t(hi_r, dw[0, 0]) + dot_t(hi_l, dw[0, 2]) + dot_t(lo_r, dw[2, 0]) + dot_t(lo_l, dw[2, 2]),
    )
    keep.wait()


def act_kernel(cells, flags, stats, hq, he, aq, ae, gain, bias, t_hbm, p_hbm, coef_out, sum_out, f32s, t_out, p_out, sems):
    parts = stats.shape[0]
    rows = hq.shape[0] - 2
    chans = hq.shape[2]
    part_n = float(cells // parts * WIDTH)
    count = float(cells * WIDTH)
    rec = stats[...]
    total = jnp.sum(rec, axis=0)
    centre = total[0:1] / parts
    dev = rec[:, 0, :] - centre
    spread = jnp.sum(dev * dev, axis=0, keepdims=True)
    back = from_lanes(chans)
    mean = exact(centre, back)
    var = exact((total[1:2] + part_n * spread) / count, back)
    inverse = lax.rsqrt(var + EPS)
    coef_out[0:1] = mean
    coef_out[1:2] = inverse
    g = gain[...]
    b = bias[...]
    odd, even = masks()
    top = jnp.where(flags[0] == 1, 0.0, 1.0)
    bias_sum = jnp.zeros((1, chans), F32)
    gain_sum = jnp.zeros((1, chans), F32)
    copies = []
    for k, (h, a, mask) in enumerate(((hq, aq, odd), (he, ae, even))):
        is_q = k == 0
        acc_b = jnp.zeros((J, chans), F32)
        acc_g = jnp.zeros((J, chans), F32)
        for r in range(rows + 2):
            normed = (h[r].astype(F32) - mean) * inverse
            shifted = g * normed + b
            sigma = 0.5 + 0.5 * jnp.tanh(0.5 * shifted)
            pre = a[r].astype(F32) * sigma * (1.0 + shifted * (1.0 - sigma))
            p_out[k, r] = pre
            copies.append(pltpu.make_async_copy(p_out.at[k, r], p_hbm.at[k, r], sems.at[len(copies)]))
            copies[-1].start()
            if 1 <= r <= rows:
                acc_b = acc_b + pre
                acc_g = acc_g + pre * normed
            if r <= rows:
                active = shifted * sigma
                if r == 0:
                    active = active * top
                if is_q:
                    f32s[...] = active.astype(BF).astype(F32)
                    t_out[r, :, 0:chans] = active[0:64].astype(BF)
                    t_out[r, :, 2 * chans :] = f32s[1:65].astype(BF)
                else:
                    t_out[r, :, chans : 2 * chans] = active[0:64].astype(BF)
                    copies.append(pltpu.make_async_copy(t_out.at[r], t_hbm.at[r], sems.at[len(copies)]))
                    copies[-1].start()
        bias_sum = bias_sum + jnp.sum(acc_b * mask, axis=0, keepdims=True)
        gain_sum = gain_sum + jnp.sum(acc_g * mask, axis=0, keepdims=True)
    payload = jnp.concatenate(
        [bias_sum[:, 0:128], bias_sum[:, 128:256], gain_sum[:, 0:128], gain_sum[:, 128:256]], axis=0
    )
    sum_out[...] = jnp.broadcast_to(payload[None], sum_out.shape)
    for copy in copies:
        copy.wait()


def halves(flags, full, keep, send):
    n = keep.shape[0]
    core = flags[2]
    keep[...] = full[pl.ds(pl.multiple_of(core * n, n), n)]
    send[...] = full[pl.ds(pl.multiple_of((1 - core) * n, n), n)].astype(BF)


def down_kernel(flags, t_hbm, c_hbm, dw, out, keep, send, t, c, grad, sems):
    half = out.shape[0]
    pairs, chans = out.shape[1:]
    loads = [pltpu.make_async_copy(t_hbm, t, sems.at[0]), pltpu.make_async_copy(c_hbm, c, sems.at[1])]
    for load in loads:
        load.start()
    for load in loads:
        load.wait()
    cot = c[1 : half + 1, 0:pairs, chans:].reshape(half * pairs, chans)
    acc = None
    for a in range(3):
        lhs = jnp.concatenate([t[2 * i + a] for i in range(half)], axis=0)
        term = dot(lhs, dw[a])
        acc = term if acc is None else acc + term
        grad[a * 3 * chans : (a + 1) * 3 * chans] = t_dot(lhs, cot)
    out[...] = acc.astype(BF).reshape(out.shape)
    halves(flags, grad, keep, send)


def grad_kernel(
    cells, flags, sums, coef, gain, h_hbm, p_hbm, x_hbm, h4_hbm, keep, send, vec_out, f32s, conv_out, h_in, p_in, x, h4_out, sems
):
    rows = p_in.shape[1] - 2
    chans = p_in.shape[3]
    loads = []
    for k in range(2):
        loads.append(pltpu.make_async_copy(h_hbm.at[k], h_in.at[k], sems.at[len(loads)]))
        loads[-1].start()
        for r in range(rows + 2):
            loads.append(pltpu.make_async_copy(p_hbm.at[k, r], p_in.at[k, r], sems.at[len(loads)]))
            loads[-1].start()
    load_x = pltpu.make_async_copy(x_hbm, x, sems.at[len(loads)])
    load_x.start()
    first_out = len(loads) + 1
    copies = []
    count = float(cells * WIDTH)
    total = jnp.sum(sums[...], axis=0)
    bias_sum = jnp.concatenate([total[0:1], total[1:2]], axis=1)
    gain_sum = jnp.concatenate([total[2:3], total[3:4]], axis=1)
    factor = 1.0 / math.sqrt(cells)
    vec_out[0:1] = gain_sum * factor
    vec_out[1:2] = bias_sum * factor
    g = gain[...]
    lanes, back = to_lanes(chans), from_lanes(chans)
    first = exact(exact(g * bias_sum, lanes), back) / count
    second = exact(exact(g * gain_sum, lanes), back) / count
    mean = coef[0:1]
    inverse = coef[1:2]
    top = jnp.where(flags[0] == 1, 0.0, 1.0)
    bottom = jnp.where(flags[1] == 1, 0.0, 1.0)
    for k in range(2):
        is_q = k == 0
        loads[k * (rows + 3)].wait()
        for r in range(rows + 2):
            loads[k * (rows + 3) + 1 + r].wait()
            normed = (h_in[k, r].astype(F32) - mean) * inverse
            value = inverse * (g * p_in[k, r] - first - normed * second)
            if r == 0:
                value = value * top
            if r == rows + 1:
                value = value * bottom
            rounded = value.astype(BF)
            f32s[...] = rounded.astype(F32)
            moved = f32s[1:65].astype(BF)
            lo = 3 if is_q else 2
            h4_out[r, :, lo * chans : (lo + 1) * chans] = rounded[0:64]
            lo = 1 if is_q else 0
            h4_out[r, :, lo * chans : (lo + 1) * chans] = moved
            if not is_q:
                copies.append(pltpu.make_async_copy(h4_out.at[r], h4_hbm.at[r], sems.at[first_out + r]))
                copies[-1].start()
    load_x.wait()
    pairs = h4_out.shape[1]
    cells_here = rows * pairs
    odd = h4_out[1 : rows + 1, :, chans : 2 * chans].reshape(cells_here, chans)
    even = h4_out[1 : rows + 1, :, 2 * chans : 3 * chans].reshape(cells_here, chans)
    for a in range(3):
        lhs = x[a : a + rows].reshape(cells_here, 4 * chans)
        part = t_dot(lhs[:, 0 : 3 * chans], even) + t_dot(lhs[:, chans : 4 * chans], odd)
        conv_out[a * 3 * chans : (a + 1) * 3 * chans] = part
    halves(flags, conv_out, keep, send)
    for copy in copies:
        copy.wait()


def input_kernel(h4, w, out, f32s):
    rows, cols, chans = out.shape
    for k, lo in ((0, 1), (1, 0)):
        acc = None
        for a in range(3):
            for b in range(3):
                lane = (lo + b) * chans
                lhs = h4[2 - a : 2 - a + rows, :, lane : lane + chans].reshape(rows * (cols // 2), chans)
                term = dot_t(lhs, w[a, b])
                acc = term if acc is None else acc + term
        acc = acc.reshape(rows, cols // 2, chans)
        for r in range(rows):
            for v in range(2):
                f32s[r, v, pl.ds(k, cols // 2, stride=2), :] = acc[r, :, v * 128 : v * 128 + 128]
    for v in range(2):
        out[:, :, v * 128 : v * 128 + 128] = f32s[:, v, 0:cols].astype(BF)


def passed(value, axes, step, wrap):
    n = lax.axis_size(axes)
    pairs = [(i, (i + step) % n) for i in range(n) if wrap or 0 <= i + step < n]
    return lax.ppermute(value, axes, pairs)


def join_kernel(conv_keep, conv_other, down_keep, down_other, out, both, sems):
    n = conv_keep.shape[0]
    step = n // 2
    copies = []
    for k, (keep, other) in enumerate(((down_keep, down_other), (conv_keep, conv_other))):
        for q in range(2):
            part = slice(q * step, (q + 1) * step)
            o = (1 - k) * n + q * step
            both[o : o + step] = (keep[part] + other[part].astype(F32)).astype(BF)
            copies.append(pltpu.make_async_copy(both.at[o : o + step], out.at[o : o + step], sems.at[2 * k + q]))
            copies[-1].start()
    for copy in copies:
        copy.wait()


def unpack_rows(core, rows, conv, down, f32s, sems):
    n = rows.shape[0] // 2
    step = n // 2
    base = pl.multiple_of(core * n, n)
    copies = []
    for k, dst in enumerate((conv, down)):
        for q in range(2):
            o = k * n + q * step
            f32s[o : o + step] = rows[o : o + step].astype(F32)
            part = dst.at[pl.ds(base + q * step, step)]
            copies.append(pltpu.make_async_copy(f32s.at[o : o + step], part, sems.at[k * 2 + q]))
            copies[-1].start()
    for copy in copies:
        copy.wait()


def unpack_own(flags, rows, conv, down, f32s, sems):
    unpack_rows(flags[2], rows, conv, down, f32s, sems)


def unpack_other(flags, rows, conv_in, down_in, conv, down, f32s, sems):
    unpack_rows(1 - flags[2], rows, conv, down, f32s, sems)


def core_swap(value):
    return lax.ppermute(value, "core", [(0, 1), (1, 0)])


def local(features, conv_weight, down_weight, norm_gain, norm_bias, cotangent):
    rows, cols, chans = features.shape
    half, pairs, _ = cotangent.shape
    devices = lax.axis_size(ALL)
    lats = lax.axis_size(LAT)
    cells = rows * cols * devices
    factor = 1.0 / math.sqrt(cells)
    lat = lax.axis_index(LAT)
    flags = jnp.stack([lat == 0, lat == lats - 1, lax.axis_index("core") == 1]).astype(jnp.int32)
    gain = norm_gain.reshape(1, chans)
    bias = norm_bias.reshape(1, chans)
    w3 = conv_weight.reshape(3, 3 * chans, chans)
    dw3 = down_weight.reshape(3, 3 * chans, chans)
    all_rows = 9 * chans
    few = lax.axis_size(FEW)
    rest = lax.axis_size(REST)

    with jax.named_scope("halo"):
        slab = (2 * rows + 16, chans)
        to_east, to_west = call(
            pack_lon,
            [(slab, BF)] * 2,
            [((2, rows, 16, chans), BF), ((2, half, 16, chans), BF), (slab, F32)],
            n_in=2,
            hbm=(0, 1),
            sems=4,
        )(pinned(features), pinned(cotangent))
        west = passed(to_east, LON, 1, True)
        east = passed(to_west, LON, -1, True)
        strip = (2 * cols + pairs + 16, chans)
        to_near, to_far = call(
            pack_lat,
            [(strip, BF)] * 2,
            [(slab, F32), (slab, F32), ((2, 16, chans), F32)],
            n_in=5,
            smem=(0,),
            hbm=(1, 2),
            sems=6,
        )(flags, pinned(features), pinned(cotangent), west, east)
        near = lax.ppermute(to_near, LAT, [(i, i ^ 1) for i in range(lats)])
        gaps = range(1, lats - 1, 2)
        far = lax.ppermute(to_far, LAT, [(i, i + 1) for i in gaps] + [(i + 1, i) for i in gaps])

    plane = (rows + 2, J, chans)
    x_shape = (rows + 2, pairs, 4 * chans)
    x_full = (rows + 4, J, 5 * chans)
    with jax.named_scope("conv"):
        x, h, hq, he, stat = call(
            conv_kernel,
            [(x_shape, BF, True), ((2,) + plane, BF, True), (plane, BF), (plane, BF), ((few, 2, 128), F32)],
            [((rows + 4, 2, cols + 56, 128), F32), ((4, 2) + (slab[0], 128), F32), (x_full, BF), ((rows, cols, chans), BF), (w3.shape, BF)],
            flops=2 * 1600 * 2304 * 256,
            n_in=7,
            smem=(0,),
            hbm=(1, 6),
            sems=5,
        )(flags, pinned(features), west, east, near, far, pinned(w3))
        local_n = float(rows * cols * WIDTH)
        stat = lax.all_to_all(stat, FEW, 0, 0, tiled=True)
        (stat,) = call(functools.partial(merged_stats, local_n), [((rest, 2, 128), F32)], n_in=1)(stat)
        stats = lax.all_to_all(stat, REST, 0, 0, tiled=True)
    c_shape = (half + 2, J, 2 * chans)
    with jax.named_scope("back"):
        c2, aq, ae = call(
            back_kernel,
            [(c_shape, BF, True), (plane, BF), (plane, BF)],
            [((half + 2, pairs + 32, chans), F32), ((4,) + slab, F32), (c_shape, BF)],
            flops=2 * 400 * 2304 * 256,
            n_in=7,
            smem=(0,),
            sems=1,
        )(flags, cotangent, west, east, near, far, down_weight)
    t_shape = (rows + 1, pairs, 3 * chans)
    with jax.named_scope("act"):
        t, p, coef, sums = call(
            functools.partial(act_kernel, cells),
            [(t_shape, BF, True), ((2,) + plane, F32, True), ((2, chans), F32), ((few, 4, 128), F32)],
            [((J, chans), F32), (t_shape, BF), ((2,) + plane, F32)],
            flops=1600 * 256 * 20,
            smem=(0,),
            n_in=8,
            sems=3 * rows + 5,
        )(flags, stats, hq, he, aq, ae, gain, bias)
        sums = lax.all_to_all(sums, FEW, 0, 0, tiled=True)
        (sums,) = call(merged_sums, [((rest, 4, 128), F32)], n_in=1)(sums)
        sums, c2 = lax.optimization_barrier((sums, c2))
        sums = lax.all_to_all(sums, REST, 0, 0, tiled=True)
    half_rows = (all_rows // 2, chans)
    with jax.named_scope("down"):
        output, down_keep, down_send = call(
            down_kernel,
            [((half, pairs, chans), BF), (half_rows, F32), (half_rows, BF)],
            [(t_shape, BF), (c_shape, BF), ((all_rows, chans), F32)],
            flops=4 * 256 * 2304 * 256,
            smem=(0,),
            hbm=(1, 2),
            n_in=4,
            sems=2,
        )(flags, pinned(t), pinned(c2), dw3)
        down_other = core_swap(down_send)
    h4_shape = (rows + 2, pairs, 4 * chans)
    with jax.named_scope("grad"):
        h4, conv_keep, conv_send, vec = call(
            functools.partial(grad_kernel, cells),
            [(h4_shape, BF, True), (half_rows, F32), (half_rows, BF), ((2, chans), F32)],
            [
                ((J, chans), F32),
                ((all_rows, chans), F32),
                ((2,) + plane, BF),
                ((2,) + plane, F32),
                (x_shape, BF),
                (h4_shape, BF),
            ],
            flops=2 * 1600 * 2304 * 256,
            smem=(0,),
            hbm=(4, 5, 6),
            n_in=7,
            sems=3 * (rows + 2) + 3,
        )(flags, sums, coef, gain, pinned(h), pinned(p), pinned(x))
    with jax.named_scope("input"):
        (input_grad,) = call(
            input_kernel,
            [((rows, cols, chans), BF)],
            [((rows, 2, cols + 8, 128), F32)],
            flops=2 * 1024 * 2304 * 256,
            n_in=2,
        )(h4, conv_weight)
    with jax.named_scope("total"):
        whole_rows = (all_rows, chans)
        (mine,) = call(
            join_kernel, [(whole_rows, BF, True)], [(whole_rows, BF)], n_in=4, sems=4
        )(conv_keep, core_swap(conv_send), down_keep, down_other)
        chips = lax.axis_size(NEAR)
        depth = lax.axis_size("z_hi")
        share = all_rows // chips
        got = lax.all_to_all(mine.reshape(chips, share, chans), NEAR, 0, 0, tiled=True)
        got, input_grad = lax.optimization_barrier((got, input_grad))
        piece = jnp.sum(got.astype(F32), axis=0).astype(BF)
        got = lax.all_to_all(jnp.broadcast_to(piece[None], (depth, share, chans)), "z_hi", 0, 0, tiled=True)
        piece = (jnp.sum(got.astype(F32), axis=0) * factor).astype(BF)
        whole = lax.all_to_all(jnp.broadcast_to(piece[None], (chips, share, chans)), NEAR, 0, 0, tiled=True)
        whole = whole.reshape(all_rows, chans)
        other = core_swap(whole)
        flat = (whole_rows, F32, True)
        room = [(whole_rows, F32)]
        conv_grad, down_grad = call(unpack_own, [flat, flat], room, smem=(0,), n_in=2, sems=4)(flags, whole)
        conv_grad, down_grad = call(
            unpack_other, [flat, flat], room, smem=(0,), hbm=(2, 3), n_in=4, sems=4, aliases={2: 0, 3: 1}
        )(flags, other, pinned(conv_grad), pinned(down_grad))
    shape = (3, 3, chans, chans)
    return output, input_grad, conv_grad.reshape(shape), down_grad.reshape(shape), vec[0], vec[1]


SIZES = {64: (4, 4, 2, 2), 2: (1, 1, 2, 1), 4: (2, 1, 2, 1), 8: (1, 2, 2, 2)}


def solution(mesh):
    lon, lat = mesh.devices.shape
    fine = Mesh(mesh.devices.reshape(SIZES[lon] + (lat // 2, 2)), ALL)
    band = P(LAT, LON, None)
    return jax.shard_map(
        local,
        mesh=fine,
        in_specs=(band, P(), P(), P(), P(), band),
        out_specs=(band, band, P(), P(), P(), P()),
        check_vma=False,
    )
```

```python
import functools
import math

import jax
import jax.numpy as jnp
from jax import lax
from jax.experimental import pallas as pl
from jax.experimental.pallas import tpu as pltpu
from jax.sharding import Mesh
from jax.sharding import PartitionSpec as P

EPS = 1e-05
WIDTH = 8
J = 80
LON = ("x", "z_hi", "z_lo", "y_hi")
LAT = ("y_lo", "core")
NEAR = ("x", "z_lo", "y_hi", "y_lo")
FEW = ("x", "core")
REST = ("z_hi", "z_lo", "y_hi", "y_lo")
ALL = LON + LAT
BF = jnp.bfloat16
F32 = jnp.float32


def call(body, outs, scratch=(), flops=0, smem=(), hbm=(), n_in=0, sems=0, aliases=None):
    spaces = [pltpu.SMEM if i in smem else pltpu.HBM if i in hbm else pltpu.VMEM for i in range(n_in)]
    out_spaces = [pltpu.HBM if len(o) > 2 else pltpu.VMEM for o in outs]
    return pl.pallas_call(
        body,
        out_shape=[pltpu.HBM(o[0], o[1]) if len(o) > 2 else jax.ShapeDtypeStruct(o[0], o[1]) for o in outs],
        in_specs=[pl.BlockSpec(memory_space=m) for m in spaces],
        out_specs=[pl.BlockSpec(memory_space=m) for m in out_spaces],
        scratch_shapes=[pltpu.VMEM(s, d) for s, d in scratch]
        + ([pltpu.SemaphoreType.DMA((sems,))] if sems else []),
        input_output_aliases=aliases or {},
        compiler_params=pltpu.CompilerParams(vmem_limit_bytes=24 * 1024 * 1024),
        cost_estimate=pl.CostEstimate(flops=flops, bytes_accessed=1 << 20, transcendentals=0),
    )


def pinned(value):
    return pltpu.with_memory_space_constraint(value, pltpu.HBM)


def dot(a, b):
    return jnp.dot(a, b, preferred_element_type=F32)


def dot_t(a, b):
    return lax.dot_general(a, b, (((1,), (1,)), ((), ())), preferred_element_type=F32)


def t_dot(a, b):
    return lax.dot_general(a, b, (((0,), (0,)), ((), ())), preferred_element_type=F32)


def spread_dot(table, *vectors):
    parts = []
    for v in vectors:
        high = v.astype(BF).astype(F32)
        mid = (v - high).astype(BF).astype(F32)
        parts += [high, mid, v - high - mid]
    parts.append(jnp.zeros((8 - len(parts), vectors[0].shape[1]), F32))
    out = dot(jnp.concatenate(parts, axis=0).astype(BF), table)
    return [out[3 * i : 3 * i + 1] + out[3 * i + 1 : 3 * i + 2] + out[3 * i + 2 : 3 * i + 3] for i in range(len(vectors))]


def table(n, m, row_width, col_width, shift):
    r = lax.broadcasted_iota(jnp.int32, (n, m), 0) // row_width
    c = lax.broadcasted_iota(jnp.int32, (n, m), 1) // col_width
    return jnp.where(r == c + shift, 1.0, 0.0).astype(BF)


def masks():
    j = lax.broadcasted_iota(jnp.int32, (J, 1), 0)
    odd = jnp.where((j >= 1) & (j <= 64), 1.0, 0.0)
    even = jnp.where(j <= 63, 1.0, 0.0)
    return odd, even


def pack_lon(feat_hbm, cot_hbm, east, west, feat, cot, f32s, sems):
    rows, cols, chans = feat_hbm.shape
    half, pairs, _ = cot_hbm.shape
    copies = []
    for k, (lo_f, lo_c) in enumerate(((cols - 16, pairs - 16), (0, 0))):
        copies.append(pltpu.make_async_copy(feat_hbm.at[:, lo_f : lo_f + 16], feat.at[k], sems.at[2 * k]))
        copies.append(pltpu.make_async_copy(cot_hbm.at[:, lo_c : lo_c + 16], cot.at[k], sems.at[2 * k + 1]))
    for copy in copies:
        copy.start()
    f32s[...] = jnp.zeros(f32s.shape, F32)
    for copy in copies:
        copy.wait()
    for k, (out, at_f, at_c) in enumerate(((east, 14, 15), (west, 0, 0))):
        for r in range(rows):
            f32s[2 * r : 2 * r + 2] = feat[k, r].astype(F32)[at_f : at_f + 2]
        for i in range(half):
            f32s[2 * rows + i : 2 * rows + i + 1] = cot[k, i].astype(F32)[at_c : at_c + 1]
        out[...] = f32s[...].astype(BF)


def pack_lat(flags, feat, cot, west, east, near, far, w32, e32, corner, sems):
    rows, cols, _ = feat.shape
    half, pairs, _ = cot.shape
    core = flags[2]
    copies = []
    for dest, last in ((near, 1 - core), (far, core)):
        top, mid = last * (rows - 2), last * (half - 1)
        parts = [(feat.at[top + k], k * cols, cols) for k in range(2)]
        parts.append((cot.at[mid], 2 * cols, pairs))
        for src, o, n in parts:
            copies.append(pltpu.make_async_copy(src, dest.at[o : o + n], sems.at[len(copies)]))
            copies[-1].start()
    w32[...] = west[...].astype(F32)
    e32[...] = east[...].astype(F32)
    corner[...] = jnp.zeros(corner.shape, F32)
    for k, (top, mid) in enumerate(((rows - 2, half - 1), (0, 0))):
        corner[k, 0:4] = w32[2 * top : 2 * top + 4]
        corner[k, 4:8] = e32[2 * top : 2 * top + 4]
        corner[k, 8:9] = w32[2 * rows + mid : 2 * rows + mid + 1]
        corner[k, 9:10] = e32[2 * rows + mid : 2 * rows + mid + 1]
    o = 2 * cols + pairs
    near[o : o + 16] = corner[core].astype(BF)
    far[o : o + 16] = corner[1 - core].astype(BF)
    for copy in copies:
        copy.wait()


def sides(flags, near, far):
    low = flags[2] == 0

    def north(lo, hi, part):
        return jnp.where(low, far[lo:hi, part].astype(F32), near[lo:hi, part].astype(F32))

    def south(lo, hi, part):
        return jnp.where(low, near[lo:hi, part].astype(F32), far[lo:hi, part].astype(F32))

    return north, south


def taps(f32s, x_out, rows, lanes):
    for r in range(rows):
        for v in range(2):
            for k in range(lanes):
                lane = k * 256 + v * 128
                x_out[r, :, lane : lane + 128] = f32s[r, v, pl.ds(14 + k, J, stride=2), :].astype(BF)


def inner_kernel(feat_hbm, west, east, w_hbm, x_hbm, rim, hq_out, he_out, f32s, edge, x_out, feat, w, sems):
    rows, cols, chans = feat.shape
    pairs = cols // 2
    load_f = pltpu.make_async_copy(feat_hbm, feat, sems.at[1])
    load_f.start()
    load_w = pltpu.make_async_copy(w_hbm, w, sems.at[2])
    load_w.start()
    f32s[:, :, 16 + cols : 56 + cols] = jnp.zeros((rows, 2, 40, 128), F32)
    for v in range(2):
        part = slice(v * 128, v * 128 + 128)
        for k, side in enumerate((west, east)):
            edge[k, v] = side[:, part].astype(F32)
        for r in range(rows):
            f32s[r, v, 14:16] = edge[0, v, 2 * r : 2 * r + 2]
            f32s[r, v, 16 + cols : 18 + cols] = edge[1, v, 2 * r : 2 * r + 2]
    load_f.wait()
    for v in range(2):
        f32s[:, v, 16 : 16 + cols] = feat[:, :, v * 128 : v * 128 + 128].astype(F32)
    taps(f32s, x_out, rows, 5)
    keep = pltpu.make_async_copy(x_out.at[:, 0:pairs, chans : 5 * chans], x_hbm, sems.at[0])
    keep.start()
    for i, r in enumerate((0, 1, rows - 2, rows - 1)):
        rim[i] = x_out[r, :, 0 : 4 * chans]
    load_w.wait()
    n = rows - 2
    for out, lo in ((hq_out, 0), (he_out, chans)):
        acc = None
        for a in range(3):
            lhs = x_out[a : a + n, :, lo : lo + 3 * chans].reshape(n * J, 3 * chans)
            term = dot(lhs, w[a])
            acc = term if acc is None else acc + term
        out[...] = acc.astype(BF).reshape(n, J, chans)
    keep.wait()


def outer_kernel(
    cols, flags, near, far, rim, hq_in, he_in, w_hbm, x_hbm, h_hbm, hq_out, he_out, stat_out, f32s, edge, x_out, w, sems
):
    rows = hq_in.shape[0] + 2
    chans = hq_in.shape[2]
    pairs = cols // 2
    load_w = pltpu.make_async_copy(w_hbm, w, sems.at[0])
    load_w.start()
    f32s[:, :, 16 + cols : 56 + cols] = jnp.zeros((4, 2, 40, 128), F32)
    for v in range(2):
        part = slice(v * 128, v * 128 + 128)
        for k, side in enumerate(sides(flags, near, far)):
            edge[k, v] = side(2 * cols + pairs, 2 * cols + pairs + 16, part)
            for q in range(2):
                row = q + 2 * k
                f32s[row, v, 16 : 16 + cols] = side(q * cols, (q + 1) * cols, part)
                f32s[row, v, 14:16] = edge[k, v, 2 * q : 2 * q + 2]
                f32s[row, v, 16 + cols : 18 + cols] = edge[k, v, 4 + 2 * q : 6 + 2 * q]
    taps(f32s, x_out, 4, 5)
    copies = []
    for i, r in enumerate((1, 2)):
        copies.append(pltpu.make_async_copy(x_out.at[r, 0:pairs, chans : 5 * chans], x_hbm.at[i], sems.at[1 + i]))
        copies[-1].start()
    hq_out[2:rows] = hq_in[...]
    he_out[2:rows] = he_in[...]
    load_w.wait()
    wanted = (
        ((x_out, 0), (x_out, 1), (rim, 2), (rim, 3)),
        ((x_out, 1), (rim, 0), (rim, 3), (x_out, 2)),
        ((rim, 0), (rim, 1), (x_out, 2), (x_out, 3)),
    )
    for k, out in enumerate((hq_out, he_out)):
        lo = k * chans
        acc = None
        for a in range(3):
            lhs = jnp.concatenate([ref[r, :, lo : lo + 3 * chans] for ref, r in wanted[a]], axis=0)
            term = dot(lhs, w[a])
            acc = term if acc is None else acc + term
        value = acc.astype(BF).reshape(4, J, chans)
        out[0:2] = value[0:2]
        out[rows : rows + 2] = value[2:4]
        copies.append(pltpu.make_async_copy(out, h_hbm.at[k], sems.at[3 + k]))
        copies[-1].start()
    odd, even = masks()
    sums = jnp.zeros((1, chans), F32)
    for out, mask in ((hq_out, odd), (he_out, even)):
        part = jnp.zeros((J, chans), F32)
        for r in range(1, rows + 1):
            part = part + out[r].astype(F32)
        sums = sums + jnp.sum(part * mask, axis=0, keepdims=True)
    n = rows * cols * WIDTH
    (total,) = spread_dot(table(chans, chans, WIDTH, WIDTH, 0), sums)
    mean = total / n
    squares = jnp.zeros((1, chans), F32)
    for out, mask in ((hq_out, odd), (he_out, even)):
        part = jnp.zeros((J, chans), F32)
        for r in range(1, rows + 1):
            d = out[r].astype(F32) - mean
            part = part + d * d
        squares = squares + jnp.sum(part * mask, axis=0, keepdims=True)
    (means,) = spread_dot(table(chans, 128, WIDTH, 1, 0), sums)
    (spreads,) = spread_dot(table(chans, 128, WIDTH, 1, -32), squares)
    stat = means / n + spreads
    stat_out[...] = jnp.broadcast_to(stat[None], stat_out.shape)
    for copy in copies:
        copy.wait()


def merged_sums(rec, out):
    out[...] = jnp.broadcast_to(jnp.sum(rec[...], axis=0)[None], out.shape)


def back_kernel(flags, cot, west, east, near, far, dw, c_hbm, aq_out, ae_out, f32s, edge, c_out, sems):
    half, pairs, chans = cot.shape
    rows = 2 * half
    cols = 2 * pairs
    f32s[:, 16 + pairs :] = jnp.zeros((half + 2, 16, chans), F32)
    for k, side in enumerate((west, east)):
        edge[k] = side[...].astype(F32)
    every = slice(None)
    for k, side in enumerate(sides(flags, near, far)):
        row = k * (half + 1)
        f32s[row, 16 : 16 + pairs] = side(2 * cols, 2 * cols + pairs, every)
        edge[2 + k, 0:16] = side(2 * cols + pairs, 2 * cols + pairs + 16, every)
        f32s[row, 15:16] = edge[2 + k, 8:9]
        f32s[row, 16 + pairs : 17 + pairs] = edge[2 + k, 9:10]
    f32s[1 : half + 1, 16 : 16 + pairs] = cot[...].astype(F32)
    for i in range(half):
        f32s[1 + i, 15:16] = edge[0, 2 * rows + i : 2 * rows + i + 1]
        f32s[1 + i, 16 + pairs : 17 + pairs] = edge[1, 2 * rows + i : 2 * rows + i + 1]
    for s in range(half + 2):
        c_out[s, :, 0:chans] = f32s[s, 15 : 15 + J].astype(BF)
        c_out[s, :, chans : 2 * chans] = f32s[s, 16 : 16 + J].astype(BF)
    keep = pltpu.make_async_copy(c_out, c_hbm, sems.at[0])
    keep.start()
    n = half + 1
    lo_l = c_out[0:n, :, 0:chans].reshape(n * J, chans)
    lo_r = c_out[0:n, :, chans:].reshape(n * J, chans)
    hi_l = c_out[1 : n + 1, :, 0:chans].reshape(n * J, chans)
    hi_r = c_out[1 : n + 1, :, chans:].reshape(n * J, chans)

    def put(out, k, value):
        value = value.astype(BF).reshape(n, J, chans)
        for i in range(n):
            out[2 * i + k] = value[i]

    put(ae_out, 1, dot_t(hi_r, dw[1, 1]))
    put(aq_out, 1, dot_t(hi_r, dw[1, 0]) + dot_t(hi_l, dw[1, 2]))
    put(ae_out, 0, dot_t(hi_r, dw[0, 1]) + dot_t(lo_r, dw[2, 1]))
    put(
        aq_out,
        0,
        dot_t(hi_r, dw[0, 0]) + dot_t(hi_l, dw[0, 2]) + dot_t(lo_r, dw[2, 0]) + dot_t(lo_l, dw[2, 2]),
    )
    keep.wait()


def act_kernel(cells, flags, stats, hq, he, aq, ae, gain, bias, t_hbm, p_hbm, coef_out, sum_out, f32s, t_out, p_out, sems):
    devices = stats.shape[0]
    rows = hq.shape[0] - 2
    chans = hq.shape[2]
    count = float(cells * WIDTH)
    local_n = count / devices
    rec = stats[...]
    total = jnp.sum(rec, axis=0)
    centre = total / devices
    dev = rec - centre[None]
    between = jnp.sum(dev * dev, axis=0)
    mean, gaps = spread_dot(table(128, chans, 1, WIDTH, 0), centre, between)
    (within,) = spread_dot(table(128, chans, 1, WIDTH, 32), total)
    var = (within + local_n * gaps) / count
    inverse = lax.rsqrt(var + EPS)
    coef_out[0:1] = mean
    coef_out[1:2] = inverse
    g = gain[...]
    b = bias[...]
    odd, even = masks()
    top = jnp.where(flags[0] == 1, 0.0, 1.0)
    bias_sum = jnp.zeros((1, chans), F32)
    gain_sum = jnp.zeros((1, chans), F32)
    copies = []
    for k, (h, a, mask) in enumerate(((hq, aq, odd), (he, ae, even))):
        is_q = k == 0
        acc_b = jnp.zeros((J, chans), F32)
        acc_g = jnp.zeros((J, chans), F32)
        for r in range(rows + 2):
            normed = (h[r].astype(F32) - mean) * inverse
            shifted = g * normed + b
            sigma = 0.5 + 0.5 * jnp.tanh(0.5 * shifted)
            pre = a[r].astype(F32) * sigma * (1.0 + shifted * (1.0 - sigma))
            p_out[k, r] = pre
            copies.append(pltpu.make_async_copy(p_out.at[k, r], p_hbm.at[k, r], sems.at[len(copies)]))
            copies[-1].start()
            if 1 <= r <= rows:
                acc_b = acc_b + pre
                acc_g = acc_g + pre * normed
            if r <= rows:
                active = shifted * sigma
                if r == 0:
                    active = active * top
                if is_q:
                    f32s[...] = active.astype(BF).astype(F32)
                    t_out[r, :, 0:chans] = active[0:64].astype(BF)
                    t_out[r, :, 2 * chans :] = f32s[1:65].astype(BF)
                else:
                    t_out[r, :, chans : 2 * chans] = active[0:64].astype(BF)
                    copies.append(pltpu.make_async_copy(t_out.at[r], t_hbm.at[r], sems.at[len(copies)]))
                    copies[-1].start()
        bias_sum = bias_sum + jnp.sum(acc_b * mask, axis=0, keepdims=True)
        gain_sum = gain_sum + jnp.sum(acc_g * mask, axis=0, keepdims=True)
    payload = jnp.concatenate(
        [bias_sum[:, 0:128], bias_sum[:, 128:256], gain_sum[:, 0:128], gain_sum[:, 128:256]], axis=0
    )
    sum_out[...] = jnp.broadcast_to(payload[None], sum_out.shape)
    for copy in copies:
        copy.wait()


def halves(flags, full, keep, send):
    n = keep.shape[0]
    core = flags[2]
    keep[...] = full[pl.ds(pl.multiple_of(core * n, n), n)]
    send[...] = full[pl.ds(pl.multiple_of((1 - core) * n, n), n)].astype(BF)


def down_kernel(flags, t_hbm, c_hbm, dw, out, keep, send, t, c, grad, sems):
    half = out.shape[0]
    pairs, chans = out.shape[1:]
    loads = [pltpu.make_async_copy(t_hbm, t, sems.at[0]), pltpu.make_async_copy(c_hbm, c, sems.at[1])]
    for load in loads:
        load.start()
    for load in loads:
        load.wait()
    cot = c[1 : half + 1, 0:pairs, chans:].reshape(half * pairs, chans)
    acc = None
    for a in range(3):
        lhs = jnp.concatenate([t[2 * i + a] for i in range(half)], axis=0)
        term = dot(lhs, dw[a])
        acc = term if acc is None else acc + term
        grad[a * 3 * chans : (a + 1) * 3 * chans] = t_dot(lhs, cot)
    out[...] = acc.astype(BF).reshape(out.shape)
    halves(flags, grad, keep, send)


def grad_kernel(
    cells, flags, sums, coef, gain, h_hbm, p_hbm, x_hbm, rim_hbm, h4_hbm, keep, send, vec_out, f32s, conv_out, h_in, p_in, x, h4_out, sems
):
    rows = p_in.shape[1] - 2
    chans = p_in.shape[3]
    loads = []
    for k in range(2):
        loads.append(pltpu.make_async_copy(h_hbm.at[k], h_in.at[k], sems.at[len(loads)]))
        loads[-1].start()
        for r in range(rows + 2):
            loads.append(pltpu.make_async_copy(p_hbm.at[k, r], p_in.at[k, r], sems.at[len(loads)]))
            loads[-1].start()
    load_x = []
    for src, dst in ((x_hbm, x.at[1 : rows + 1]), (rim_hbm.at[0], x.at[0]), (rim_hbm.at[1], x.at[rows + 1])):
        load_x.append(pltpu.make_async_copy(src, dst, sems.at[len(loads) + len(load_x)]))
        load_x[-1].start()
    first_out = len(loads) + len(load_x)
    copies = []
    count = float(cells * WIDTH)
    total = jnp.sum(sums[...], axis=0)
    bias_sum = jnp.concatenate([total[0:1], total[1:2]], axis=1)
    gain_sum = jnp.concatenate([total[2:3], total[3:4]], axis=1)
    factor = 1.0 / math.sqrt(cells)
    vec_out[0:1] = gain_sum * factor
    vec_out[1:2] = bias_sum * factor
    g = gain[...]
    first, second = spread_dot(table(chans, chans, WIDTH, WIDTH, 0), g * bias_sum, g * gain_sum)
    first = first / count
    second = second / count
    mean = coef[0:1]
    inverse = coef[1:2]
    top = jnp.where(flags[0] == 1, 0.0, 1.0)
    bottom = jnp.where(flags[1] == 1, 0.0, 1.0)
    for k in range(2):
        is_q = k == 0
        loads[k * (rows + 3)].wait()
        for r in range(rows + 2):
            loads[k * (rows + 3) + 1 + r].wait()
            normed = (h_in[k, r].astype(F32) - mean) * inverse
            value = inverse * (g * p_in[k, r] - first - normed * second)
            if r == 0:
                value = value * top
            if r == rows + 1:
                value = value * bottom
            rounded = value.astype(BF)
            f32s[...] = rounded.astype(F32)
            moved = f32s[1:65].astype(BF)
            lo = 3 if is_q else 2
            h4_out[r, :, lo * chans : (lo + 1) * chans] = rounded[0:64]
            lo = 1 if is_q else 0
            h4_out[r, :, lo * chans : (lo + 1) * chans] = moved
            if not is_q:
                copies.append(pltpu.make_async_copy(h4_out.at[r], h4_hbm.at[r], sems.at[first_out + r]))
                copies[-1].start()
    for load in load_x:
        load.wait()
    pairs = h4_out.shape[1]
    cells_here = rows * pairs
    odd = h4_out[1 : rows + 1, :, chans : 2 * chans].reshape(cells_here, chans)
    even = h4_out[1 : rows + 1, :, 2 * chans : 3 * chans].reshape(cells_here, chans)
    for a in range(3):
        lhs = x[a : a + rows].reshape(cells_here, 4 * chans)
        part = t_dot(lhs[:, 0 : 3 * chans], even) + t_dot(lhs[:, chans : 4 * chans], odd)
        conv_out[a * 3 * chans : (a + 1) * 3 * chans] = part
    halves(flags, conv_out, keep, send)
    for copy in copies:
        copy.wait()


def input_kernel(h4, w, out, f32s):
    rows, cols, chans = out.shape
    for k, lo in ((0, 1), (1, 0)):
        acc = None
        for a in range(3):
            for b in range(3):
                lane = (lo + b) * chans
                lhs = h4[2 - a : 2 - a + rows, :, lane : lane + chans].reshape(rows * (cols // 2), chans)
                term = dot_t(lhs, w[a, b])
                acc = term if acc is None else acc + term
        acc = acc.reshape(rows, cols // 2, chans)
        for r in range(rows):
            for v in range(2):
                f32s[r, v, pl.ds(k, cols // 2, stride=2), :] = acc[r, :, v * 128 : v * 128 + 128]
    for v in range(2):
        out[:, :, v * 128 : v * 128 + 128] = f32s[:, v, 0:cols].astype(BF)


def passed(value, axes, step, wrap):
    n = lax.axis_size(axes)
    pairs = [(i, (i + step) % n) for i in range(n) if wrap or 0 <= i + step < n]
    return lax.ppermute(value, axes, pairs)


def join_kernel(conv_keep, conv_other, down_keep, down_other, out, both, sems):
    n = conv_keep.shape[0]
    step = n // 2
    copies = []
    for k, (keep, other) in enumerate(((down_keep, down_other), (conv_keep, conv_other))):
        for q in range(2):
            part = slice(q * step, (q + 1) * step)
            o = (1 - k) * n + q * step
            both[o : o + step] = (keep[part] + other[part].astype(F32)).astype(BF)
            copies.append(pltpu.make_async_copy(both.at[o : o + step], out.at[o : o + step], sems.at[2 * k + q]))
            copies[-1].start()
    for copy in copies:
        copy.wait()


def unpack_rows(core, rows, conv, down, f32s, sems):
    n = rows.shape[0] // 2
    step = n // 2
    base = pl.multiple_of(core * n, n)
    copies = []
    for k, dst in enumerate((conv, down)):
        for q in range(2):
            o = k * n + q * step
            f32s[o : o + step] = rows[o : o + step].astype(F32)
            part = dst.at[pl.ds(base + q * step, step)]
            copies.append(pltpu.make_async_copy(f32s.at[o : o + step], part, sems.at[k * 2 + q]))
            copies[-1].start()
    for copy in copies:
        copy.wait()


def unpack_own(flags, rows, conv, down, f32s, sems):
    unpack_rows(flags[2], rows, conv, down, f32s, sems)


def unpack_other(flags, rows, conv_in, down_in, conv, down, f32s, sems):
    unpack_rows(1 - flags[2], rows, conv, down, f32s, sems)


def core_swap(value):
    return lax.ppermute(value, "core", [(0, 1), (1, 0)])


def local(features, conv_weight, down_weight, norm_gain, norm_bias, cotangent):
    rows, cols, chans = features.shape
    half, pairs, _ = cotangent.shape
    devices = lax.axis_size(ALL)
    lats = lax.axis_size(LAT)
    cells = rows * cols * devices
    factor = 1.0 / math.sqrt(cells)
    lat = lax.axis_index(LAT)
    flags = jnp.stack([lat == 0, lat == lats - 1, lax.axis_index("core") == 1]).astype(jnp.int32)
    gain = norm_gain.reshape(1, chans)
    bias = norm_bias.reshape(1, chans)
    w3 = conv_weight.reshape(3, 3 * chans, chans)
    dw3 = down_weight.reshape(3, 3 * chans, chans)
    all_rows = 9 * chans
    few = lax.axis_size(FEW)
    rest = lax.axis_size(REST)

    with jax.named_scope("halo"):
        slab = (2 * rows + 16, chans)
        to_east, to_west = call(
            pack_lon,
            [(slab, BF)] * 2,
            [((2, rows, 16, chans), BF), ((2, half, 16, chans), BF), (slab, F32)],
            n_in=2,
            hbm=(0, 1),
            sems=4,
        )(pinned(features), pinned(cotangent))
        west = passed(to_east, LON, 1, True)
        east = passed(to_west, LON, -1, True)
        strip = (2 * cols + pairs + 16, chans)
        to_near, to_far = call(
            pack_lat,
            [(strip, BF)] * 2,
            [(slab, F32), (slab, F32), ((2, 16, chans), F32)],
            n_in=5,
            smem=(0,),
            hbm=(1, 2),
            sems=6,
        )(flags, pinned(features), pinned(cotangent), west, east)
        near = lax.ppermute(to_near, LAT, [(i, i ^ 1) for i in range(lats)])
        gaps = range(1, lats - 1, 2)
        far = lax.ppermute(to_far, LAT, [(i, i + 1) for i in gaps] + [(i + 1, i) for i in gaps])

    plane = (rows + 2, J, chans)
    x_shape = (rows, pairs, 4 * chans)
    rim_shape = (2, pairs, 4 * chans)
    inner_plane = (rows - 2, J, chans)
    with jax.named_scope("conv"):
        x, rim, hq_in, he_in = call(
            inner_kernel,
            [(x_shape, BF, True), ((4, J, 4 * chans), BF), (inner_plane, BF), (inner_plane, BF)],
            [
                ((rows, 2, cols + 56, 128), F32),
                ((2, 2, slab[0], 128), F32),
                ((rows, J, 5 * chans), BF),
                ((rows, cols, chans), BF),
                (w3.shape, BF),
            ],
            flops=2 * 960 * 2304 * 256,
            n_in=4,
            hbm=(0, 3),
            sems=3,
        )(pinned(features), west, east, pinned(w3))
        x_rim, h, hq, he, stat = call(
            functools.partial(outer_kernel, cols),
            [(rim_shape, BF, True), ((2,) + plane, BF, True), (plane, BF), (plane, BF), ((devices, 1, 128), F32)],
            [
                ((4, 2, cols + 56, 128), F32),
                ((2, 2, 16, 128), F32),
                ((4, J, 5 * chans), BF),
                (w3.shape, BF),
            ],
            flops=2 * 640 * 2304 * 256,
            n_in=7,
            smem=(0,),
            hbm=(6,),
            sems=5,
        )(flags, near, far, rim, hq_in, he_in, pinned(w3))
        stats = lax.all_to_all(stat, ALL, 0, 0, tiled=True)
    c_shape = (half + 2, J, 2 * chans)
    with jax.named_scope("back"):
        c2, aq, ae = call(
            back_kernel,
            [(c_shape, BF, True), (plane, BF), (plane, BF)],
            [((half + 2, pairs + 32, chans), F32), ((4,) + slab, F32), (c_shape, BF)],
            flops=2 * 400 * 2304 * 256,
            n_in=7,
            smem=(0,),
            sems=1,
        )(flags, cotangent, west, east, near, far, down_weight)
    t_shape = (rows + 1, pairs, 3 * chans)
    with jax.named_scope("act"):
        t, p, coef, sums = call(
            functools.partial(act_kernel, cells),
            [(t_shape, BF, True), ((2,) + plane, F32, True), ((2, chans), F32), ((few, 4, 128), F32)],
            [((J, chans), F32), (t_shape, BF), ((2,) + plane, F32)],
            flops=1600 * 256 * 20,
            smem=(0,),
            n_in=8,
            sems=3 * rows + 5,
        )(flags, stats, hq, he, aq, ae, gain, bias)
        sums = lax.all_to_all(sums, FEW, 0, 0, tiled=True)
        (sums,) = call(merged_sums, [((rest, 4, 128), F32)], n_in=1)(sums)
        sums, c2 = lax.optimization_barrier((sums, c2))
        sums = lax.all_to_all(sums, REST, 0, 0, tiled=True)
    half_rows = (all_rows // 2, chans)
    with jax.named_scope("down"):
        output, down_keep, down_send = call(
            down_kernel,
            [((half, pairs, chans), BF), (half_rows, F32), (half_rows, BF)],
            [(t_shape, BF), (c_shape, BF), ((all_rows, chans), F32)],
            flops=4 * 256 * 2304 * 256,
            smem=(0,),
            hbm=(1, 2),
            n_in=4,
            sems=2,
        )(flags, pinned(t), pinned(c2), dw3)
        down_other = core_swap(down_send)
    h4_shape = (rows + 2, pairs, 4 * chans)
    with jax.named_scope("grad"):
        h4, conv_keep, conv_send, vec = call(
            functools.partial(grad_kernel, cells),
            [(h4_shape, BF, True), (half_rows, F32), (half_rows, BF), ((2, chans), F32)],
            [
                ((J, chans), F32),
                ((all_rows, chans), F32),
                ((2,) + plane, BF),
                ((2,) + plane, F32),
                ((rows + 2, pairs, 4 * chans), BF),
                (h4_shape, BF),
            ],
            flops=2 * 1600 * 2304 * 256,
            smem=(0,),
            hbm=(4, 5, 6, 7),
            n_in=8,
            sems=3 * (rows + 2) + 5,
        )(flags, sums, coef, gain, pinned(h), pinned(p), pinned(x), pinned(x_rim))
    with jax.named_scope("input"):
        (input_grad,) = call(
            input_kernel,
            [((rows, cols, chans), BF)],
            [((rows, 2, cols + 8, 128), F32)],
            flops=2 * 1024 * 2304 * 256,
            n_in=2,
        )(h4, conv_weight)
    with jax.named_scope("total"):
        whole_rows = (all_rows, chans)
        (mine,) = call(
            join_kernel, [(whole_rows, BF, True)], [(whole_rows, BF)], n_in=4, sems=4
        )(conv_keep, core_swap(conv_send), down_keep, down_other)
        chips = lax.axis_size(NEAR)
        depth = lax.axis_size("z_hi")
        share = all_rows // chips
        got = lax.all_to_all(mine.reshape(chips, share, chans), NEAR, 0, 0, tiled=True)
        got, input_grad = lax.optimization_barrier((got, input_grad))
        piece = jnp.sum(got.astype(F32), axis=0).astype(BF)
        got = lax.all_to_all(jnp.broadcast_to(piece[None], (depth, share, chans)), "z_hi", 0, 0, tiled=True)
        piece = (jnp.sum(got.astype(F32), axis=0) * factor).astype(BF)
        whole = lax.all_to_all(jnp.broadcast_to(piece[None], (chips, share, chans)), NEAR, 0, 0, tiled=True)
        whole = whole.reshape(all_rows, chans)
        other = core_swap(whole)
        flat = (whole_rows, F32, True)
        room = [(whole_rows, F32)]
        conv_grad, down_grad = call(unpack_own, [flat, flat], room, smem=(0,), n_in=2, sems=4)(flags, whole)
        conv_grad, down_grad = call(
            unpack_other, [flat, flat], room, smem=(0,), hbm=(2, 3), n_in=4, sems=4, aliases={2: 0, 3: 1}
        )(flags, other, pinned(conv_grad), pinned(down_grad))
    shape = (3, 3, chans, chans)
    return output, input_grad, conv_grad.reshape(shape), down_grad.reshape(shape), vec[0], vec[1]


SIZES = {64: (4, 4, 2, 2), 2: (1, 1, 2, 1), 4: (2, 1, 2, 1), 8: (1, 2, 2, 2)}


def solution(mesh):
    lon, lat = mesh.devices.shape
    fine = Mesh(mesh.devices.reshape(SIZES[lon] + (lat // 2, 2)), ALL)
    band = P(LAT, LON, None)
    return jax.shard_map(
        local,
        mesh=fine,
        in_specs=(band, P(), P(), P(), P(), band),
        out_specs=(band, band, P(), P(), P(), P()),
        check_vma=False,
    )
```

```python
import functools
import math

import jax
import jax.numpy as jnp
from jax import lax
from jax.experimental import pallas as pl
from jax.experimental.pallas import tpu as pltpu
from jax.sharding import Mesh
from jax.sharding import PartitionSpec as P

EPS = 1e-05
WIDTH = 8
J = 80
LON = ("x", "z_hi", "z_lo", "y_hi")
LAT = ("y_lo", "core")
NEAR = ("x", "z_lo", "y_hi", "y_lo")
FEW = ("x", "core")
REST = ("z_hi", "z_lo", "y_hi", "y_lo")
ALL = LON + LAT
BF = jnp.bfloat16
F32 = jnp.float32


def call(body, outs, scratch=(), flops=0, smem=(), hbm=(), n_in=0, sems=0, aliases=None):
    spaces = [pltpu.SMEM if i in smem else pltpu.HBM if i in hbm else pltpu.VMEM for i in range(n_in)]
    out_spaces = [pltpu.HBM if len(o) > 2 else pltpu.VMEM for o in outs]
    return pl.pallas_call(
        body,
        out_shape=[pltpu.HBM(o[0], o[1]) if len(o) > 2 else jax.ShapeDtypeStruct(o[0], o[1]) for o in outs],
        in_specs=[pl.BlockSpec(memory_space=m) for m in spaces],
        out_specs=[pl.BlockSpec(memory_space=m) for m in out_spaces],
        scratch_shapes=[pltpu.VMEM(s, d) for s, d in scratch]
        + ([pltpu.SemaphoreType.DMA((sems,))] if sems else []),
        input_output_aliases=aliases or {},
        compiler_params=pltpu.CompilerParams(vmem_limit_bytes=24 * 1024 * 1024),
        cost_estimate=pl.CostEstimate(flops=flops, bytes_accessed=1 << 20, transcendentals=0),
    )


def pinned(value):
    return pltpu.with_memory_space_constraint(value, pltpu.HBM)


def dot(a, b):
    return jnp.dot(a, b, preferred_element_type=F32)


def dot_t(a, b):
    return lax.dot_general(a, b, (((1,), (1,)), ((), ())), preferred_element_type=F32)


def t_dot(a, b):
    return lax.dot_general(a, b, (((0,), (0,)), ((), ())), preferred_element_type=F32)


def spread_dot(table, *vectors):
    parts = []
    for v in vectors:
        high = v.astype(BF).astype(F32)
        mid = (v - high).astype(BF).astype(F32)
        parts += [high, mid, v - high - mid]
    parts.append(jnp.zeros((8 - len(parts), vectors[0].shape[1]), F32))
    out = dot(jnp.concatenate(parts, axis=0).astype(BF), table)
    return [out[3 * i : 3 * i + 1] + out[3 * i + 1 : 3 * i + 2] + out[3 * i + 2 : 3 * i + 3] for i in range(len(vectors))]


def table(n, m, row_width, col_width, shift):
    r = lax.broadcasted_iota(jnp.int32, (n, m), 0) // row_width
    c = lax.broadcasted_iota(jnp.int32, (n, m), 1) // col_width
    return jnp.where(r == c + shift, 1.0, 0.0).astype(BF)


def masks():
    j = lax.broadcasted_iota(jnp.int32, (J, 1), 0)
    odd = jnp.where((j >= 1) & (j <= 64), 1.0, 0.0)
    even = jnp.where(j <= 63, 1.0, 0.0)
    return odd, even


def pack_lon(feat_hbm, cot_hbm, out, feat, cot, f32s, sems):
    rows, cols, chans = feat_hbm.shape
    half, pairs, _ = cot_hbm.shape
    copies = []
    for k, (lo_f, lo_c) in enumerate(((cols - 16, pairs - 16), (0, 0))):
        copies.append(pltpu.make_async_copy(feat_hbm.at[:, lo_f : lo_f + 16], feat.at[k], sems.at[2 * k]))
        copies.append(pltpu.make_async_copy(cot_hbm.at[:, lo_c : lo_c + 16], cot.at[k], sems.at[2 * k + 1]))
    for copy in copies:
        copy.start()
    f32s[...] = jnp.zeros(f32s.shape, F32)
    for copy in copies:
        copy.wait()
    for k, (at_f, at_c) in enumerate(((14, 15), (0, 0))):
        for r in range(rows):
            f32s[2 * r : 2 * r + 2] = feat[k, r].astype(F32)[at_f : at_f + 2]
        for i in range(half):
            f32s[2 * rows + i : 2 * rows + i + 1] = cot[k, i].astype(F32)[at_c : at_c + 1]
        out[k] = f32s[...].astype(BF)


def columns(flags, pair, next_pair, part=slice(None)):
    low = flags[3] == 0
    west = jnp.where(low, next_pair[0, :, part].astype(F32), pair[0, :, part].astype(F32))
    east = jnp.where(low, pair[1, :, part].astype(F32), next_pair[1, :, part].astype(F32))
    return west, east


def pack_lat(flags, feat, cot, pair, next_pair, near, far, w32, e32, corner, sems):
    rows, cols, _ = feat.shape
    half, pairs, _ = cot.shape
    core = flags[2]
    copies = []
    for dest, last in ((near, 1 - core), (far, core)):
        top, mid = last * (rows - 2), last * (half - 1)
        parts = [(feat.at[top + k], k * cols, cols) for k in range(2)]
        parts.append((cot.at[mid], 2 * cols, pairs))
        for src, o, n in parts:
            copies.append(pltpu.make_async_copy(src, dest.at[o : o + n], sems.at[len(copies)]))
            copies[-1].start()
    w32[...], e32[...] = columns(flags, pair, next_pair)
    corner[...] = jnp.zeros(corner.shape, F32)
    for k, (top, mid) in enumerate(((rows - 2, half - 1), (0, 0))):
        corner[k, 0:4] = w32[2 * top : 2 * top + 4]
        corner[k, 4:8] = e32[2 * top : 2 * top + 4]
        corner[k, 8:9] = w32[2 * rows + mid : 2 * rows + mid + 1]
        corner[k, 9:10] = e32[2 * rows + mid : 2 * rows + mid + 1]
    o = 2 * cols + pairs
    near[o : o + 16] = corner[core].astype(BF)
    far[o : o + 16] = corner[1 - core].astype(BF)
    for copy in copies:
        copy.wait()


def sides(flags, near, far):
    low = flags[2] == 0

    def north(lo, hi, part):
        return jnp.where(low, far[lo:hi, part].astype(F32), near[lo:hi, part].astype(F32))

    def south(lo, hi, part):
        return jnp.where(low, near[lo:hi, part].astype(F32), far[lo:hi, part].astype(F32))

    return north, south


def taps(f32s, x_out, rows, lanes):
    for r in range(rows):
        for v in range(2):
            for k in range(lanes):
                lane = k * 256 + v * 128
                x_out[r, :, lane : lane + 128] = f32s[r, v, pl.ds(14 + k, J, stride=2), :].astype(BF)


def moments(planes, cols):
    chans = planes[0][0].shape[2]
    sums = jnp.zeros((1, chans), F32)
    for (ref, rows), mask in zip(planes, masks()):
        part = jnp.zeros((J, chans), F32)
        for r in rows:
            part = part + ref[r].astype(F32)
        sums = sums + jnp.sum(part * mask, axis=0, keepdims=True)
    (total,) = spread_dot(table(chans, chans, WIDTH, WIDTH, 0), sums)
    mean = total / (len(planes[0][1]) * cols * WIDTH)
    squares = jnp.zeros((1, chans), F32)
    for (ref, rows), mask in zip(planes, masks()):
        part = jnp.zeros((J, chans), F32)
        for r in rows:
            d = ref[r].astype(F32) - mean
            part = part + d * d
        squares = squares + jnp.sum(part * mask, axis=0, keepdims=True)
    return sums, squares


def inner_kernel(
    flags, feat_hbm, pair, next_pair, w_hbm, x_hbm, rim, hq_out, he_out, vec_out, f32s, edge, x_out, feat, w, sems
):
    rows, cols, chans = feat.shape
    pairs = cols // 2
    load_f = pltpu.make_async_copy(feat_hbm, feat, sems.at[1])
    load_f.start()
    load_w = pltpu.make_async_copy(w_hbm, w, sems.at[2])
    load_w.start()
    f32s[:, :, 16 + cols : 56 + cols] = jnp.zeros((rows, 2, 40, 128), F32)
    for v in range(2):
        part = slice(v * 128, v * 128 + 128)
        edge[0, v], edge[1, v] = columns(flags, pair, next_pair, part)
        for r in range(rows):
            f32s[r, v, 14:16] = edge[0, v, 2 * r : 2 * r + 2]
            f32s[r, v, 16 + cols : 18 + cols] = edge[1, v, 2 * r : 2 * r + 2]
    load_f.wait()
    for v in range(2):
        f32s[:, v, 16 : 16 + cols] = feat[:, :, v * 128 : v * 128 + 128].astype(F32)
    taps(f32s, x_out, rows, 5)
    keep = pltpu.make_async_copy(x_out.at[:, 0:pairs, chans : 5 * chans], x_hbm, sems.at[0])
    keep.start()
    for i, r in enumerate((0, 1, rows - 2, rows - 1)):
        rim[i] = x_out[r, :, 0 : 4 * chans]
    load_w.wait()
    n = rows - 2
    for out, lo in ((hq_out, 0), (he_out, chans)):
        acc = None
        for a in range(3):
            lhs = x_out[a : a + n, :, lo : lo + 3 * chans].reshape(n * J, 3 * chans)
            term = dot(lhs, w[a])
            acc = term if acc is None else acc + term
        out[...] = acc.astype(BF).reshape(n, J, chans)
    sums, squares = moments(((hq_out, range(n)), (he_out, range(n))), cols)
    vec_out[0:1] = sums
    vec_out[1:2] = squares
    keep.wait()


def outer_kernel(
    cols, flags, near, far, rim, hq_in, he_in, vec, w_hbm, x_hbm, h_hbm, hq_out, he_out, stat_out, f32s, edge, x_out, w, sems
):
    rows = hq_in.shape[0] + 2
    chans = hq_in.shape[2]
    pairs = cols // 2
    load_w = pltpu.make_async_copy(w_hbm, w, sems.at[0])
    load_w.start()
    f32s[:, :, 16 + cols : 56 + cols] = jnp.zeros((4, 2, 40, 128), F32)
    for v in range(2):
        part = slice(v * 128, v * 128 + 128)
        for k, side in enumerate(sides(flags, near, far)):
            edge[k, v] = side(2 * cols + pairs, 2 * cols + pairs + 16, part)
            for q in range(2):
                row = q + 2 * k
                f32s[row, v, 16 : 16 + cols] = side(q * cols, (q + 1) * cols, part)
                f32s[row, v, 14:16] = edge[k, v, 2 * q : 2 * q + 2]
                f32s[row, v, 16 + cols : 18 + cols] = edge[k, v, 4 + 2 * q : 6 + 2 * q]
    taps(f32s, x_out, 4, 5)
    copies = []
    for i, r in enumerate((1, 2)):
        copies.append(pltpu.make_async_copy(x_out.at[r, 0:pairs, chans : 5 * chans], x_hbm.at[i], sems.at[1 + i]))
        copies[-1].start()
    hq_out[2:rows] = hq_in[...]
    he_out[2:rows] = he_in[...]
    load_w.wait()
    wanted = (
        ((x_out, 0), (x_out, 1), (rim, 2), (rim, 3)),
        ((x_out, 1), (rim, 0), (rim, 3), (x_out, 2)),
        ((rim, 0), (rim, 1), (x_out, 2), (x_out, 3)),
    )
    for k, out in enumerate((hq_out, he_out)):
        lo = k * chans
        acc = None
        for a in range(3):
            lhs = jnp.concatenate([ref[r, :, lo : lo + 3 * chans] for ref, r in wanted[a]], axis=0)
            term = dot(lhs, w[a])
            acc = term if acc is None else acc + term
        value = acc.astype(BF).reshape(4, J, chans)
        out[0:2] = value[0:2]
        out[rows : rows + 2] = value[2:4]
        copies.append(pltpu.make_async_copy(out, h_hbm.at[k], sems.at[3 + k]))
        copies[-1].start()
    edges = (1, rows)
    sums, squares = moments(((hq_out, edges), (he_out, edges)), cols)
    n_in = (rows - 2) * cols * WIDTH
    n_out = 2 * cols * WIDTH
    n = n_in + n_out
    gap = vec[0:1] / n_in - sums / n_out
    (means,) = spread_dot(table(chans, 128, WIDTH, 1, 0), vec[0:1] + sums)
    within, gaps = spread_dot(table(chans, 128, WIDTH, 1, -32), vec[1:2] + squares, gap)
    stat = means / n + within + (n_in * n_out / n) * gaps * gaps
    stat_out[...] = jnp.broadcast_to(stat[None], stat_out.shape)
    for copy in copies:
        copy.wait()


def merged_sums(rec, out):
    out[...] = jnp.broadcast_to(jnp.sum(rec[...], axis=0)[None], out.shape)


def back_kernel(flags, cot, pair, next_pair, near, far, dw, c_hbm, aq_out, ae_out, f32s, edge, c_out, sems):
    half, pairs, chans = cot.shape
    rows = 2 * half
    cols = 2 * pairs
    f32s[:, 16 + pairs :] = jnp.zeros((half + 2, 16, chans), F32)
    edge[0], edge[1] = columns(flags, pair, next_pair)
    every = slice(None)
    for k, side in enumerate(sides(flags, near, far)):
        row = k * (half + 1)
        f32s[row, 16 : 16 + pairs] = side(2 * cols, 2 * cols + pairs, every)
        edge[2 + k, 0:16] = side(2 * cols + pairs, 2 * cols + pairs + 16, every)
        f32s[row, 15:16] = edge[2 + k, 8:9]
        f32s[row, 16 + pairs : 17 + pairs] = edge[2 + k, 9:10]
    f32s[1 : half + 1, 16 : 16 + pairs] = cot[...].astype(F32)
    for i in range(half):
        f32s[1 + i, 15:16] = edge[0, 2 * rows + i : 2 * rows + i + 1]
        f32s[1 + i, 16 + pairs : 17 + pairs] = edge[1, 2 * rows + i : 2 * rows + i + 1]
    for s in range(half + 2):
        c_out[s, :, 0:chans] = f32s[s, 15 : 15 + J].astype(BF)
        c_out[s, :, chans : 2 * chans] = f32s[s, 16 : 16 + J].astype(BF)
    keep = pltpu.make_async_copy(c_out, c_hbm, sems.at[0])
    keep.start()
    n = half + 1
    lo_l = c_out[0:n, :, 0:chans].reshape(n * J, chans)
    lo_r = c_out[0:n, :, chans:].reshape(n * J, chans)
    hi_l = c_out[1 : n + 1, :, 0:chans].reshape(n * J, chans)
    hi_r = c_out[1 : n + 1, :, chans:].reshape(n * J, chans)

    def put(out, k, value):
        value = value.astype(BF).reshape(n, J, chans)
        for i in range(n):
            out[2 * i + k] = value[i]

    put(ae_out, 1, dot_t(hi_r, dw[1, 1]))
    put(aq_out, 1, dot_t(hi_r, dw[1, 0]) + dot_t(hi_l, dw[1, 2]))
    put(ae_out, 0, dot_t(hi_r, dw[0, 1]) + dot_t(lo_r, dw[2, 1]))
    put(
        aq_out,
        0,
        dot_t(hi_r, dw[0, 0]) + dot_t(hi_l, dw[0, 2]) + dot_t(lo_r, dw[2, 0]) + dot_t(lo_l, dw[2, 2]),
    )
    keep.wait()


def act_kernel(cells, flags, stats, hq, he, aq, ae, gain, bias, t_hbm, p_hbm, coef_out, sum_out, f32s, t_out, p_out, sems):
    devices = stats.shape[0]
    rows = hq.shape[0] - 2
    chans = hq.shape[2]
    count = float(cells * WIDTH)
    local_n = count / devices
    rec = stats[...]
    total = jnp.sum(rec, axis=0)
    centre = total / devices
    dev = rec - centre[None]
    between = jnp.sum(dev * dev, axis=0)
    mean, gaps = spread_dot(table(128, chans, 1, WIDTH, 0), centre, between)
    (within,) = spread_dot(table(128, chans, 1, WIDTH, 32), total)
    var = (within + local_n * gaps) / count
    inverse = lax.rsqrt(var + EPS)
    coef_out[0:1] = mean
    coef_out[1:2] = inverse
    g = gain[...]
    b = bias[...]
    odd, even = masks()
    top = jnp.where(flags[0] == 1, 0.0, 1.0)
    bias_sum = jnp.zeros((1, chans), F32)
    gain_sum = jnp.zeros((1, chans), F32)
    copies = []
    for k, (h, a, mask) in enumerate(((hq, aq, odd), (he, ae, even))):
        is_q = k == 0
        acc_b = jnp.zeros((J, chans), F32)
        acc_g = jnp.zeros((J, chans), F32)
        for r in range(rows + 2):
            normed = (h[r].astype(F32) - mean) * inverse
            shifted = g * normed + b
            sigma = 0.5 + 0.5 * jnp.tanh(0.5 * shifted)
            pre = a[r].astype(F32) * sigma * (1.0 + shifted * (1.0 - sigma))
            p_out[k, r] = pre
            copies.append(pltpu.make_async_copy(p_out.at[k, r], p_hbm.at[k, r], sems.at[len(copies)]))
            copies[-1].start()
            if 1 <= r <= rows:
                acc_b = acc_b + pre
                acc_g = acc_g + pre * normed
            if r <= rows:
                active = shifted * sigma
                if r == 0:
                    active = active * top
                if is_q:
                    f32s[...] = active.astype(BF).astype(F32)
                    t_out[r, :, 0:chans] = active[0:64].astype(BF)
                    t_out[r, :, 2 * chans :] = f32s[1:65].astype(BF)
                else:
                    t_out[r, :, chans : 2 * chans] = active[0:64].astype(BF)
                    copies.append(pltpu.make_async_copy(t_out.at[r], t_hbm.at[r], sems.at[len(copies)]))
                    copies[-1].start()
        bias_sum = bias_sum + jnp.sum(acc_b * mask, axis=0, keepdims=True)
        gain_sum = gain_sum + jnp.sum(acc_g * mask, axis=0, keepdims=True)
    payload = jnp.concatenate(
        [bias_sum[:, 0:128], bias_sum[:, 128:256], gain_sum[:, 0:128], gain_sum[:, 128:256]], axis=0
    )
    sum_out[...] = jnp.broadcast_to(payload[None], sum_out.shape)
    for copy in copies:
        copy.wait()


def halves(flags, full, keep, send):
    n = keep.shape[0]
    core = flags[2]
    keep[...] = full[pl.ds(pl.multiple_of(core * n, n), n)]
    send[...] = full[pl.ds(pl.multiple_of((1 - core) * n, n), n)].astype(BF)


def down_kernel(flags, t_hbm, c_hbm, dw, out, keep, send, t, c, grad, sems):
    half = out.shape[0]
    pairs, chans = out.shape[1:]
    loads = [pltpu.make_async_copy(t_hbm, t, sems.at[0]), pltpu.make_async_copy(c_hbm, c, sems.at[1])]
    for load in loads:
        load.start()
    for load in loads:
        load.wait()
    cot = c[1 : half + 1, 0:pairs, chans:].reshape(half * pairs, chans)
    acc = None
    for a in range(3):
        lhs = jnp.concatenate([t[2 * i + a] for i in range(half)], axis=0)
        term = dot(lhs, dw[a])
        acc = term if acc is None else acc + term
        grad[a * 3 * chans : (a + 1) * 3 * chans] = t_dot(lhs, cot)
    out[...] = acc.astype(BF).reshape(out.shape)
    halves(flags, grad, keep, send)


def grad_kernel(
    cells, flags, sums, coef, gain, h_hbm, p_hbm, x_hbm, rim_hbm, h4_hbm, keep, send, vec_out, f32s, conv_out, h_in, p_in, x, h4_out, sems
):
    rows = p_in.shape[1] - 2
    chans = p_in.shape[3]
    loads = []
    for k in range(2):
        loads.append(pltpu.make_async_copy(h_hbm.at[k], h_in.at[k], sems.at[len(loads)]))
        loads[-1].start()
        for r in range(rows + 2):
            loads.append(pltpu.make_async_copy(p_hbm.at[k, r], p_in.at[k, r], sems.at[len(loads)]))
            loads[-1].start()
    load_x = []
    for src, dst in ((x_hbm, x.at[1 : rows + 1]), (rim_hbm.at[0], x.at[0]), (rim_hbm.at[1], x.at[rows + 1])):
        load_x.append(pltpu.make_async_copy(src, dst, sems.at[len(loads) + len(load_x)]))
        load_x[-1].start()
    first_out = len(loads) + len(load_x)
    copies = []
    count = float(cells * WIDTH)
    total = jnp.sum(sums[...], axis=0)
    bias_sum = jnp.concatenate([total[0:1], total[1:2]], axis=1)
    gain_sum = jnp.concatenate([total[2:3], total[3:4]], axis=1)
    factor = 1.0 / math.sqrt(cells)
    vec_out[0:1] = gain_sum * factor
    vec_out[1:2] = bias_sum * factor
    g = gain[...]
    first, second = spread_dot(table(chans, chans, WIDTH, WIDTH, 0), g * bias_sum, g * gain_sum)
    first = first / count
    second = second / count
    mean = coef[0:1]
    inverse = coef[1:2]
    top = jnp.where(flags[0] == 1, 0.0, 1.0)
    bottom = jnp.where(flags[1] == 1, 0.0, 1.0)
    for k in range(2):
        is_q = k == 0
        loads[k * (rows + 3)].wait()
        for r in range(rows + 2):
            loads[k * (rows + 3) + 1 + r].wait()
            normed = (h_in[k, r].astype(F32) - mean) * inverse
            value = inverse * (g * p_in[k, r] - first - normed * second)
            if r == 0:
                value = value * top
            if r == rows + 1:
                value = value * bottom
            rounded = value.astype(BF)
            f32s[...] = rounded.astype(F32)
            moved = f32s[1:65].astype(BF)
            lo = 3 if is_q else 2
            h4_out[r, :, lo * chans : (lo + 1) * chans] = rounded[0:64]
            lo = 1 if is_q else 0
            h4_out[r, :, lo * chans : (lo + 1) * chans] = moved
            if not is_q:
                copies.append(pltpu.make_async_copy(h4_out.at[r], h4_hbm.at[r], sems.at[first_out + r]))
                copies[-1].start()
    for load in load_x:
        load.wait()
    pairs = h4_out.shape[1]
    cells_here = rows * pairs
    odd = h4_out[1 : rows + 1, :, chans : 2 * chans].reshape(cells_here, chans)
    even = h4_out[1 : rows + 1, :, 2 * chans : 3 * chans].reshape(cells_here, chans)
    for a in range(3):
        lhs = x[a : a + rows].reshape(cells_here, 4 * chans)
        part = t_dot(lhs[:, 0 : 3 * chans], even) + t_dot(lhs[:, chans : 4 * chans], odd)
        conv_out[a * 3 * chans : (a + 1) * 3 * chans] = part
    halves(flags, conv_out, keep, send)
    for copy in copies:
        copy.wait()


def input_kernel(h4, w, out, f32s):
    rows, cols, chans = out.shape
    for k, lo in ((0, 1), (1, 0)):
        acc = None
        for a in range(3):
            for b in range(3):
                lane = (lo + b) * chans
                lhs = h4[2 - a : 2 - a + rows, :, lane : lane + chans].reshape(rows * (cols // 2), chans)
                term = dot_t(lhs, w[a, b])
                acc = term if acc is None else acc + term
        acc = acc.reshape(rows, cols // 2, chans)
        for r in range(rows):
            for v in range(2):
                f32s[r, v, pl.ds(k, cols // 2, stride=2), :] = acc[r, :, v * 128 : v * 128 + 128]
    for v in range(2):
        out[:, :, v * 128 : v * 128 + 128] = f32s[:, v, 0:cols].astype(BF)


def ring_total(value, axis):
    n = lax.axis_size(axis)
    total = value.astype(F32)
    if n == 1:
        return total
    after, across, before = (lax.ppermute(value, axis, [(i, (i + k) % n) for i in range(n)]).astype(F32) for k in (1, 2, 3))
    return (total + across) + (after + before)


def join_kernel(conv_keep, conv_other, down_keep, down_other, out, both, sems):
    n = conv_keep.shape[0]
    step = n // 2
    copies = []
    for k, (keep, other) in enumerate(((down_keep, down_other), (conv_keep, conv_other))):
        for q in range(2):
            part = slice(q * step, (q + 1) * step)
            o = (1 - k) * n + q * step
            both[o : o + step] = (keep[part] + other[part].astype(F32)).astype(BF)
            copies.append(pltpu.make_async_copy(both.at[o : o + step], out.at[o : o + step], sems.at[2 * k + q]))
            copies[-1].start()
    for copy in copies:
        copy.wait()


def unpack_rows(core, rows, conv, down, f32s, sems):
    n = rows.shape[0] // 2
    step = n // 6
    base = pl.multiple_of(core * n, n)
    copies = []
    for k, dst in enumerate((conv, down)):
        for q in range(6):
            o = k * n + q * step
            f32s[o : o + step] = rows[o : o + step].astype(F32)
            part = dst.at[pl.ds(base + q * step, step)]
            copies.append(pltpu.make_async_copy(f32s.at[o : o + step], part, sems.at[k * 6 + q]))
            copies[-1].start()
    for copy in copies:
        copy.wait()


def unpack_own(flags, rows, conv, down, f32s, sems):
    unpack_rows(flags[2], rows, conv, down, f32s, sems)


def unpack_other(flags, rows, conv_in, down_in, conv, down, f32s, sems):
    unpack_rows(1 - flags[2], rows, conv, down, f32s, sems)


def core_swap(value):
    return lax.ppermute(value, "core", [(0, 1), (1, 0)])


def local(features, conv_weight, down_weight, norm_gain, norm_bias, cotangent):
    rows, cols, chans = features.shape
    half, pairs, _ = cotangent.shape
    devices = lax.axis_size(ALL)
    lats = lax.axis_size(LAT)
    cells = rows * cols * devices
    factor = 1.0 / math.sqrt(cells)
    lat = lax.axis_index(LAT)
    odd = lax.axis_index(LON) % 2 == 1
    flags = jnp.stack([lat == 0, lat == lats - 1, lax.axis_index("core") == 1, odd]).astype(jnp.int32)
    gain = norm_gain.reshape(1, chans)
    bias = norm_bias.reshape(1, chans)
    w3 = conv_weight.reshape(3, 3 * chans, chans)
    dw3 = down_weight.reshape(3, 3 * chans, chans)
    all_rows = 9 * chans
    few = lax.axis_size(FEW)
    rest = lax.axis_size(REST)

    with jax.named_scope("halo"):
        slab = (2 * rows + 16, chans)
        (edges,) = call(
            pack_lon,
            [((2,) + slab, BF)],
            [((2, rows, 16, chans), BF), ((2, half, 16, chans), BF), (slab, F32)],
            n_in=2,
            hbm=(0, 1),
            sems=4,
        )(pinned(features), pinned(cotangent))
        lons = lax.axis_size(LON)
        pair = lax.ppermute(edges, LON, [(i, i ^ 1) for i in range(lons)])
        next_pair = lax.ppermute(edges, LON, [(i, (i + 2 * (i % 2) - 1) % lons) for i in range(lons)])
        strip = (2 * cols + pairs + 16, chans)
        to_near, to_far = call(
            pack_lat,
            [(strip, BF)] * 2,
            [(slab, F32), (slab, F32), ((2, 16, chans), F32)],
            n_in=5,
            smem=(0,),
            hbm=(1, 2),
            sems=6,
        )(flags, pinned(features), pinned(cotangent), pair, next_pair)
        near = lax.ppermute(to_near, LAT, [(i, i ^ 1) for i in range(lats)])
        gaps = range(1, lats - 1, 2)
        far = lax.ppermute(to_far, LAT, [(i, i + 1) for i in gaps] + [(i + 1, i) for i in gaps])

    plane = (rows + 2, J, chans)
    x_shape = (rows, pairs, 4 * chans)
    rim_shape = (2, pairs, 4 * chans)
    inner_plane = (rows - 2, J, chans)
    with jax.named_scope("conv"):
        x, rim, hq_in, he_in, vec = call(
            inner_kernel,
            [(x_shape, BF, True), ((4, J, 4 * chans), BF), (inner_plane, BF), (inner_plane, BF), ((2, chans), F32)],
            [
                ((rows, 2, cols + 56, 128), F32),
                ((2, 2, slab[0], 128), F32),
                ((rows, J, 5 * chans), BF),
                ((rows, cols, chans), BF),
                (w3.shape, BF),
            ],
            flops=2 * 960 * 2304 * 256,
            n_in=5,
            smem=(0,),
            hbm=(1, 4),
            sems=3,
        )(flags, pinned(features), pair, next_pair, pinned(w3))
        x_rim, h, hq, he, stat = call(
            functools.partial(outer_kernel, cols),
            [(rim_shape, BF, True), ((2,) + plane, BF, True), (plane, BF), (plane, BF), ((devices, 1, 128), F32)],
            [
                ((4, 2, cols + 56, 128), F32),
                ((2, 2, 16, 128), F32),
                ((4, J, 5 * chans), BF),
                (w3.shape, BF),
            ],
            flops=2 * 640 * 2304 * 256,
            n_in=8,
            smem=(0,),
            hbm=(7,),
            sems=5,
        )(flags, near, far, rim, hq_in, he_in, vec, pinned(w3))
        stats = lax.all_to_all(stat, ALL, 0, 0, tiled=True)
    c_shape = (half + 2, J, 2 * chans)
    with jax.named_scope("back"):
        c2, aq, ae = call(
            back_kernel,
            [(c_shape, BF, True), (plane, BF), (plane, BF)],
            [((half + 2, pairs + 32, chans), F32), ((4,) + slab, F32), (c_shape, BF)],
            flops=2 * 400 * 2304 * 256,
            n_in=7,
            smem=(0,),
            sems=1,
        )(flags, cotangent, pair, next_pair, near, far, down_weight)
    t_shape = (rows + 1, pairs, 3 * chans)
    with jax.named_scope("act"):
        t, p, coef, sums = call(
            functools.partial(act_kernel, cells),
            [(t_shape, BF, True), ((2,) + plane, F32, True), ((2, chans), F32), ((few, 4, 128), F32)],
            [((J, chans), F32), (t_shape, BF), ((2,) + plane, F32)],
            flops=1600 * 256 * 20,
            smem=(0,),
            n_in=8,
            sems=3 * rows + 5,
        )(flags, stats, hq, he, aq, ae, gain, bias)
        sums = lax.all_to_all(sums, FEW, 0, 0, tiled=True)
        (sums,) = call(merged_sums, [((rest, 4, 128), F32)], n_in=1)(sums)
        sums, c2 = lax.optimization_barrier((sums, c2))
        sums = lax.all_to_all(sums, REST, 0, 0, tiled=True)
    half_rows = (all_rows // 2, chans)
    with jax.named_scope("down"):
        output, down_keep, down_send = call(
            down_kernel,
            [((half, pairs, chans), BF), (half_rows, F32), (half_rows, BF)],
            [(t_shape, BF), (c_shape, BF), ((all_rows, chans), F32)],
            flops=4 * 256 * 2304 * 256,
            smem=(0,),
            hbm=(1, 2),
            n_in=4,
            sems=2,
        )(flags, pinned(t), pinned(c2), dw3)
        down_other = core_swap(down_send)
    h4_shape = (rows + 2, pairs, 4 * chans)
    with jax.named_scope("grad"):
        h4, conv_keep, conv_send, vec = call(
            functools.partial(grad_kernel, cells),
            [(h4_shape, BF, True), (half_rows, F32), (half_rows, BF), ((2, chans), F32)],
            [
                ((J, chans), F32),
                ((all_rows, chans), F32),
                ((2,) + plane, BF),
                ((2,) + plane, F32),
                ((rows + 2, pairs, 4 * chans), BF),
                (h4_shape, BF),
            ],
            flops=2 * 1600 * 2304 * 256,
            smem=(0,),
            hbm=(4, 5, 6, 7),
            n_in=8,
            sems=3 * (rows + 2) + 5,
        )(flags, sums, coef, gain, pinned(h), pinned(p), pinned(x), pinned(x_rim))
    with jax.named_scope("input"):
        (input_grad,) = call(
            input_kernel,
            [((rows, cols, chans), BF)],
            [((rows, 2, cols + 8, 128), F32)],
            flops=2 * 1024 * 2304 * 256,
            n_in=2,
        )(h4, conv_weight)
    with jax.named_scope("total"):
        whole_rows = (all_rows, chans)
        (mine,) = call(
            join_kernel, [(whole_rows, BF, True)], [(whole_rows, BF)], n_in=4, sems=4
        )(conv_keep, core_swap(conv_send), down_keep, down_other)
        chips = lax.axis_size(NEAR)
        share = all_rows // chips
        got = lax.all_to_all(mine.reshape(chips, share, chans), NEAR, 0, 0, tiled=True)
        got, input_grad = lax.optimization_barrier((got, input_grad))
        piece = jnp.sum(got.astype(F32), axis=0).astype(BF)
        piece = (ring_total(piece, "z_hi") * factor).astype(BF)
        whole = lax.all_to_all(jnp.broadcast_to(piece[None], (chips, share, chans)), NEAR, 0, 0, tiled=True)
        whole = whole.reshape(all_rows, chans)
        other = core_swap(whole)
        flat = (whole_rows, F32, True)
        room = [(whole_rows, F32)]
        conv_grad, down_grad = call(unpack_own, [flat, flat], room, smem=(0,), n_in=2, sems=12)(flags, whole)
        conv_grad, down_grad = call(
            unpack_other, [flat, flat], room, smem=(0,), hbm=(2, 3), n_in=4, sems=12, aliases={2: 0, 3: 1}
        )(flags, other, pinned(conv_grad), pinned(down_grad))
    shape = (3, 3, chans, chans)
    return output, input_grad, conv_grad.reshape(shape), down_grad.reshape(shape), vec[0], vec[1]


SIZES = {64: (4, 4, 2, 2), 2: (1, 1, 2, 1), 4: (2, 1, 2, 1), 8: (1, 2, 2, 2)}


def solution(mesh):
    lon, lat = mesh.devices.shape
    fine = Mesh(mesh.devices.reshape(SIZES[lon] + (lat // 2, 2)), ALL)
    band = P(LAT, LON, None)
    return jax.shard_map(
        local,
        mesh=fine,
        in_specs=(band, P(), P(), P(), P(), band),
        out_specs=(band, band, P(), P(), P(), P()),
        check_vma=False,
    )
```

```python
import functools
import math

import jax
import jax.numpy as jnp
from jax import lax
from jax.experimental import pallas as pl
from jax.experimental.pallas import tpu as pltpu
from jax.sharding import Mesh
from jax.sharding import PartitionSpec as P

EPS = 1e-05
WIDTH = 8
J = 80
LON = ("x", "z_hi", "z_lo", "y_hi")
LAT = ("y_lo", "core")
NEAR = ("x", "z_lo", "y_hi", "y_lo")
FEW = ("x", "core")
REST = ("z_hi", "z_lo", "y_hi", "y_lo")
ALL = LON + LAT
BF = jnp.bfloat16
F32 = jnp.float32


def call(body, outs, scratch=(), flops=0, smem=(), hbm=(), n_in=0, sems=0, aliases=None):
    spaces = [pltpu.SMEM if i in smem else pltpu.HBM if i in hbm else pltpu.VMEM for i in range(n_in)]
    out_spaces = [pltpu.HBM if len(o) > 2 else pltpu.VMEM for o in outs]
    return pl.pallas_call(
        body,
        out_shape=[pltpu.HBM(o[0], o[1]) if len(o) > 2 else jax.ShapeDtypeStruct(o[0], o[1]) for o in outs],
        in_specs=[pl.BlockSpec(memory_space=m) for m in spaces],
        out_specs=[pl.BlockSpec(memory_space=m) for m in out_spaces],
        scratch_shapes=[pltpu.VMEM(s, d) for s, d in scratch]
        + ([pltpu.SemaphoreType.DMA((sems,))] if sems else []),
        input_output_aliases=aliases or {},
        compiler_params=pltpu.CompilerParams(vmem_limit_bytes=24 * 1024 * 1024),
        cost_estimate=pl.CostEstimate(flops=flops, bytes_accessed=1 << 20, transcendentals=0),
    )


def pinned(value):
    return pltpu.with_memory_space_constraint(value, pltpu.HBM)


def dot(a, b):
    return jnp.dot(a, b, preferred_element_type=F32)


def dot_t(a, b):
    return lax.dot_general(a, b, (((1,), (1,)), ((), ())), preferred_element_type=F32)


def t_dot(a, b):
    return lax.dot_general(a, b, (((0,), (0,)), ((), ())), preferred_element_type=F32)


def spread_dot(table, *vectors):
    parts = []
    for v in vectors:
        high = v.astype(BF).astype(F32)
        mid = (v - high).astype(BF).astype(F32)
        parts += [high, mid, v - high - mid]
    parts.append(jnp.zeros((8 - len(parts), vectors[0].shape[1]), F32))
    out = dot(jnp.concatenate(parts, axis=0).astype(BF), table)
    return [out[3 * i : 3 * i + 1] + out[3 * i + 1 : 3 * i + 2] + out[3 * i + 2 : 3 * i + 3] for i in range(len(vectors))]


def table(n, m, row_width, col_width, shift):
    r = lax.broadcasted_iota(jnp.int32, (n, m), 0) // row_width
    c = lax.broadcasted_iota(jnp.int32, (n, m), 1) // col_width
    return jnp.where(r == c + shift, 1.0, 0.0).astype(BF)


def masks():
    j = lax.broadcasted_iota(jnp.int32, (J, 1), 0)
    odd = jnp.where((j >= 1) & (j <= 64), 1.0, 0.0)
    even = jnp.where(j <= 63, 1.0, 0.0)
    return odd, even


def pack_lon(feat_hbm, cot_hbm, out, feat, cot, f32s, sems):
    rows, cols, chans = feat_hbm.shape
    half, pairs, _ = cot_hbm.shape
    copies = []
    for k, (lo_f, lo_c) in enumerate(((cols - 16, pairs - 16), (0, 0))):
        copies.append(pltpu.make_async_copy(feat_hbm.at[:, lo_f : lo_f + 16], feat.at[k], sems.at[2 * k]))
        copies.append(pltpu.make_async_copy(cot_hbm.at[:, lo_c : lo_c + 16], cot.at[k], sems.at[2 * k + 1]))
    for copy in copies:
        copy.start()
    f32s[...] = jnp.zeros(f32s.shape, F32)
    for copy in copies:
        copy.wait()
    for k, (at_f, at_c) in enumerate(((14, 15), (0, 0))):
        for r in range(rows):
            f32s[2 * r : 2 * r + 2] = feat[k, r].astype(F32)[at_f : at_f + 2]
        for i in range(half):
            f32s[2 * rows + i : 2 * rows + i + 1] = cot[k, i].astype(F32)[at_c : at_c + 1]
        out[k] = f32s[...].astype(BF)


def fetch(feat_hbm, cot_hbm, w_hbm, feat, cot, w, sems):
    copies = [
        pltpu.make_async_copy(src, dst, sems.at[i])
        for i, (src, dst) in enumerate(((feat_hbm, feat), (cot_hbm, cot), (w_hbm, w)))
    ]
    for copy in copies:
        copy.start()
    for copy in copies:
        copy.wait()


def columns(flags, pair, next_pair, part=slice(None)):
    low = flags[3] == 0
    west = jnp.where(low, next_pair[0, :, part].astype(F32), pair[0, :, part].astype(F32))
    east = jnp.where(low, pair[1, :, part].astype(F32), next_pair[1, :, part].astype(F32))
    return west, east


def pack_lat(flags, feat, cot, pair, next_pair, near, far, w32, e32, corner):
    rows, cols, _ = feat.shape
    half, pairs, _ = cot.shape
    core = flags[2]
    for dest, last in ((near, 1 - core), (far, core)):
        top, mid = last * (rows - 2), last * (half - 1)
        for k in range(2):
            dest[k * cols : (k + 1) * cols] = feat[top + k]
        dest[2 * cols : 2 * cols + pairs] = cot[mid]
    w32[...], e32[...] = columns(flags, pair, next_pair)
    corner[...] = jnp.zeros(corner.shape, F32)
    for k, (top, mid) in enumerate(((rows - 2, half - 1), (0, 0))):
        corner[k, 0:4] = w32[2 * top : 2 * top + 4]
        corner[k, 4:8] = e32[2 * top : 2 * top + 4]
        corner[k, 8:9] = w32[2 * rows + mid : 2 * rows + mid + 1]
        corner[k, 9:10] = e32[2 * rows + mid : 2 * rows + mid + 1]
    o = 2 * cols + pairs
    near[o : o + 16] = corner[core].astype(BF)
    far[o : o + 16] = corner[1 - core].astype(BF)


def sides(flags, near, far):
    low = flags[2] == 0

    def north(lo, hi, part):
        return jnp.where(low, far[lo:hi, part].astype(F32), near[lo:hi, part].astype(F32))

    def south(lo, hi, part):
        return jnp.where(low, near[lo:hi, part].astype(F32), far[lo:hi, part].astype(F32))

    return north, south


def taps(f32s, x_out, rows, lanes):
    for r in range(rows):
        for v in range(2):
            for k in range(lanes):
                lane = k * 256 + v * 128
                x_out[r, :, lane : lane + 128] = f32s[r, v, pl.ds(14 + k, J, stride=2), :].astype(BF)


def moments(planes, cols):
    chans = planes[0][0].shape[2]
    sums = jnp.zeros((1, chans), F32)
    for (ref, rows), mask in zip(planes, masks()):
        part = jnp.zeros((J, chans), F32)
        for r in rows:
            part = part + ref[r].astype(F32)
        sums = sums + jnp.sum(part * mask, axis=0, keepdims=True)
    (total,) = spread_dot(table(chans, chans, WIDTH, WIDTH, 0), sums)
    mean = total / (len(planes[0][1]) * cols * WIDTH)
    squares = jnp.zeros((1, chans), F32)
    for (ref, rows), mask in zip(planes, masks()):
        part = jnp.zeros((J, chans), F32)
        for r in rows:
            d = ref[r].astype(F32) - mean
            part = part + d * d
        squares = squares + jnp.sum(part * mask, axis=0, keepdims=True)
    return sums, squares


def inner_kernel(
    flags, feat, pair, next_pair, w, x_hbm, rim, hq_out, he_out, vec_out, f32s, edge, x_out, sems
):
    rows, cols, chans = feat.shape
    pairs = cols // 2
    f32s[:, :, 16 + cols : 56 + cols] = jnp.zeros((rows, 2, 40, 128), F32)
    for v in range(2):
        part = slice(v * 128, v * 128 + 128)
        edge[0, v], edge[1, v] = columns(flags, pair, next_pair, part)
        for r in range(rows):
            f32s[r, v, 14:16] = edge[0, v, 2 * r : 2 * r + 2]
            f32s[r, v, 16 + cols : 18 + cols] = edge[1, v, 2 * r : 2 * r + 2]
    for v in range(2):
        f32s[:, v, 16 : 16 + cols] = feat[:, :, v * 128 : v * 128 + 128].astype(F32)
    taps(f32s, x_out, rows, 5)
    keep = pltpu.make_async_copy(x_out.at[:, 0:pairs, chans : 5 * chans], x_hbm, sems.at[0])
    keep.start()
    for i, r in enumerate((0, 1, rows - 2, rows - 1)):
        rim[i] = x_out[r, :, 0 : 4 * chans]
    n = rows - 2
    for out, lo in ((hq_out, 0), (he_out, chans)):
        acc = None
        for a in range(3):
            lhs = x_out[a : a + n, :, lo : lo + 3 * chans].reshape(n * J, 3 * chans)
            term = dot(lhs, w[a])
            acc = term if acc is None else acc + term
        out[...] = acc.astype(BF).reshape(n, J, chans)
    sums, squares = moments(((hq_out, range(n)), (he_out, range(n))), cols)
    vec_out[0:1] = sums
    vec_out[1:2] = squares
    keep.wait()


def outer_kernel(
    cols, flags, near, far, rim, hq_in, he_in, vec, w, x_hbm, hq_out, he_out, stat_out, f32s, edge, x_out, sems
):
    rows = hq_in.shape[0] + 2
    chans = hq_in.shape[2]
    pairs = cols // 2
    f32s[:, :, 16 + cols : 56 + cols] = jnp.zeros((4, 2, 40, 128), F32)
    for v in range(2):
        part = slice(v * 128, v * 128 + 128)
        for k, side in enumerate(sides(flags, near, far)):
            edge[k, v] = side(2 * cols + pairs, 2 * cols + pairs + 16, part)
            for q in range(2):
                row = q + 2 * k
                f32s[row, v, 16 : 16 + cols] = side(q * cols, (q + 1) * cols, part)
                f32s[row, v, 14:16] = edge[k, v, 2 * q : 2 * q + 2]
                f32s[row, v, 16 + cols : 18 + cols] = edge[k, v, 4 + 2 * q : 6 + 2 * q]
    taps(f32s, x_out, 4, 5)
    copies = []
    for i, r in enumerate((1, 2)):
        copies.append(pltpu.make_async_copy(x_out.at[r, 0:pairs, chans : 5 * chans], x_hbm.at[i], sems.at[i]))
        copies[-1].start()
    hq_out[2:rows] = hq_in[...]
    he_out[2:rows] = he_in[...]
    wanted = (
        ((x_out, 0), (x_out, 1), (rim, 2), (rim, 3)),
        ((x_out, 1), (rim, 0), (rim, 3), (x_out, 2)),
        ((rim, 0), (rim, 1), (x_out, 2), (x_out, 3)),
    )
    for k, out in enumerate((hq_out, he_out)):
        lo = k * chans
        acc = None
        for a in range(3):
            lhs = jnp.concatenate([ref[r, :, lo : lo + 3 * chans] for ref, r in wanted[a]], axis=0)
            term = dot(lhs, w[a])
            acc = term if acc is None else acc + term
        value = acc.astype(BF).reshape(4, J, chans)
        out[0:2] = value[0:2]
        out[rows : rows + 2] = value[2:4]
    edges = (1, rows)
    sums, squares = moments(((hq_out, edges), (he_out, edges)), cols)
    n_in = (rows - 2) * cols * WIDTH
    n_out = 2 * cols * WIDTH
    n = n_in + n_out
    gap = vec[0:1] / n_in - sums / n_out
    (means,) = spread_dot(table(chans, 128, WIDTH, 1, 0), vec[0:1] + sums)
    within, gaps = spread_dot(table(chans, 128, WIDTH, 1, -32), vec[1:2] + squares, gap)
    stat = means / n + within + (n_in * n_out / n) * gaps * gaps
    stat_out[...] = jnp.broadcast_to(stat[None], stat_out.shape)
    for copy in copies:
        copy.wait()


def merged_sums(rec, out):
    out[...] = jnp.broadcast_to(jnp.sum(rec[...], axis=0)[None], out.shape)


def back_kernel(flags, cot, pair, next_pair, near, far, dw, hq, he, c_hbm, h_hbm, aq_out, ae_out, f32s, edge, c_out, sems):
    keep_h = [pltpu.make_async_copy(h, h_hbm.at[k], sems.at[1 + k]) for k, h in enumerate((hq, he))]
    for copy in keep_h:
        copy.start()
    half, pairs, chans = cot.shape
    rows = 2 * half
    cols = 2 * pairs
    f32s[:, 16 + pairs :] = jnp.zeros((half + 2, 16, chans), F32)
    edge[0], edge[1] = columns(flags, pair, next_pair)
    every = slice(None)
    for k, side in enumerate(sides(flags, near, far)):
        row = k * (half + 1)
        f32s[row, 16 : 16 + pairs] = side(2 * cols, 2 * cols + pairs, every)
        edge[2 + k, 0:16] = side(2 * cols + pairs, 2 * cols + pairs + 16, every)
        f32s[row, 15:16] = edge[2 + k, 8:9]
        f32s[row, 16 + pairs : 17 + pairs] = edge[2 + k, 9:10]
    f32s[1 : half + 1, 16 : 16 + pairs] = cot[...].astype(F32)
    for i in range(half):
        f32s[1 + i, 15:16] = edge[0, 2 * rows + i : 2 * rows + i + 1]
        f32s[1 + i, 16 + pairs : 17 + pairs] = edge[1, 2 * rows + i : 2 * rows + i + 1]
    for s in range(half + 2):
        c_out[s, :, 0:chans] = f32s[s, 15 : 15 + J].astype(BF)
        c_out[s, :, chans : 2 * chans] = f32s[s, 16 : 16 + J].astype(BF)
    keep = pltpu.make_async_copy(c_out, c_hbm, sems.at[0])
    keep.start()
    n = half + 1
    lo_l = c_out[0:n, :, 0:chans].reshape(n * J, chans)
    lo_r = c_out[0:n, :, chans:].reshape(n * J, chans)
    hi_l = c_out[1 : n + 1, :, 0:chans].reshape(n * J, chans)
    hi_r = c_out[1 : n + 1, :, chans:].reshape(n * J, chans)

    def put(out, k, value):
        value = value.astype(BF).reshape(n, J, chans)
        for i in range(n):
            out[2 * i + k] = value[i]

    put(ae_out, 1, dot_t(hi_r, dw[1, 1]))
    put(aq_out, 1, dot_t(hi_r, dw[1, 0]) + dot_t(hi_l, dw[1, 2]))
    put(ae_out, 0, dot_t(hi_r, dw[0, 1]) + dot_t(lo_r, dw[2, 1]))
    put(
        aq_out,
        0,
        dot_t(hi_r, dw[0, 0]) + dot_t(hi_l, dw[0, 2]) + dot_t(lo_r, dw[2, 0]) + dot_t(lo_l, dw[2, 2]),
    )
    keep.wait()
    for copy in keep_h:
        copy.wait()


def act_kernel(cells, flags, stats, hq, he, aq, ae, gain, bias, t_hbm, pq_hbm, pe_hbm, coef_out, sum_out, f32s, t_out, p_out, sems):
    devices = stats.shape[0]
    rows = hq.shape[0] - 2
    chans = hq.shape[2]
    count = float(cells * WIDTH)
    local_n = count / devices
    rec = stats[...]
    total = jnp.sum(rec, axis=0)
    centre = total / devices
    dev = rec - centre[None]
    between = jnp.sum(dev * dev, axis=0)
    mean, gaps = spread_dot(table(128, chans, 1, WIDTH, 0), centre, between)
    (within,) = spread_dot(table(128, chans, 1, WIDTH, 32), total)
    var = (within + local_n * gaps) / count
    inverse = lax.rsqrt(var + EPS)
    coef_out[0:1] = mean
    coef_out[1:2] = inverse
    g = gain[...]
    b = bias[...]
    odd, even = masks()
    top = jnp.where(flags[0] == 1, 0.0, 1.0)
    bias_sum = jnp.zeros((1, chans), F32)
    gain_sum = jnp.zeros((1, chans), F32)
    copies = []
    for k, (h, a, mask) in enumerate(((hq, aq, odd), (he, ae, even))):
        is_q = k == 0
        acc_b = jnp.zeros((J, chans), F32)
        acc_g = jnp.zeros((J, chans), F32)
        for r in range(rows + 2):
            normed = (h[r].astype(F32) - mean) * inverse
            shifted = g * normed + b
            sigma = 0.5 + 0.5 * jnp.tanh(0.5 * shifted)
            pre = a[r].astype(F32) * sigma * (1.0 + shifted * (1.0 - sigma))
            p_out[k, r] = pre
            dest = pq_hbm if is_q else pe_hbm
            copies.append(pltpu.make_async_copy(p_out.at[k, r], dest.at[r], sems.at[len(copies)]))
            copies[-1].start()
            if 1 <= r <= rows:
                acc_b = acc_b + pre
                acc_g = acc_g + pre * normed
            if r <= rows:
                active = shifted * sigma
                if r == 0:
                    active = active * top
                if is_q:
                    f32s[...] = active.astype(BF).astype(F32)
                    t_out[r, :, 0:chans] = active[0:64].astype(BF)
                    t_out[r, :, 2 * chans :] = f32s[1:65].astype(BF)
                else:
                    t_out[r, :, chans : 2 * chans] = active[0:64].astype(BF)
                    copies.append(pltpu.make_async_copy(t_out.at[r], t_hbm.at[r], sems.at[len(copies)]))
                    copies[-1].start()
        bias_sum = bias_sum + jnp.sum(acc_b * mask, axis=0, keepdims=True)
        gain_sum = gain_sum + jnp.sum(acc_g * mask, axis=0, keepdims=True)
    payload = jnp.concatenate(
        [bias_sum[:, 0:128], bias_sum[:, 128:256], gain_sum[:, 0:128], gain_sum[:, 128:256]], axis=0
    )
    sum_out[...] = jnp.broadcast_to(payload[None], sum_out.shape)
    for copy in copies:
        copy.wait()


def halves(flags, full, keep, send):
    n = keep.shape[0]
    core = flags[2]
    keep[...] = full[pl.ds(pl.multiple_of(core * n, n), n)]
    send[...] = full[pl.ds(pl.multiple_of((1 - core) * n, n), n)].astype(BF)


def down_kernel(flags, t_hbm, c_hbm, dw_hbm, out, keep, send, t, c, dw, grad, sems):
    half = out.shape[0]
    pairs, chans = out.shape[1:]
    sources = ((t_hbm, t), (c_hbm, c), (dw_hbm, dw))
    loads = [pltpu.make_async_copy(src, dst, sems.at[i]) for i, (src, dst) in enumerate(sources)]
    for load in loads:
        load.start()
    for load in loads:
        load.wait()
    cot = c[1 : half + 1, 0:pairs, chans:].reshape(half * pairs, chans)
    acc = None
    for a in range(3):
        lhs = jnp.concatenate([t[2 * i + a] for i in range(half)], axis=0)
        term = dot(lhs, dw[a])
        acc = term if acc is None else acc + term
        grad[a * 3 * chans : (a + 1) * 3 * chans] = t_dot(lhs, cot)
    out[...] = acc.astype(BF).reshape(out.shape)
    halves(flags, grad, keep, send)


def grad_kernel(
    cells, flags, sums, coef, gain, pq, h_in, pe_hbm, x_hbm, rim_hbm, h4_hbm, keep, send, vec_out, f32s, conv_out, pe, x, h4_out, sems
):
    rows = pq.shape[0] - 2
    chans = pq.shape[2]
    loads = []
    loads.append(pltpu.make_async_copy(pe_hbm, pe, sems.at[0]))
    loads[0].start()
    load_x = []
    for src, dst in ((x_hbm, x.at[1 : rows + 1]), (rim_hbm.at[0], x.at[0]), (rim_hbm.at[1], x.at[rows + 1])):
        load_x.append(pltpu.make_async_copy(src, dst, sems.at[len(loads) + len(load_x)]))
        load_x[-1].start()
    first_out = len(loads) + len(load_x)
    copies = []
    count = float(cells * WIDTH)
    total = jnp.sum(sums[...], axis=0)
    bias_sum = jnp.concatenate([total[0:1], total[1:2]], axis=1)
    gain_sum = jnp.concatenate([total[2:3], total[3:4]], axis=1)
    factor = 1.0 / math.sqrt(cells)
    vec_out[0:1] = gain_sum * factor
    vec_out[1:2] = bias_sum * factor
    g = gain[...]
    first, second = spread_dot(table(chans, chans, WIDTH, WIDTH, 0), g * bias_sum, g * gain_sum)
    first = first / count
    second = second / count
    mean = coef[0:1]
    inverse = coef[1:2]
    top = jnp.where(flags[0] == 1, 0.0, 1.0)
    bottom = jnp.where(flags[1] == 1, 0.0, 1.0)
    for k in range(2):
        is_q = k == 0
        p_in = pq if is_q else pe
        if not is_q:
            loads[0].wait()
        for r in range(rows + 2):
            normed = (h_in[k, r].astype(F32) - mean) * inverse
            value = inverse * (g * p_in[r] - first - normed * second)
            if r == 0:
                value = value * top
            if r == rows + 1:
                value = value * bottom
            rounded = value.astype(BF)
            f32s[...] = rounded.astype(F32)
            moved = f32s[1:65].astype(BF)
            lo = 3 if is_q else 2
            h4_out[r, :, lo * chans : (lo + 1) * chans] = rounded[0:64]
            lo = 1 if is_q else 0
            h4_out[r, :, lo * chans : (lo + 1) * chans] = moved
            if not is_q:
                copies.append(pltpu.make_async_copy(h4_out.at[r], h4_hbm.at[r], sems.at[first_out + r]))
                copies[-1].start()
    for load in load_x:
        load.wait()
    pairs = h4_out.shape[1]
    cells_here = rows * pairs
    odd = h4_out[1 : rows + 1, :, chans : 2 * chans].reshape(cells_here, chans)
    even = h4_out[1 : rows + 1, :, 2 * chans : 3 * chans].reshape(cells_here, chans)
    for a in range(3):
        lhs = x[a : a + rows].reshape(cells_here, 4 * chans)
        part = t_dot(lhs[:, 0 : 3 * chans], even) + t_dot(lhs[:, chans : 4 * chans], odd)
        conv_out[a * 3 * chans : (a + 1) * 3 * chans] = part
    halves(flags, conv_out, keep, send)
    for copy in copies:
        copy.wait()


def input_kernel(h4, w, out, f32s):
    rows, cols, chans = out.shape
    for k, lo in ((0, 1), (1, 0)):
        acc = None
        for a in range(3):
            for b in range(3):
                lane = (lo + b) * chans
                lhs = h4[2 - a : 2 - a + rows, :, lane : lane + chans].reshape(rows * (cols // 2), chans)
                term = dot_t(lhs, w[a, b])
                acc = term if acc is None else acc + term
        acc = acc.reshape(rows, cols // 2, chans)
        for r in range(rows):
            for v in range(2):
                f32s[r, v, pl.ds(k, cols // 2, stride=2), :] = acc[r, :, v * 128 : v * 128 + 128]
    for v in range(2):
        out[:, :, v * 128 : v * 128 + 128] = f32s[:, v, 0:cols].astype(BF)


def join_kernel(conv_keep, conv_other, down_keep, down_other, out, both, sems):
    n = conv_keep.shape[0]
    step = n // 2
    copies = []
    for k, (keep, other) in enumerate(((down_keep, down_other), (conv_keep, conv_other))):
        for q in range(2):
            part = slice(q * step, (q + 1) * step)
            o = (1 - k) * n + q * step
            both[o : o + step] = (keep[part] + other[part].astype(F32)).astype(BF)
            copies.append(pltpu.make_async_copy(both.at[o : o + step], out.at[o : o + step], sems.at[2 * k + q]))
            copies[-1].start()
    for copy in copies:
        copy.wait()


def unpack_rows(core, rows, conv, down, f32s, sems):
    n = rows.shape[0] // 2
    step = n // 6
    base = pl.multiple_of(core * n, n)
    copies = []
    for k, dst in enumerate((conv, down)):
        for q in range(6):
            o = k * n + q * step
            f32s[o : o + step] = rows[o : o + step].astype(F32)
            part = dst.at[pl.ds(base + q * step, step)]
            copies.append(pltpu.make_async_copy(f32s.at[o : o + step], part, sems.at[k * 6 + q]))
            copies[-1].start()
    for copy in copies:
        copy.wait()


def unpack_own(flags, rows, conv, down, f32s, sems):
    unpack_rows(flags[2], rows, conv, down, f32s, sems)


def unpack_other(flags, rows, conv_in, down_in, conv, down, f32s, sems):
    unpack_rows(1 - flags[2], rows, conv, down, f32s, sems)


def core_swap(value):
    return lax.ppermute(value, "core", [(0, 1), (1, 0)])


def local(features, conv_weight, down_weight, norm_gain, norm_bias, cotangent):
    rows, cols, chans = features.shape
    half, pairs, _ = cotangent.shape
    devices = lax.axis_size(ALL)
    lats = lax.axis_size(LAT)
    cells = rows * cols * devices
    factor = 1.0 / math.sqrt(cells)
    lat = lax.axis_index(LAT)
    odd = lax.axis_index(LON) % 2 == 1
    flags = jnp.stack([lat == 0, lat == lats - 1, lax.axis_index("core") == 1, odd]).astype(jnp.int32)
    gain = norm_gain.reshape(1, chans)
    bias = norm_bias.reshape(1, chans)
    w3 = conv_weight.reshape(3, 3 * chans, chans)
    dw3 = down_weight.reshape(3, 3 * chans, chans)
    all_rows = 9 * chans
    few = lax.axis_size(FEW)
    rest = lax.axis_size(REST)

    with jax.named_scope("halo"):
        slab = (2 * rows + 16, chans)
        (edges,) = call(
            pack_lon,
            [((2,) + slab, BF)],
            [((2, rows, 16, chans), BF), ((2, half, 16, chans), BF), (slab, F32)],
            n_in=2,
            hbm=(0, 1),
            sems=4,
        )(pinned(features), pinned(cotangent))
        lons = lax.axis_size(LON)
        pair = lax.ppermute(edges, LON, [(i, i ^ 1) for i in range(lons)])
        next_pair = lax.ppermute(edges, LON, [(i, (i + 2 * (i % 2) - 1) % lons) for i in range(lons)])
        feat, cot, w_in = call(
            fetch, [(features.shape, BF), (cotangent.shape, BF), (w3.shape, BF)], n_in=3, hbm=(0, 1, 2), sems=3
        )(pinned(features), pinned(cotangent), pinned(w3))
        strip = (2 * cols + pairs + 16, chans)
        to_near, to_far = call(
            pack_lat,
            [(strip, BF)] * 2,
            [(slab, F32), (slab, F32), ((2, 16, chans), F32)],
            n_in=5,
            smem=(0,),
        )(flags, feat, cot, pair, next_pair)
        near = lax.ppermute(to_near, LAT, [(i, i ^ 1) for i in range(lats)])
        gaps = range(1, lats - 1, 2)
        far = lax.ppermute(to_far, LAT, [(i, i + 1) for i in gaps] + [(i + 1, i) for i in gaps])

    plane = (rows + 2, J, chans)
    x_shape = (rows, pairs, 4 * chans)
    rim_shape = (2, pairs, 4 * chans)
    inner_plane = (rows - 2, J, chans)
    with jax.named_scope("conv"):
        x, rim, hq_in, he_in, vec = call(
            inner_kernel,
            [(x_shape, BF, True), ((4, J, 4 * chans), BF), (inner_plane, BF), (inner_plane, BF), ((2, chans), F32)],
            [
                ((rows, 2, cols + 56, 128), F32),
                ((2, 2, slab[0], 128), F32),
                ((rows, J, 5 * chans), BF),
            ],
            flops=2 * 960 * 2304 * 256,
            n_in=5,
            smem=(0,),
            sems=1,
        )(flags, feat, pair, next_pair, w_in)
        x_rim, hq, he, stat = call(
            functools.partial(outer_kernel, cols),
            [(rim_shape, BF, True), (plane, BF), (plane, BF), ((devices, 1, 128), F32)],
            [
                ((4, 2, cols + 56, 128), F32),
                ((2, 2, 16, 128), F32),
                ((4, J, 5 * chans), BF),
            ],
            flops=2 * 640 * 2304 * 256,
            n_in=8,
            smem=(0,),
            sems=2,
        )(flags, near, far, rim, hq_in, he_in, vec, w_in)
        stats = lax.all_to_all(stat, ALL, 0, 0, tiled=True)
    c_shape = (half + 2, J, 2 * chans)
    with jax.named_scope("back"):
        c2, h, aq, ae = call(
            back_kernel,
            [(c_shape, BF, True), ((2,) + plane, BF, True), (plane, BF), (plane, BF)],
            [((half + 2, pairs + 32, chans), F32), ((4,) + slab, F32), (c_shape, BF)],
            flops=2 * 400 * 2304 * 256,
            n_in=9,
            smem=(0,),
            sems=3,
        )(flags, cot, pair, next_pair, near, far, down_weight, hq, he)
    t_shape = (rows + 1, pairs, 3 * chans)
    with jax.named_scope("act"):
        t, pq, pe, coef, sums = call(
            functools.partial(act_kernel, cells),
            [(t_shape, BF, True), (plane, F32, True), (plane, F32, True), ((2, chans), F32), ((few, 4, 128), F32)],
            [((J, chans), F32), (t_shape, BF), ((2,) + plane, F32)],
            flops=1600 * 256 * 20,
            smem=(0,),
            n_in=8,
            sems=3 * rows + 5,
        )(flags, stats, hq, he, aq, ae, gain, bias)
        sums = lax.all_to_all(sums, FEW, 0, 0, tiled=True)
        (sums,) = call(merged_sums, [((rest, 4, 128), F32)], n_in=1)(sums)
        sums, c2 = lax.optimization_barrier((sums, c2))
        sums = lax.all_to_all(sums, REST, 0, 0, tiled=True)
    half_rows = (all_rows // 2, chans)
    with jax.named_scope("down"):
        output, down_keep, down_send = call(
            down_kernel,
            [((half, pairs, chans), BF), (half_rows, F32), (half_rows, BF)],
            [(t_shape, BF), (c_shape, BF), (dw3.shape, BF), ((all_rows, chans), F32)],
            flops=4 * 256 * 2304 * 256,
            smem=(0,),
            hbm=(1, 2, 3),
            n_in=4,
            sems=3,
        )(flags, pinned(t), pinned(c2), pinned(dw3))
        down_other = core_swap(down_send)
    h4_shape = (rows + 2, pairs, 4 * chans)
    with jax.named_scope("grad"):
        h4, conv_keep, conv_send, vec = call(
            functools.partial(grad_kernel, cells),
            [(h4_shape, BF, True), (half_rows, F32), (half_rows, BF), ((2, chans), F32)],
            [
                ((J, chans), F32),
                ((all_rows, chans), F32),
                (plane, F32),
                ((rows + 2, pairs, 4 * chans), BF),
                (h4_shape, BF),
            ],
            flops=2 * 1600 * 2304 * 256,
            smem=(0,),
            hbm=(6, 7, 8),
            n_in=9,
            sems=3 * (rows + 2) + 3,
        )(flags, sums, coef, gain, pq, h, pinned(pe), pinned(x), pinned(x_rim))
    with jax.named_scope("input"):
        (input_grad,) = call(
            input_kernel,
            [((rows, cols, chans), BF)],
            [((rows, 2, cols + 8, 128), F32)],
            flops=2 * 1024 * 2304 * 256,
            n_in=2,
        )(h4, conv_weight)
    with jax.named_scope("total"):
        whole_rows = (all_rows, chans)
        (mine,) = call(
            join_kernel, [(whole_rows, BF, True)], [(whole_rows, BF)], n_in=4, sems=4
        )(conv_keep, core_swap(conv_send), down_keep, down_other)
        chips = lax.axis_size(NEAR)
        share = all_rows // chips
        got = lax.all_to_all(mine.reshape(chips, share, chans), NEAR, 0, 0, tiled=True)
        got, input_grad = lax.optimization_barrier((got, input_grad))
        piece = jnp.sum(got.astype(F32), axis=0).astype(BF)
        got = lax.all_to_all(
            jnp.broadcast_to(piece[None], (lax.axis_size("z_hi"), share, chans)), "z_hi", 0, 0, tiled=True
        )
        piece = (jnp.sum(got.astype(F32), axis=0) * factor).astype(BF)
        whole = lax.all_to_all(jnp.broadcast_to(piece[None], (chips, share, chans)), NEAR, 0, 0, tiled=True)
        whole = whole.reshape(all_rows, chans)
        other = core_swap(whole)
        flat = (whole_rows, F32, True)
        room = [(whole_rows, F32)]
        conv_grad, down_grad = call(unpack_own, [flat, flat], room, smem=(0,), n_in=2, sems=12)(flags, whole)
        conv_grad, down_grad = call(
            unpack_other, [flat, flat], room, smem=(0,), hbm=(2, 3), n_in=4, sems=12, aliases={2: 0, 3: 1}
        )(flags, other, pinned(conv_grad), pinned(down_grad))
    shape = (3, 3, chans, chans)
    return output, input_grad, conv_grad.reshape(shape), down_grad.reshape(shape), vec[0], vec[1]


SIZES = {64: (4, 4, 2, 2), 2: (1, 1, 2, 1), 4: (2, 1, 2, 1), 8: (1, 2, 2, 2)}


def solution(mesh):
    lon, lat = mesh.devices.shape
    fine = Mesh(mesh.devices.reshape(SIZES[lon] + (lat // 2, 2)), ALL)
    band = P(LAT, LON, None)
    return jax.shard_map(
        local,
        mesh=fine,
        in_specs=(band, P(), P(), P(), P(), band),
        out_specs=(band, band, P(), P(), P(), P()),
        check_vma=False,
    )
```

```python
import functools
import math

import jax
import jax.numpy as jnp
from jax import lax
from jax.experimental import pallas as pl
from jax.experimental.pallas import tpu as pltpu
from jax.sharding import Mesh
from jax.sharding import PartitionSpec as P

EPS = 1e-05
WIDTH = 8
J = 80
LON = ("x", "z_hi", "z_lo", "y_hi")
LAT = ("y_lo", "core")
NEAR = ("x", "z_lo", "y_hi", "y_lo")
FEW = ("x", "core")
REST = ("z_hi", "z_lo", "y_hi", "y_lo")
ALL = LON + LAT
BF = jnp.bfloat16
F32 = jnp.float32


def call(body, outs, scratch=(), flops=0, smem=(), hbm=(), n_in=0, sems=0, aliases=None):
    spaces = [pltpu.SMEM if i in smem else pltpu.HBM if i in hbm else pltpu.VMEM for i in range(n_in)]
    out_spaces = [pltpu.HBM if len(o) > 2 else pltpu.VMEM for o in outs]
    return pl.pallas_call(
        body,
        out_shape=[pltpu.HBM(o[0], o[1]) if len(o) > 2 else jax.ShapeDtypeStruct(o[0], o[1]) for o in outs],
        in_specs=[pl.BlockSpec(memory_space=m) for m in spaces],
        out_specs=[pl.BlockSpec(memory_space=m) for m in out_spaces],
        scratch_shapes=[pltpu.VMEM(s, d) for s, d in scratch]
        + ([pltpu.SemaphoreType.DMA((sems,))] if sems else []),
        input_output_aliases=aliases or {},
        compiler_params=pltpu.CompilerParams(vmem_limit_bytes=24 * 1024 * 1024),
        cost_estimate=pl.CostEstimate(flops=flops, bytes_accessed=1 << 20, transcendentals=0),
    )


def pinned(value):
    return pltpu.with_memory_space_constraint(value, pltpu.HBM)


def dot(a, b):
    return jnp.dot(a, b, preferred_element_type=F32)


def dot_t(a, b):
    return lax.dot_general(a, b, (((1,), (1,)), ((), ())), preferred_element_type=F32)


def t_dot(a, b):
    return lax.dot_general(a, b, (((0,), (0,)), ((), ())), preferred_element_type=F32)


def spread_dot(table, *vectors):
    parts = []
    for v in vectors:
        high = v.astype(BF).astype(F32)
        mid = (v - high).astype(BF).astype(F32)
        parts += [high, mid, v - high - mid]
    parts.append(jnp.zeros((8 - len(parts), vectors[0].shape[1]), F32))
    out = dot(jnp.concatenate(parts, axis=0).astype(BF), table)
    return [out[3 * i : 3 * i + 1] + out[3 * i + 1 : 3 * i + 2] + out[3 * i + 2 : 3 * i + 3] for i in range(len(vectors))]


def table(n, m, row_width, col_width, shift):
    r = lax.broadcasted_iota(jnp.int32, (n, m), 0) // row_width
    c = lax.broadcasted_iota(jnp.int32, (n, m), 1) // col_width
    return jnp.where(r == c + shift, 1.0, 0.0).astype(BF)


def masks():
    j = lax.broadcasted_iota(jnp.int32, (J, 1), 0)
    odd = jnp.where((j >= 1) & (j <= 64), 1.0, 0.0)
    even = jnp.where(j <= 63, 1.0, 0.0)
    return odd, even


def pack_lon(feat_hbm, cot_hbm, out, feat, cot, f32s, sems):
    rows, cols, chans = feat_hbm.shape
    half, pairs, _ = cot_hbm.shape
    copies = []
    for k, (lo_f, lo_c) in enumerate(((cols - 16, pairs - 16), (0, 0))):
        copies.append(pltpu.make_async_copy(feat_hbm.at[:, lo_f : lo_f + 16], feat.at[k], sems.at[2 * k]))
        copies.append(pltpu.make_async_copy(cot_hbm.at[:, lo_c : lo_c + 16], cot.at[k], sems.at[2 * k + 1]))
    for copy in copies:
        copy.start()
    f32s[...] = jnp.zeros(f32s.shape, F32)
    for copy in copies:
        copy.wait()
    for k, (at_f, at_c) in enumerate(((14, 15), (0, 0))):
        for r in range(rows):
            f32s[2 * r : 2 * r + 2] = feat[k, r].astype(F32)[at_f : at_f + 2]
        for i in range(half):
            f32s[2 * rows + i : 2 * rows + i + 1] = cot[k, i].astype(F32)[at_c : at_c + 1]
        out[k] = f32s[...].astype(BF)


def fetch(feat_hbm, cot_hbm, w_hbm, feat, cot, w, sems):
    copies = [
        pltpu.make_async_copy(src, dst, sems.at[i])
        for i, (src, dst) in enumerate(((feat_hbm, feat), (cot_hbm, cot), (w_hbm, w)))
    ]
    for copy in copies:
        copy.start()
    for copy in copies:
        copy.wait()


def columns(flags, pair, next_pair, part=slice(None)):
    low = flags[3] == 0
    west = jnp.where(low, next_pair[0, :, part].astype(F32), pair[0, :, part].astype(F32))
    east = jnp.where(low, pair[1, :, part].astype(F32), next_pair[1, :, part].astype(F32))
    return west, east


def pack_lat(flags, feat, cot, pair, next_pair, near, far, w32, e32, corner):
    rows, cols, _ = feat.shape
    half, pairs, _ = cot.shape
    core = flags[2]
    for dest, last in ((near, 1 - core), (far, core)):
        top, mid = last * (rows - 2), last * (half - 1)
        for k in range(2):
            dest[k * cols : (k + 1) * cols] = feat[top + k]
        dest[2 * cols : 2 * cols + pairs] = cot[mid]
    w32[...], e32[...] = columns(flags, pair, next_pair)
    corner[...] = jnp.zeros(corner.shape, F32)
    for k, (top, mid) in enumerate(((rows - 2, half - 1), (0, 0))):
        corner[k, 0:4] = w32[2 * top : 2 * top + 4]
        corner[k, 4:8] = e32[2 * top : 2 * top + 4]
        corner[k, 8:9] = w32[2 * rows + mid : 2 * rows + mid + 1]
        corner[k, 9:10] = e32[2 * rows + mid : 2 * rows + mid + 1]
    o = 2 * cols + pairs
    near[o : o + 16] = corner[core].astype(BF)
    far[o : o + 16] = corner[1 - core].astype(BF)


def sides(flags, near, far):
    low = flags[2] == 0

    def north(lo, hi, part):
        return jnp.where(low, far[lo:hi, part].astype(F32), near[lo:hi, part].astype(F32))

    def south(lo, hi, part):
        return jnp.where(low, near[lo:hi, part].astype(F32), far[lo:hi, part].astype(F32))

    return north, south


def taps(f32s, x_out, rows, lanes):
    for r in range(rows):
        for v in range(2):
            for k in range(lanes):
                lane = k * 256 + v * 128
                x_out[r, :, lane : lane + 128] = f32s[r, v, pl.ds(14 + k, J, stride=2), :].astype(BF)


def moments(planes, cols):
    chans = planes[0][0].shape[2]
    sums = jnp.zeros((1, chans), F32)
    for (ref, rows), mask in zip(planes, masks()):
        part = jnp.zeros((J, chans), F32)
        for r in rows:
            part = part + ref[r].astype(F32)
        sums = sums + jnp.sum(part * mask, axis=0, keepdims=True)
    (total,) = spread_dot(table(chans, chans, WIDTH, WIDTH, 0), sums)
    mean = total / (len(planes[0][1]) * cols * WIDTH)
    squares = jnp.zeros((1, chans), F32)
    for (ref, rows), mask in zip(planes, masks()):
        part = jnp.zeros((J, chans), F32)
        for r in rows:
            d = ref[r].astype(F32) - mean
            part = part + d * d
        squares = squares + jnp.sum(part * mask, axis=0, keepdims=True)
    return sums, squares


def inner_kernel(
    flags, feat, pair, next_pair, w, x_hbm, rim, hq_out, he_out, vec_out, f32s, edge, x_out, sems
):
    rows, cols, chans = feat.shape
    pairs = cols // 2
    f32s[:, :, 16 + cols : 56 + cols] = jnp.zeros((rows, 2, 40, 128), F32)
    for v in range(2):
        part = slice(v * 128, v * 128 + 128)
        edge[0, v], edge[1, v] = columns(flags, pair, next_pair, part)
        for r in range(rows):
            f32s[r, v, 14:16] = edge[0, v, 2 * r : 2 * r + 2]
            f32s[r, v, 16 + cols : 18 + cols] = edge[1, v, 2 * r : 2 * r + 2]
    for v in range(2):
        f32s[:, v, 16 : 16 + cols] = feat[:, :, v * 128 : v * 128 + 128].astype(F32)
    taps(f32s, x_out, rows, 5)
    keep = pltpu.make_async_copy(x_out.at[:, 0:pairs, chans : 5 * chans], x_hbm, sems.at[0])
    keep.start()
    for i, r in enumerate((0, 1, rows - 2, rows - 1)):
        rim[i] = x_out[r, :, 0 : 4 * chans]
    n = rows - 2
    for out, lo in ((hq_out, 0), (he_out, chans)):
        acc = None
        for a in range(3):
            lhs = x_out[a : a + n, :, lo : lo + 3 * chans].reshape(n * J, 3 * chans)
            term = dot(lhs, w[a])
            acc = term if acc is None else acc + term
        out[...] = acc.astype(BF).reshape(n, J, chans)
    sums, squares = moments(((hq_out, range(n)), (he_out, range(n))), cols)
    vec_out[0:1] = sums
    vec_out[1:2] = squares
    keep.wait()


def outer_kernel(
    cols, flags, near, far, rim, hq_in, he_in, vec, w, x_hbm, hq_out, he_out, stat_out, f32s, edge, x_out, sems
):
    rows = hq_in.shape[0] + 2
    chans = hq_in.shape[2]
    pairs = cols // 2
    f32s[:, :, 16 + cols : 56 + cols] = jnp.zeros((4, 2, 40, 128), F32)
    for v in range(2):
        part = slice(v * 128, v * 128 + 128)
        for k, side in enumerate(sides(flags, near, far)):
            edge[k, v] = side(2 * cols + pairs, 2 * cols + pairs + 16, part)
            for q in range(2):
                row = q + 2 * k
                f32s[row, v, 16 : 16 + cols] = side(q * cols, (q + 1) * cols, part)
                f32s[row, v, 14:16] = edge[k, v, 2 * q : 2 * q + 2]
                f32s[row, v, 16 + cols : 18 + cols] = edge[k, v, 4 + 2 * q : 6 + 2 * q]
    taps(f32s, x_out, 4, 5)
    copies = []
    for i, r in enumerate((1, 2)):
        copies.append(pltpu.make_async_copy(x_out.at[r, 0:pairs, chans : 5 * chans], x_hbm.at[i], sems.at[i]))
        copies[-1].start()
    hq_out[2:rows] = hq_in[...]
    he_out[2:rows] = he_in[...]
    wanted = (
        ((x_out, 0), (x_out, 1), (rim, 2), (rim, 3)),
        ((x_out, 1), (rim, 0), (rim, 3), (x_out, 2)),
        ((rim, 0), (rim, 1), (x_out, 2), (x_out, 3)),
    )
    for k, out in enumerate((hq_out, he_out)):
        lo = k * chans
        acc = None
        for a in range(3):
            lhs = jnp.concatenate([ref[r, :, lo : lo + 3 * chans] for ref, r in wanted[a]], axis=0)
            term = dot(lhs, w[a])
            acc = term if acc is None else acc + term
        value = acc.astype(BF).reshape(4, J, chans)
        out[0:2] = value[0:2]
        out[rows : rows + 2] = value[2:4]
    edges = (1, rows)
    sums, squares = moments(((hq_out, edges), (he_out, edges)), cols)
    n_in = (rows - 2) * cols * WIDTH
    n_out = 2 * cols * WIDTH
    n = n_in + n_out
    gap = vec[0:1] / n_in - sums / n_out
    (means,) = spread_dot(table(chans, 128, WIDTH, 1, 0), vec[0:1] + sums)
    within, gaps = spread_dot(table(chans, 128, WIDTH, 1, -32), vec[1:2] + squares, gap)
    stat = means / n + within + (n_in * n_out / n) * gaps * gaps
    stat_out[...] = jnp.broadcast_to(stat[None], stat_out.shape)
    for copy in copies:
        copy.wait()


def merged_sums(rec, out):
    out[...] = jnp.broadcast_to(jnp.sum(rec[...], axis=0)[None], out.shape)


def back_kernel(flags, cot, pair, next_pair, near, far, dw, hq, he, c_hbm, h_hbm, aq_out, ae_out, f32s, edge, c_out, sems):
    keep_h = [pltpu.make_async_copy(h, h_hbm.at[k], sems.at[1 + k]) for k, h in enumerate((hq, he))]
    for copy in keep_h:
        copy.start()
    half, pairs, chans = cot.shape
    rows = 2 * half
    cols = 2 * pairs
    f32s[:, 16 + pairs :] = jnp.zeros((half + 2, 16, chans), F32)
    edge[0], edge[1] = columns(flags, pair, next_pair)
    every = slice(None)
    for k, side in enumerate(sides(flags, near, far)):
        row = k * (half + 1)
        f32s[row, 16 : 16 + pairs] = side(2 * cols, 2 * cols + pairs, every)
        edge[2 + k, 0:16] = side(2 * cols + pairs, 2 * cols + pairs + 16, every)
        f32s[row, 15:16] = edge[2 + k, 8:9]
        f32s[row, 16 + pairs : 17 + pairs] = edge[2 + k, 9:10]
    f32s[1 : half + 1, 16 : 16 + pairs] = cot[...].astype(F32)
    for i in range(half):
        f32s[1 + i, 15:16] = edge[0, 2 * rows + i : 2 * rows + i + 1]
        f32s[1 + i, 16 + pairs : 17 + pairs] = edge[1, 2 * rows + i : 2 * rows + i + 1]
    for s in range(half + 2):
        c_out[s, :, 0:chans] = f32s[s, 15 : 15 + J].astype(BF)
        c_out[s, :, chans : 2 * chans] = f32s[s, 16 : 16 + J].astype(BF)
    keep = pltpu.make_async_copy(c_out, c_hbm, sems.at[0])
    keep.start()
    n = half + 1
    lo_l = c_out[0:n, :, 0:chans].reshape(n * J, chans)
    lo_r = c_out[0:n, :, chans:].reshape(n * J, chans)
    hi_l = c_out[1 : n + 1, :, 0:chans].reshape(n * J, chans)
    hi_r = c_out[1 : n + 1, :, chans:].reshape(n * J, chans)

    def put(out, k, value):
        value = value.astype(BF).reshape(n, J, chans)
        for i in range(n):
            out[2 * i + k] = value[i]

    put(ae_out, 1, dot_t(hi_r, dw[1, 1]))
    put(aq_out, 1, dot_t(hi_r, dw[1, 0]) + dot_t(hi_l, dw[1, 2]))
    put(ae_out, 0, dot_t(hi_r, dw[0, 1]) + dot_t(lo_r, dw[2, 1]))
    put(
        aq_out,
        0,
        dot_t(hi_r, dw[0, 0]) + dot_t(hi_l, dw[0, 2]) + dot_t(lo_r, dw[2, 0]) + dot_t(lo_l, dw[2, 2]),
    )
    keep.wait()
    for copy in keep_h:
        copy.wait()


def act_kernel(cells, flags, stats, hq, he, aq, ae, gain, bias, t_hbm, pq_hbm, pe_hbm, coef_out, sum_out, f32s, t_out, p_out, sems):
    devices = stats.shape[0]
    rows = hq.shape[0] - 2
    chans = hq.shape[2]
    count = float(cells * WIDTH)
    local_n = count / devices
    rec = stats[...]
    total = jnp.sum(rec, axis=0)
    centre = total / devices
    dev = rec - centre[None]
    between = jnp.sum(dev * dev, axis=0)
    mean, gaps = spread_dot(table(128, chans, 1, WIDTH, 0), centre, between)
    (within,) = spread_dot(table(128, chans, 1, WIDTH, 32), total)
    var = (within + local_n * gaps) / count
    inverse = lax.rsqrt(var + EPS)
    coef_out[0:1] = mean
    coef_out[1:2] = inverse
    g = gain[...]
    b = bias[...]
    odd, even = masks()
    top = jnp.where(flags[0] == 1, 0.0, 1.0)
    bias_sum = jnp.zeros((1, chans), F32)
    gain_sum = jnp.zeros((1, chans), F32)
    copies = []
    for k, (h, a, mask) in enumerate(((hq, aq, odd), (he, ae, even))):
        is_q = k == 0
        acc_b = jnp.zeros((J, chans), F32)
        acc_g = jnp.zeros((J, chans), F32)
        for r in range(rows + 2):
            normed = (h[r].astype(F32) - mean) * inverse
            shifted = g * normed + b
            sigma = 0.5 + 0.5 * jnp.tanh(0.5 * shifted)
            pre = a[r].astype(F32) * sigma * (1.0 + shifted * (1.0 - sigma))
            p_out[k, r] = pre
            dest = pq_hbm if is_q else pe_hbm
            copies.append(pltpu.make_async_copy(p_out.at[k, r], dest.at[r], sems.at[len(copies)]))
            copies[-1].start()
            if 1 <= r <= rows:
                acc_b = acc_b + pre
                acc_g = acc_g + pre * normed
            if r <= rows:
                active = shifted * sigma
                if r == 0:
                    active = active * top
                if is_q:
                    f32s[...] = active.astype(BF).astype(F32)
                    t_out[r, :, 0:chans] = active[0:64].astype(BF)
                    t_out[r, :, 2 * chans :] = f32s[1:65].astype(BF)
                else:
                    t_out[r, :, chans : 2 * chans] = active[0:64].astype(BF)
                    copies.append(pltpu.make_async_copy(t_out.at[r], t_hbm.at[r], sems.at[len(copies)]))
                    copies[-1].start()
        bias_sum = bias_sum + jnp.sum(acc_b * mask, axis=0, keepdims=True)
        gain_sum = gain_sum + jnp.sum(acc_g * mask, axis=0, keepdims=True)
    payload = jnp.concatenate(
        [bias_sum[:, 0:128], bias_sum[:, 128:256], gain_sum[:, 0:128], gain_sum[:, 128:256]], axis=0
    )
    sum_out[...] = jnp.broadcast_to(payload[None], sum_out.shape)
    for copy in copies:
        copy.wait()


def halves(flags, full, keep, send):
    n = keep.shape[0]
    core = flags[2]
    keep[...] = full[pl.ds(pl.multiple_of(core * n, n), n)]
    send[...] = full[pl.ds(pl.multiple_of((1 - core) * n, n), n)].astype(BF)


def down_kernel(flags, t_hbm, c_hbm, dw_hbm, out, keep, send, t, c, dw, grad, sems):
    half = out.shape[0]
    pairs, chans = out.shape[1:]
    sources = ((t_hbm, t), (c_hbm, c), (dw_hbm, dw))
    loads = [pltpu.make_async_copy(src, dst, sems.at[i]) for i, (src, dst) in enumerate(sources)]
    for load in loads:
        load.start()
    for load in loads:
        load.wait()
    cot = c[1 : half + 1, 0:pairs, chans:].reshape(half * pairs, chans)
    acc = None
    for a in range(3):
        lhs = jnp.concatenate([t[2 * i + a] for i in range(half)], axis=0)
        term = dot(lhs, dw[a])
        acc = term if acc is None else acc + term
        grad[a * 3 * chans : (a + 1) * 3 * chans] = t_dot(lhs, cot)
    out[...] = acc.astype(BF).reshape(out.shape)
    halves(flags, grad, keep, send)


def grad_kernel(
    cells, flags, sums, coef, gain, pq, h_in, pe_hbm, x_hbm, rim_hbm, h4_hbm, keep, send, vec_out, f32s, conv_out, pe, x, h4_out, sems
):
    rows = pq.shape[0] - 2
    chans = pq.shape[2]
    loads = []
    loads.append(pltpu.make_async_copy(pe_hbm, pe, sems.at[0]))
    loads[0].start()
    load_x = []
    for src, dst in ((x_hbm, x.at[1 : rows + 1]), (rim_hbm.at[0], x.at[0]), (rim_hbm.at[1], x.at[rows + 1])):
        load_x.append(pltpu.make_async_copy(src, dst, sems.at[len(loads) + len(load_x)]))
        load_x[-1].start()
    first_out = len(loads) + len(load_x)
    copies = []
    count = float(cells * WIDTH)
    total = jnp.sum(sums[...], axis=0)
    bias_sum = jnp.concatenate([total[0:1], total[1:2]], axis=1)
    gain_sum = jnp.concatenate([total[2:3], total[3:4]], axis=1)
    factor = 1.0 / math.sqrt(cells)
    vec_out[0:1] = gain_sum * factor
    vec_out[1:2] = bias_sum * factor
    g = gain[...]
    first, second = spread_dot(table(chans, chans, WIDTH, WIDTH, 0), g * bias_sum, g * gain_sum)
    first = first / count
    second = second / count
    mean = coef[0:1]
    inverse = coef[1:2]
    top = jnp.where(flags[0] == 1, 0.0, 1.0)
    bottom = jnp.where(flags[1] == 1, 0.0, 1.0)
    for k in range(2):
        is_q = k == 0
        p_in = pq if is_q else pe
        if not is_q:
            loads[0].wait()
        for r in range(rows + 2):
            normed = (h_in[k, r].astype(F32) - mean) * inverse
            value = inverse * (g * p_in[r] - first - normed * second)
            if r == 0:
                value = value * top
            if r == rows + 1:
                value = value * bottom
            rounded = value.astype(BF)
            f32s[...] = rounded.astype(F32)
            moved = f32s[1:65].astype(BF)
            lo = 3 if is_q else 2
            h4_out[r, :, lo * chans : (lo + 1) * chans] = rounded[0:64]
            lo = 1 if is_q else 0
            h4_out[r, :, lo * chans : (lo + 1) * chans] = moved
            if not is_q:
                copies.append(pltpu.make_async_copy(h4_out.at[r], h4_hbm.at[r], sems.at[first_out + r]))
                copies[-1].start()
    for load in load_x:
        load.wait()
    pairs = h4_out.shape[1]
    cells_here = rows * pairs
    odd = h4_out[1 : rows + 1, :, chans : 2 * chans].reshape(cells_here, chans)
    even = h4_out[1 : rows + 1, :, 2 * chans : 3 * chans].reshape(cells_here, chans)
    for a in range(3):
        lhs = x[a : a + rows].reshape(cells_here, 4 * chans)
        part = t_dot(lhs[:, 0 : 3 * chans], even) + t_dot(lhs[:, chans : 4 * chans], odd)
        conv_out[a * 3 * chans : (a + 1) * 3 * chans] = part
    halves(flags, conv_out, keep, send)
    for copy in copies:
        copy.wait()


def input_kernel(h4_hbm, w_hbm, out, f32s, h4, w, sems):
    rows, cols, chans = out.shape
    loads = [pltpu.make_async_copy(h4_hbm, h4, sems.at[0]), pltpu.make_async_copy(w_hbm, w, sems.at[1])]
    for load in loads:
        load.start()
    for load in loads:
        load.wait()
    for k, lo in ((0, 1), (1, 0)):
        acc = None
        for a in range(3):
            for b in range(3):
                lane = (lo + b) * chans
                lhs = h4[2 - a : 2 - a + rows, :, lane : lane + chans].reshape(rows * (cols // 2), chans)
                term = dot_t(lhs, w[a, b])
                acc = term if acc is None else acc + term
        acc = acc.reshape(rows, cols // 2, chans)
        for r in range(rows):
            for v in range(2):
                f32s[r, v, pl.ds(k, cols // 2, stride=2), :] = acc[r, :, v * 128 : v * 128 + 128]
    for v in range(2):
        out[:, :, v * 128 : v * 128 + 128] = f32s[:, v, 0:cols].astype(BF)


def join_kernel(conv_keep, conv_other, down_keep, down_other, out, both, sems):
    n = conv_keep.shape[0]
    step = n // 2
    copies = []
    for k, (keep, other) in enumerate(((down_keep, down_other), (conv_keep, conv_other))):
        for q in range(2):
            part = slice(q * step, (q + 1) * step)
            o = (1 - k) * n + q * step
            both[o : o + step] = (keep[part] + other[part].astype(F32)).astype(BF)
            copies.append(pltpu.make_async_copy(both.at[o : o + step], out.at[o : o + step], sems.at[2 * k + q]))
            copies[-1].start()
    for copy in copies:
        copy.wait()


def unpack_rows(core, rows, conv, down, f32s, sems):
    n = rows.shape[0] // 2
    step = n // 6
    base = pl.multiple_of(core * n, n)
    copies = []
    for k, dst in enumerate((conv, down)):
        for q in range(6):
            o = k * n + q * step
            f32s[o : o + step] = rows[o : o + step].astype(F32)
            part = dst.at[pl.ds(base + q * step, step)]
            copies.append(pltpu.make_async_copy(f32s.at[o : o + step], part, sems.at[k * 6 + q]))
            copies[-1].start()
    for copy in copies:
        copy.wait()


def unpack_own(flags, rows, conv, down, f32s, sems):
    unpack_rows(flags[2], rows, conv, down, f32s, sems)


def unpack_other(flags, rows, conv_in, down_in, conv, down, f32s, sems):
    unpack_rows(1 - flags[2], rows, conv, down, f32s, sems)


def core_swap(value):
    return lax.ppermute(value, "core", [(0, 1), (1, 0)])


def local(features, conv_weight, down_weight, norm_gain, norm_bias, cotangent):
    rows, cols, chans = features.shape
    half, pairs, _ = cotangent.shape
    devices = lax.axis_size(ALL)
    lats = lax.axis_size(LAT)
    cells = rows * cols * devices
    factor = 1.0 / math.sqrt(cells)
    lat = lax.axis_index(LAT)
    odd = lax.axis_index(LON) % 2 == 1
    flags = jnp.stack([lat == 0, lat == lats - 1, lax.axis_index("core") == 1, odd]).astype(jnp.int32)
    gain = norm_gain.reshape(1, chans)
    bias = norm_bias.reshape(1, chans)
    w3 = conv_weight.reshape(3, 3 * chans, chans)
    dw3 = down_weight.reshape(3, 3 * chans, chans)
    all_rows = 9 * chans
    few = lax.axis_size(FEW)
    rest = lax.axis_size(REST)

    with jax.named_scope("halo"):
        slab = (2 * rows + 16, chans)
        (edges,) = call(
            pack_lon,
            [((2,) + slab, BF)],
            [((2, rows, 16, chans), BF), ((2, half, 16, chans), BF), (slab, F32)],
            n_in=2,
            hbm=(0, 1),
            sems=4,
        )(pinned(features), pinned(cotangent))
        lons = lax.axis_size(LON)
        pair = lax.ppermute(edges, LON, [(i, i ^ 1) for i in range(lons)])
        next_pair = lax.ppermute(edges, LON, [(i, (i + 2 * (i % 2) - 1) % lons) for i in range(lons)])
        feat, cot, w_in = call(
            fetch, [(features.shape, BF), (cotangent.shape, BF), (w3.shape, BF)], n_in=3, hbm=(0, 1, 2), sems=3
        )(pinned(features), pinned(cotangent), pinned(w3))
        strip = (2 * cols + pairs + 16, chans)
        to_near, to_far = call(
            pack_lat,
            [(strip, BF)] * 2,
            [(slab, F32), (slab, F32), ((2, 16, chans), F32)],
            n_in=5,
            smem=(0,),
        )(flags, feat, cot, pair, next_pair)
        near = lax.ppermute(to_near, LAT, [(i, i ^ 1) for i in range(lats)])
        gaps = range(1, lats - 1, 2)
        far = lax.ppermute(to_far, LAT, [(i, i + 1) for i in gaps] + [(i + 1, i) for i in gaps])

    plane = (rows + 2, J, chans)
    x_shape = (rows, pairs, 4 * chans)
    rim_shape = (2, pairs, 4 * chans)
    inner_plane = (rows - 2, J, chans)
    with jax.named_scope("conv"):
        x, rim, hq_in, he_in, vec = call(
            inner_kernel,
            [(x_shape, BF, True), ((4, J, 4 * chans), BF), (inner_plane, BF), (inner_plane, BF), ((2, chans), F32)],
            [
                ((rows, 2, cols + 56, 128), F32),
                ((2, 2, slab[0], 128), F32),
                ((rows, J, 5 * chans), BF),
            ],
            flops=2 * 960 * 2304 * 256,
            n_in=5,
            smem=(0,),
            sems=1,
        )(flags, feat, pair, next_pair, w_in)
        x_rim, hq, he, stat = call(
            functools.partial(outer_kernel, cols),
            [(rim_shape, BF, True), (plane, BF), (plane, BF), ((devices, 1, 128), F32)],
            [
                ((4, 2, cols + 56, 128), F32),
                ((2, 2, 16, 128), F32),
                ((4, J, 5 * chans), BF),
            ],
            flops=2 * 640 * 2304 * 256,
            n_in=8,
            smem=(0,),
            sems=2,
        )(flags, near, far, rim, hq_in, he_in, vec, w_in)
        stats = lax.all_to_all(stat, ALL, 0, 0, tiled=True)
    c_shape = (half + 2, J, 2 * chans)
    with jax.named_scope("back"):
        c2, h, aq, ae = call(
            back_kernel,
            [(c_shape, BF, True), ((2,) + plane, BF, True), (plane, BF), (plane, BF)],
            [((half + 2, pairs + 32, chans), F32), ((4,) + slab, F32), (c_shape, BF)],
            flops=2 * 400 * 2304 * 256,
            n_in=9,
            smem=(0,),
            sems=3,
        )(flags, cot, pair, next_pair, near, far, down_weight, hq, he)
    t_shape = (rows + 1, pairs, 3 * chans)
    with jax.named_scope("act"):
        t, pq, pe, coef, sums = call(
            functools.partial(act_kernel, cells),
            [(t_shape, BF, True), (plane, F32, True), (plane, F32, True), ((2, chans), F32), ((few, 4, 128), F32)],
            [((J, chans), F32), (t_shape, BF), ((2,) + plane, F32)],
            flops=1600 * 256 * 20,
            smem=(0,),
            n_in=8,
            sems=3 * rows + 5,
        )(flags, stats, hq, he, aq, ae, gain, bias)
        sums = lax.all_to_all(sums, FEW, 0, 0, tiled=True)
        (sums,) = call(merged_sums, [((rest, 4, 128), F32)], n_in=1)(sums)
        sums, c2 = lax.optimization_barrier((sums, c2))
        sums = lax.all_to_all(sums, REST, 0, 0, tiled=True)
    half_rows = (all_rows // 2, chans)
    with jax.named_scope("down"):
        output, down_keep, down_send = call(
            down_kernel,
            [((half, pairs, chans), BF), (half_rows, F32), (half_rows, BF)],
            [(t_shape, BF), (c_shape, BF), (dw3.shape, BF), ((all_rows, chans), F32)],
            flops=4 * 256 * 2304 * 256,
            smem=(0,),
            hbm=(1, 2, 3),
            n_in=4,
            sems=3,
        )(flags, pinned(t), pinned(c2), pinned(dw3))
        down_other = core_swap(down_send)
    h4_shape = (rows + 2, pairs, 4 * chans)
    with jax.named_scope("grad"):
        h4, conv_keep, conv_send, vec = call(
            functools.partial(grad_kernel, cells),
            [(h4_shape, BF, True), (half_rows, F32), (half_rows, BF), ((2, chans), F32)],
            [
                ((J, chans), F32),
                ((all_rows, chans), F32),
                (plane, F32),
                ((rows + 2, pairs, 4 * chans), BF),
                (h4_shape, BF),
            ],
            flops=2 * 1600 * 2304 * 256,
            smem=(0,),
            hbm=(6, 7, 8),
            n_in=9,
            sems=3 * (rows + 2) + 3,
        )(flags, sums, coef, gain, pq, h, pinned(pe), pinned(x), pinned(x_rim))
    with jax.named_scope("input"):
        (input_grad,) = call(
            input_kernel,
            [((rows, cols, chans), BF)],
            [((rows, 2, cols + 8, 128), F32), (h4_shape, BF), (conv_weight.shape, BF)],
            flops=2 * 1024 * 2304 * 256,
            n_in=2,
            hbm=(0, 1),
            sems=2,
        )(pinned(h4), pinned(conv_weight))
    with jax.named_scope("total"):
        whole_rows = (all_rows, chans)
        (mine,) = call(
            join_kernel, [(whole_rows, BF, True)], [(whole_rows, BF)], n_in=4, sems=4
        )(conv_keep, core_swap(conv_send), down_keep, down_other)
        chips = lax.axis_size(NEAR)
        share = all_rows // chips
        got = lax.all_to_all(mine.reshape(chips, share, chans), NEAR, 0, 0, tiled=True)
        got, input_grad = lax.optimization_barrier((got, input_grad))
        piece = jnp.sum(got.astype(F32), axis=0).astype(BF)
        got = lax.all_to_all(
            jnp.broadcast_to(piece[None], (lax.axis_size("z_hi"), share, chans)), "z_hi", 0, 0, tiled=True
        )
        piece = (jnp.sum(got.astype(F32), axis=0) * factor).astype(BF)
        whole = lax.all_to_all(jnp.broadcast_to(piece[None], (chips, share, chans)), NEAR, 0, 0, tiled=True)
        whole = whole.reshape(all_rows, chans)
        other = core_swap(whole)
        flat = (whole_rows, F32, True)
        room = [(whole_rows, F32)]
        conv_grad, down_grad = call(unpack_own, [flat, flat], room, smem=(0,), n_in=2, sems=12)(flags, whole)
        conv_grad, down_grad = call(
            unpack_other, [flat, flat], room, smem=(0,), hbm=(2, 3), n_in=4, sems=12, aliases={2: 0, 3: 1}
        )(flags, other, pinned(conv_grad), pinned(down_grad))
    shape = (3, 3, chans, chans)
    return output, input_grad, conv_grad.reshape(shape), down_grad.reshape(shape), vec[0], vec[1]


SIZES = {64: (4, 4, 2, 2), 2: (1, 1, 2, 1), 4: (2, 1, 2, 1), 8: (1, 2, 2, 2)}


def solution(mesh):
    lon, lat = mesh.devices.shape
    fine = Mesh(mesh.devices.reshape(SIZES[lon] + (lat // 2, 2)), ALL)
    band = P(LAT, LON, None)
    return jax.shard_map(
        local,
        mesh=fine,
        in_specs=(band, P(), P(), P(), P(), band),
        out_specs=(band, band, P(), P(), P(), P()),
        check_vma=False,
    )
```

```python
import functools
import math

import jax
import jax.numpy as jnp
from jax import lax
from jax.experimental import pallas as pl
from jax.experimental.pallas import tpu as pltpu
from jax.sharding import Mesh
from jax.sharding import PartitionSpec as P

EPS = 1e-05
WIDTH = 8
J = 80
LON = ("x", "z_hi", "z_lo", "y_hi")
LAT = ("y_lo", "core")
NEAR = ("x", "z_lo", "y_hi", "y_lo")
FEW = ("x", "core")
REST = ("z_hi", "z_lo", "y_hi", "y_lo")
ALL = LON + LAT
BF = jnp.bfloat16
F32 = jnp.float32


def call(body, outs, scratch=(), flops=0, smem=(), hbm=(), n_in=0, sems=0, aliases=None):
    spaces = [pltpu.SMEM if i in smem else pltpu.HBM if i in hbm else pltpu.VMEM for i in range(n_in)]
    out_spaces = [pltpu.HBM if len(o) > 2 else pltpu.VMEM for o in outs]
    return pl.pallas_call(
        body,
        out_shape=[pltpu.HBM(o[0], o[1]) if len(o) > 2 else jax.ShapeDtypeStruct(o[0], o[1]) for o in outs],
        in_specs=[pl.BlockSpec(memory_space=m) for m in spaces],
        out_specs=[pl.BlockSpec(memory_space=m) for m in out_spaces],
        scratch_shapes=[pltpu.VMEM(s, d) for s, d in scratch]
        + ([pltpu.SemaphoreType.DMA((sems,))] if sems else []),
        input_output_aliases=aliases or {},
        compiler_params=pltpu.CompilerParams(vmem_limit_bytes=24 * 1024 * 1024),
        cost_estimate=pl.CostEstimate(flops=flops, bytes_accessed=1 << 20, transcendentals=0),
    )


def pinned(value):
    return pltpu.with_memory_space_constraint(value, pltpu.HBM)


def dot(a, b):
    return jnp.dot(a, b, preferred_element_type=F32)


def dot_t(a, b):
    return lax.dot_general(a, b, (((1,), (1,)), ((), ())), preferred_element_type=F32)


def t_dot(a, b):
    return lax.dot_general(a, b, (((0,), (0,)), ((), ())), preferred_element_type=F32)


def spread_dot(table, *vectors):
    parts = []
    for v in vectors:
        high = v.astype(BF).astype(F32)
        mid = (v - high).astype(BF).astype(F32)
        parts += [high, mid, v - high - mid]
    parts.append(jnp.zeros((8 - len(parts), vectors[0].shape[1]), F32))
    out = dot(jnp.concatenate(parts, axis=0).astype(BF), table)
    return [out[3 * i : 3 * i + 1] + out[3 * i + 1 : 3 * i + 2] + out[3 * i + 2 : 3 * i + 3] for i in range(len(vectors))]


def table(n, m, row_width, col_width, shift):
    r = lax.broadcasted_iota(jnp.int32, (n, m), 0) // row_width
    c = lax.broadcasted_iota(jnp.int32, (n, m), 1) // col_width
    return jnp.where(r == c + shift, 1.0, 0.0).astype(BF)


def masks():
    j = lax.broadcasted_iota(jnp.int32, (J, 1), 0)
    odd = jnp.where((j >= 1) & (j <= 64), 1.0, 0.0)
    even = jnp.where(j <= 63, 1.0, 0.0)
    return odd, even


def pack_lon(feat_hbm, cot_hbm, out, feat, cot, f32s, sems):
    rows, cols, chans = feat_hbm.shape
    half, pairs, _ = cot_hbm.shape
    copies = []
    for k, (lo_f, lo_c) in enumerate(((cols - 16, pairs - 16), (0, 0))):
        copies.append(pltpu.make_async_copy(feat_hbm.at[:, lo_f : lo_f + 16], feat.at[k], sems.at[2 * k]))
        copies.append(pltpu.make_async_copy(cot_hbm.at[:, lo_c : lo_c + 16], cot.at[k], sems.at[2 * k + 1]))
    for copy in copies:
        copy.start()
    f32s[...] = jnp.zeros(f32s.shape, F32)
    for copy in copies:
        copy.wait()
    for k, (at_f, at_c) in enumerate(((14, 15), (0, 0))):
        for r in range(rows):
            f32s[2 * r : 2 * r + 2] = feat[k, r].astype(F32)[at_f : at_f + 2]
        for i in range(half):
            f32s[2 * rows + i : 2 * rows + i + 1] = cot[k, i].astype(F32)[at_c : at_c + 1]
        out[k] = f32s[...].astype(BF)


def fetch(feat_hbm, cot_hbm, w_hbm, feat, cot, w, sems):
    copies = [
        pltpu.make_async_copy(src, dst, sems.at[i])
        for i, (src, dst) in enumerate(((feat_hbm, feat), (cot_hbm, cot), (w_hbm, w)))
    ]
    for copy in copies:
        copy.start()
    for copy in copies:
        copy.wait()


def columns(from_west, from_east, part=slice(None)):
    return from_west[0, :, part].astype(F32), from_east[1, :, part].astype(F32)


def pack_lat(flags, feat, cot, from_west, from_east, near, far, w32, e32, corner):
    rows, cols, _ = feat.shape
    half, pairs, _ = cot.shape
    core = flags[2]
    for dest, last in ((near, 1 - core), (far, core)):
        top, mid = last * (rows - 2), last * (half - 1)
        for k in range(2):
            dest[k * cols : (k + 1) * cols] = feat[top + k]
        dest[2 * cols : 2 * cols + pairs] = cot[mid]
    w32[...], e32[...] = columns(from_west, from_east)
    corner[...] = jnp.zeros(corner.shape, F32)
    for k, (top, mid) in enumerate(((rows - 2, half - 1), (0, 0))):
        corner[k, 0:4] = w32[2 * top : 2 * top + 4]
        corner[k, 4:8] = e32[2 * top : 2 * top + 4]
        corner[k, 8:9] = w32[2 * rows + mid : 2 * rows + mid + 1]
        corner[k, 9:10] = e32[2 * rows + mid : 2 * rows + mid + 1]
    o = 2 * cols + pairs
    near[o : o + 16] = corner[core].astype(BF)
    far[o : o + 16] = corner[1 - core].astype(BF)


def sides(flags, near, far):
    low = flags[2] == 0

    def north(lo, hi, part):
        return jnp.where(low, far[lo:hi, part].astype(F32), near[lo:hi, part].astype(F32))

    def south(lo, hi, part):
        return jnp.where(low, near[lo:hi, part].astype(F32), far[lo:hi, part].astype(F32))

    return north, south


def taps(f32s, x_out, rows, lanes):
    for r in range(rows):
        for v in range(2):
            for k in range(lanes):
                lane = k * 256 + v * 128
                x_out[r, :, lane : lane + 128] = f32s[r, v, pl.ds(14 + k, J, stride=2), :].astype(BF)


def moments(planes, cols):
    chans = planes[0][0].shape[2]
    sums = jnp.zeros((1, chans), F32)
    for (ref, rows), mask in zip(planes, masks()):
        part = jnp.zeros((J, chans), F32)
        for r in rows:
            part = part + ref[r].astype(F32)
        sums = sums + jnp.sum(part * mask, axis=0, keepdims=True)
    (total,) = spread_dot(table(chans, chans, WIDTH, WIDTH, 0), sums)
    mean = total / (len(planes[0][1]) * cols * WIDTH)
    squares = jnp.zeros((1, chans), F32)
    for (ref, rows), mask in zip(planes, masks()):
        part = jnp.zeros((J, chans), F32)
        for r in rows:
            d = ref[r].astype(F32) - mean
            part = part + d * d
        squares = squares + jnp.sum(part * mask, axis=0, keepdims=True)
    return sums, squares


def inner_kernel(
    flags, feat, from_west, from_east, w, x_hbm, rim, hq_out, he_out, vec_out, f32s, edge, x_out, sems
):
    rows, cols, chans = feat.shape
    pairs = cols // 2
    f32s[:, :, 16 + cols : 56 + cols] = jnp.zeros((rows, 2, 40, 128), F32)
    for v in range(2):
        part = slice(v * 128, v * 128 + 128)
        edge[0, v], edge[1, v] = columns(from_west, from_east, part)
        for r in range(rows):
            f32s[r, v, 14:16] = edge[0, v, 2 * r : 2 * r + 2]
            f32s[r, v, 16 + cols : 18 + cols] = edge[1, v, 2 * r : 2 * r + 2]
    for v in range(2):
        f32s[:, v, 16 : 16 + cols] = feat[:, :, v * 128 : v * 128 + 128].astype(F32)
    taps(f32s, x_out, rows, 5)
    keep = pltpu.make_async_copy(x_out.at[:, 0:pairs, chans : 5 * chans], x_hbm, sems.at[0])
    keep.start()
    for i, r in enumerate((0, 1, rows - 2, rows - 1)):
        rim[i] = x_out[r, :, 0 : 4 * chans]
    n = rows - 2
    for out, lo in ((hq_out, 0), (he_out, chans)):
        acc = None
        for a in range(3):
            lhs = x_out[a : a + n, :, lo : lo + 3 * chans].reshape(n * J, 3 * chans)
            term = dot(lhs, w[a])
            acc = term if acc is None else acc + term
        out[...] = acc.astype(BF).reshape(n, J, chans)
    sums, squares = moments(((hq_out, range(n)), (he_out, range(n))), cols)
    vec_out[0:1] = sums
    vec_out[1:2] = squares
    keep.wait()


def outer_kernel(
    cols, flags, near, far, rim, hq_in, he_in, vec, w, x_hbm, hq_out, he_out, stat_out, f32s, edge, x_out, sems
):
    rows = hq_in.shape[0] + 2
    chans = hq_in.shape[2]
    pairs = cols // 2
    f32s[:, :, 16 + cols : 56 + cols] = jnp.zeros((4, 2, 40, 128), F32)
    for v in range(2):
        part = slice(v * 128, v * 128 + 128)
        for k, side in enumerate(sides(flags, near, far)):
            edge[k, v] = side(2 * cols + pairs, 2 * cols + pairs + 16, part)
            for q in range(2):
                row = q + 2 * k
                f32s[row, v, 16 : 16 + cols] = side(q * cols, (q + 1) * cols, part)
                f32s[row, v, 14:16] = edge[k, v, 2 * q : 2 * q + 2]
                f32s[row, v, 16 + cols : 18 + cols] = edge[k, v, 4 + 2 * q : 6 + 2 * q]
    taps(f32s, x_out, 4, 5)
    copies = []
    for i, r in enumerate((1, 2)):
        copies.append(pltpu.make_async_copy(x_out.at[r, 0:pairs, chans : 5 * chans], x_hbm.at[i], sems.at[i]))
        copies[-1].start()
    hq_out[2:rows] = hq_in[...]
    he_out[2:rows] = he_in[...]
    wanted = (
        ((x_out, 0), (x_out, 1), (rim, 2), (rim, 3)),
        ((x_out, 1), (rim, 0), (rim, 3), (x_out, 2)),
        ((rim, 0), (rim, 1), (x_out, 2), (x_out, 3)),
    )
    for k, out in enumerate((hq_out, he_out)):
        lo = k * chans
        acc = None
        for a in range(3):
            lhs = jnp.concatenate([ref[r, :, lo : lo + 3 * chans] for ref, r in wanted[a]], axis=0)
            term = dot(lhs, w[a])
            acc = term if acc is None else acc + term
        value = acc.astype(BF).reshape(4, J, chans)
        out[0:2] = value[0:2]
        out[rows : rows + 2] = value[2:4]
    edges = (1, rows)
    sums, squares = moments(((hq_out, edges), (he_out, edges)), cols)
    n_in = (rows - 2) * cols * WIDTH
    n_out = 2 * cols * WIDTH
    n = n_in + n_out
    gap = vec[0:1] / n_in - sums / n_out
    (means,) = spread_dot(table(chans, 128, WIDTH, 1, 0), vec[0:1] + sums)
    within, gaps = spread_dot(table(chans, 128, WIDTH, 1, -32), vec[1:2] + squares, gap)
    stat = means / n + within + (n_in * n_out / n) * gaps * gaps
    stat_out[...] = jnp.broadcast_to(stat[None], stat_out.shape)
    for copy in copies:
        copy.wait()


def merged_sums(rec, out):
    out[...] = jnp.broadcast_to(jnp.sum(rec[...], axis=0)[None], out.shape)


def back_kernel(flags, cot, from_west, from_east, near, far, dw, hq, he, c_hbm, h_hbm, aq_out, ae_out, f32s, edge, c_out, sems):
    keep_h = [pltpu.make_async_copy(h, h_hbm.at[k], sems.at[1 + k]) for k, h in enumerate((hq, he))]
    for copy in keep_h:
        copy.start()
    half, pairs, chans = cot.shape
    rows = 2 * half
    cols = 2 * pairs
    f32s[:, 16 + pairs :] = jnp.zeros((half + 2, 16, chans), F32)
    edge[0], edge[1] = columns(from_west, from_east)
    every = slice(None)
    for k, side in enumerate(sides(flags, near, far)):
        row = k * (half + 1)
        f32s[row, 16 : 16 + pairs] = side(2 * cols, 2 * cols + pairs, every)
        edge[2 + k, 0:16] = side(2 * cols + pairs, 2 * cols + pairs + 16, every)
        f32s[row, 15:16] = edge[2 + k, 8:9]
        f32s[row, 16 + pairs : 17 + pairs] = edge[2 + k, 9:10]
    f32s[1 : half + 1, 16 : 16 + pairs] = cot[...].astype(F32)
    for i in range(half):
        f32s[1 + i, 15:16] = edge[0, 2 * rows + i : 2 * rows + i + 1]
        f32s[1 + i, 16 + pairs : 17 + pairs] = edge[1, 2 * rows + i : 2 * rows + i + 1]
    for s in range(half + 2):
        c_out[s, :, 0:chans] = f32s[s, 15 : 15 + J].astype(BF)
        c_out[s, :, chans : 2 * chans] = f32s[s, 16 : 16 + J].astype(BF)
    keep = pltpu.make_async_copy(c_out, c_hbm, sems.at[0])
    keep.start()
    n = half + 1
    lo_l = c_out[0:n, :, 0:chans].reshape(n * J, chans)
    lo_r = c_out[0:n, :, chans:].reshape(n * J, chans)
    hi_l = c_out[1 : n + 1, :, 0:chans].reshape(n * J, chans)
    hi_r = c_out[1 : n + 1, :, chans:].reshape(n * J, chans)

    def put(out, k, value):
        value = value.astype(BF).reshape(n, J, chans)
        for i in range(n):
            out[2 * i + k] = value[i]

    put(ae_out, 1, dot_t(hi_r, dw[1, 1]))
    put(aq_out, 1, dot_t(hi_r, dw[1, 0]) + dot_t(hi_l, dw[1, 2]))
    put(ae_out, 0, dot_t(hi_r, dw[0, 1]) + dot_t(lo_r, dw[2, 1]))
    put(
        aq_out,
        0,
        dot_t(hi_r, dw[0, 0]) + dot_t(hi_l, dw[0, 2]) + dot_t(lo_r, dw[2, 0]) + dot_t(lo_l, dw[2, 2]),
    )
    keep.wait()
    for copy in keep_h:
        copy.wait()


def act_kernel(cells, flags, stats, hq, he, aq, ae, gain, bias, t_hbm, pq_hbm, pe_hbm, coef_out, sum_out, f32s, t_out, p_out, sems):
    devices = stats.shape[0]
    rows = hq.shape[0] - 2
    chans = hq.shape[2]
    count = float(cells * WIDTH)
    local_n = count / devices
    rec = stats[...]
    total = jnp.sum(rec, axis=0)
    centre = total / devices
    dev = rec - centre[None]
    between = jnp.sum(dev * dev, axis=0)
    mean, gaps = spread_dot(table(128, chans, 1, WIDTH, 0), centre, between)
    (within,) = spread_dot(table(128, chans, 1, WIDTH, 32), total)
    var = (within + local_n * gaps) / count
    inverse = lax.rsqrt(var + EPS)
    coef_out[0:1] = mean
    coef_out[1:2] = inverse
    g = gain[...]
    b = bias[...]
    odd, even = masks()
    top = jnp.where(flags[0] == 1, 0.0, 1.0)
    bias_sum = jnp.zeros((1, chans), F32)
    gain_sum = jnp.zeros((1, chans), F32)
    copies = []
    for k, (h, a, mask) in enumerate(((hq, aq, odd), (he, ae, even))):
        is_q = k == 0
        acc_b = jnp.zeros((J, chans), F32)
        acc_g = jnp.zeros((J, chans), F32)
        for r in range(rows + 2):
            normed = (h[r].astype(F32) - mean) * inverse
            shifted = g * normed + b
            sigma = 0.5 + 0.5 * jnp.tanh(0.5 * shifted)
            pre = a[r].astype(F32) * sigma * (1.0 + shifted * (1.0 - sigma))
            p_out[k, r] = pre
            dest = pq_hbm if is_q else pe_hbm
            copies.append(pltpu.make_async_copy(p_out.at[k, r], dest.at[r], sems.at[len(copies)]))
            copies[-1].start()
            if 1 <= r <= rows:
                acc_b = acc_b + pre
                acc_g = acc_g + pre * normed
            if r <= rows:
                active = shifted * sigma
                if r == 0:
                    active = active * top
                if is_q:
                    f32s[...] = active.astype(BF).astype(F32)
                    t_out[r, :, 0:chans] = active[0:64].astype(BF)
                    t_out[r, :, 2 * chans :] = f32s[1:65].astype(BF)
                else:
                    t_out[r, :, chans : 2 * chans] = active[0:64].astype(BF)
                    copies.append(pltpu.make_async_copy(t_out.at[r], t_hbm.at[r], sems.at[len(copies)]))
                    copies[-1].start()
        bias_sum = bias_sum + jnp.sum(acc_b * mask, axis=0, keepdims=True)
        gain_sum = gain_sum + jnp.sum(acc_g * mask, axis=0, keepdims=True)
    payload = jnp.concatenate(
        [bias_sum[:, 0:128], bias_sum[:, 128:256], gain_sum[:, 0:128], gain_sum[:, 128:256]], axis=0
    )
    sum_out[...] = jnp.broadcast_to(payload[None], sum_out.shape)
    for copy in copies:
        copy.wait()


def halves(flags, full, keep, send):
    n = keep.shape[0]
    core = flags[2]
    keep[...] = full[pl.ds(pl.multiple_of(core * n, n), n)]
    send[...] = full[pl.ds(pl.multiple_of((1 - core) * n, n), n)].astype(BF)


def down_kernel(flags, t_hbm, c_hbm, dw_hbm, out, keep, send, t, c, dw, grad, sems):
    half = out.shape[0]
    pairs, chans = out.shape[1:]
    sources = ((t_hbm, t), (c_hbm, c), (dw_hbm, dw))
    loads = [pltpu.make_async_copy(src, dst, sems.at[i]) for i, (src, dst) in enumerate(sources)]
    for load in loads:
        load.start()
    for load in loads:
        load.wait()
    cot = c[1 : half + 1, 0:pairs, chans:].reshape(half * pairs, chans)
    acc = None
    for a in range(3):
        lhs = jnp.concatenate([t[2 * i + a] for i in range(half)], axis=0)
        term = dot(lhs, dw[a])
        acc = term if acc is None else acc + term
        grad[a * 3 * chans : (a + 1) * 3 * chans] = t_dot(lhs, cot)
    out[...] = acc.astype(BF).reshape(out.shape)
    halves(flags, grad, keep, send)


def grad_kernel(
    cells, flags, sums, coef, gain, pq, h_in, pe_hbm, x_hbm, rim_hbm, h4_hbm, keep, send, vec_out, f32s, conv_out, pe, x, h4_out, sems
):
    rows = pq.shape[0] - 2
    chans = pq.shape[2]
    loads = []
    loads.append(pltpu.make_async_copy(pe_hbm, pe, sems.at[0]))
    loads[0].start()
    load_x = []
    for src, dst in ((x_hbm, x.at[1 : rows + 1]), (rim_hbm.at[0], x.at[0]), (rim_hbm.at[1], x.at[rows + 1])):
        load_x.append(pltpu.make_async_copy(src, dst, sems.at[len(loads) + len(load_x)]))
        load_x[-1].start()
    first_out = len(loads) + len(load_x)
    copies = []
    count = float(cells * WIDTH)
    total = jnp.sum(sums[...], axis=0)
    bias_sum = jnp.concatenate([total[0:1], total[1:2]], axis=1)
    gain_sum = jnp.concatenate([total[2:3], total[3:4]], axis=1)
    factor = 1.0 / math.sqrt(cells)
    vec_out[0:1] = gain_sum * factor
    vec_out[1:2] = bias_sum * factor
    g = gain[...]
    first, second = spread_dot(table(chans, chans, WIDTH, WIDTH, 0), g * bias_sum, g * gain_sum)
    first = first / count
    second = second / count
    mean = coef[0:1]
    inverse = coef[1:2]
    top = jnp.where(flags[0] == 1, 0.0, 1.0)
    bottom = jnp.where(flags[1] == 1, 0.0, 1.0)
    for k in range(2):
        is_q = k == 0
        p_in = pq if is_q else pe
        if not is_q:
            loads[0].wait()
        for r in range(rows + 2):
            normed = (h_in[k, r].astype(F32) - mean) * inverse
            value = inverse * (g * p_in[r] - first - normed * second)
            if r == 0:
                value = value * top
            if r == rows + 1:
                value = value * bottom
            rounded = value.astype(BF)
            f32s[...] = rounded.astype(F32)
            moved = f32s[1:65].astype(BF)
            lo = 3 if is_q else 2
            h4_out[r, :, lo * chans : (lo + 1) * chans] = rounded[0:64]
            lo = 1 if is_q else 0
            h4_out[r, :, lo * chans : (lo + 1) * chans] = moved
            if not is_q:
                copies.append(pltpu.make_async_copy(h4_out.at[r], h4_hbm.at[r], sems.at[first_out + r]))
                copies[-1].start()
    for load in load_x:
        load.wait()
    pairs = h4_out.shape[1]
    cells_here = rows * pairs
    odd = h4_out[1 : rows + 1, :, chans : 2 * chans].reshape(cells_here, chans)
    even = h4_out[1 : rows + 1, :, 2 * chans : 3 * chans].reshape(cells_here, chans)
    for a in range(3):
        lhs = x[a : a + rows].reshape(cells_here, 4 * chans)
        part = t_dot(lhs[:, 0 : 3 * chans], even) + t_dot(lhs[:, chans : 4 * chans], odd)
        conv_out[a * 3 * chans : (a + 1) * 3 * chans] = part
    halves(flags, conv_out, keep, send)
    for copy in copies:
        copy.wait()


def input_kernel(h4_hbm, w_hbm, out, f32s, h4, w, sems):
    rows, cols, chans = out.shape
    loads = [pltpu.make_async_copy(h4_hbm, h4, sems.at[0]), pltpu.make_async_copy(w_hbm, w, sems.at[1])]
    for load in loads:
        load.start()
    for load in loads:
        load.wait()
    for k, lo in ((0, 1), (1, 0)):
        acc = None
        for a in range(3):
            for b in range(3):
                lane = (lo + b) * chans
                lhs = h4[2 - a : 2 - a + rows, :, lane : lane + chans].reshape(rows * (cols // 2), chans)
                term = dot_t(lhs, w[a, b])
                acc = term if acc is None else acc + term
        acc = acc.reshape(rows, cols // 2, chans)
        for r in range(rows):
            for v in range(2):
                f32s[r, v, pl.ds(k, cols // 2, stride=2), :] = acc[r, :, v * 128 : v * 128 + 128]
    for v in range(2):
        out[:, :, v * 128 : v * 128 + 128] = f32s[:, v, 0:cols].astype(BF)


def join_kernel(conv_keep, conv_other, down_keep, down_other, out, both, sems):
    n = conv_keep.shape[0]
    step = n // 2
    copies = []
    for k, (keep, other) in enumerate(((down_keep, down_other), (conv_keep, conv_other))):
        for q in range(2):
            part = slice(q * step, (q + 1) * step)
            o = (1 - k) * n + q * step
            both[o : o + step] = (keep[part] + other[part].astype(F32)).astype(BF)
            copies.append(pltpu.make_async_copy(both.at[o : o + step], out.at[o : o + step], sems.at[2 * k + q]))
            copies[-1].start()
    for copy in copies:
        copy.wait()


def unpack_rows(core, rows, conv, down, f32s, sems):
    n = rows.shape[0] // 2
    step = n // 6
    base = pl.multiple_of(core * n, n)
    copies = []
    for k, dst in enumerate((conv, down)):
        for q in range(6):
            o = k * n + q * step
            f32s[o : o + step] = rows[o : o + step].astype(F32)
            part = dst.at[pl.ds(base + q * step, step)]
            copies.append(pltpu.make_async_copy(f32s.at[o : o + step], part, sems.at[k * 6 + q]))
            copies[-1].start()
    for copy in copies:
        copy.wait()


def unpack_own(flags, rows, conv, down, f32s, sems):
    unpack_rows(flags[2], rows, conv, down, f32s, sems)


def unpack_other(flags, rows, conv_in, down_in, conv, down, f32s, sems):
    unpack_rows(1 - flags[2], rows, conv, down, f32s, sems)


def core_swap(value):
    return lax.ppermute(value, "core", [(0, 1), (1, 0)])


def local(features, conv_weight, down_weight, norm_gain, norm_bias, cotangent):
    rows, cols, chans = features.shape
    half, pairs, _ = cotangent.shape
    devices = lax.axis_size(ALL)
    lats = lax.axis_size(LAT)
    cells = rows * cols * devices
    factor = 1.0 / math.sqrt(cells)
    lat = lax.axis_index(LAT)
    flags = jnp.stack([lat == 0, lat == lats - 1, lax.axis_index("core") == 1]).astype(jnp.int32)
    gain = norm_gain.reshape(1, chans)
    bias = norm_bias.reshape(1, chans)
    w3 = conv_weight.reshape(3, 3 * chans, chans)
    dw3 = down_weight.reshape(3, 3 * chans, chans)
    all_rows = 9 * chans
    few = lax.axis_size(FEW)
    rest = lax.axis_size(REST)

    with jax.named_scope("halo"):
        slab = (2 * rows + 16, chans)
        (edges,) = call(
            pack_lon,
            [((2,) + slab, BF)],
            [((2, rows, 16, chans), BF), ((2, half, 16, chans), BF), (slab, F32)],
            n_in=2,
            hbm=(0, 1),
            sems=4,
        )(pinned(features), pinned(cotangent))
        lons = lax.axis_size(LON)
        from_west = lax.ppermute(edges, LON, [(i, (i + 1) % lons) for i in range(lons)])
        from_east = lax.ppermute(edges, LON, [(i, (i - 1) % lons) for i in range(lons)])
        feat, cot, w_in = call(
            fetch, [(features.shape, BF), (cotangent.shape, BF), (w3.shape, BF)], n_in=3, hbm=(0, 1, 2), sems=3
        )(pinned(features), pinned(cotangent), pinned(w3))
        strip = (2 * cols + pairs + 16, chans)
        to_near, to_far = call(
            pack_lat,
            [(strip, BF)] * 2,
            [(slab, F32), (slab, F32), ((2, 16, chans), F32)],
            n_in=5,
            smem=(0,),
        )(flags, feat, cot, from_west, from_east)
        near = lax.ppermute(to_near, LAT, [(i, i ^ 1) for i in range(lats)])
        gaps = range(1, lats - 1, 2)
        far = lax.ppermute(to_far, LAT, [(i, i + 1) for i in gaps] + [(i + 1, i) for i in gaps])

    plane = (rows + 2, J, chans)
    x_shape = (rows, pairs, 4 * chans)
    rim_shape = (2, pairs, 4 * chans)
    inner_plane = (rows - 2, J, chans)
    with jax.named_scope("conv"):
        x, rim, hq_in, he_in, vec = call(
            inner_kernel,
            [(x_shape, BF, True), ((4, J, 4 * chans), BF), (inner_plane, BF), (inner_plane, BF), ((2, chans), F32)],
            [
                ((rows, 2, cols + 56, 128), F32),
                ((2, 2, slab[0], 128), F32),
                ((rows, J, 5 * chans), BF),
            ],
            flops=2 * 960 * 2304 * 256,
            n_in=5,
            smem=(0,),
            sems=1,
        )(flags, feat, from_west, from_east, w_in)
        x_rim, hq, he, stat = call(
            functools.partial(outer_kernel, cols),
            [(rim_shape, BF, True), (plane, BF), (plane, BF), ((devices, 1, 128), F32)],
            [
                ((4, 2, cols + 56, 128), F32),
                ((2, 2, 16, 128), F32),
                ((4, J, 5 * chans), BF),
            ],
            flops=2 * 640 * 2304 * 256,
            n_in=8,
            smem=(0,),
            sems=2,
        )(flags, near, far, rim, hq_in, he_in, vec, w_in)
        stats = lax.all_to_all(stat, ALL, 0, 0, tiled=True)
    c_shape = (half + 2, J, 2 * chans)
    with jax.named_scope("back"):
        c2, h, aq, ae = call(
            back_kernel,
            [(c_shape, BF, True), ((2,) + plane, BF, True), (plane, BF), (plane, BF)],
            [((half + 2, pairs + 32, chans), F32), ((4,) + slab, F32), (c_shape, BF)],
            flops=2 * 400 * 2304 * 256,
            n_in=9,
            smem=(0,),
            sems=3,
        )(flags, cot, from_west, from_east, near, far, down_weight, hq, he)
    t_shape = (rows + 1, pairs, 3 * chans)
    with jax.named_scope("act"):
        t, pq, pe, coef, sums = call(
            functools.partial(act_kernel, cells),
            [(t_shape, BF, True), (plane, F32, True), (plane, F32, True), ((2, chans), F32), ((few, 4, 128), F32)],
            [((J, chans), F32), (t_shape, BF), ((2,) + plane, F32)],
            flops=1600 * 256 * 20,
            smem=(0,),
            n_in=8,
            sems=3 * rows + 5,
        )(flags, stats, hq, he, aq, ae, gain, bias)
        sums = lax.all_to_all(sums, FEW, 0, 0, tiled=True)
        (sums,) = call(merged_sums, [((rest, 4, 128), F32)], n_in=1)(sums)
        sums, c2 = lax.optimization_barrier((sums, c2))
        sums = lax.all_to_all(sums, REST, 0, 0, tiled=True)
    half_rows = (all_rows // 2, chans)
    with jax.named_scope("down"):
        output, down_keep, down_send = call(
            down_kernel,
            [((half, pairs, chans), BF), (half_rows, F32), (half_rows, BF)],
            [(t_shape, BF), (c_shape, BF), (dw3.shape, BF), ((all_rows, chans), F32)],
            flops=4 * 256 * 2304 * 256,
            smem=(0,),
            hbm=(1, 2, 3),
            n_in=4,
            sems=3,
        )(flags, pinned(t), pinned(c2), pinned(dw3))
        down_other = core_swap(down_send)
    h4_shape = (rows + 2, pairs, 4 * chans)
    with jax.named_scope("grad"):
        h4, conv_keep, conv_send, vec = call(
            functools.partial(grad_kernel, cells),
            [(h4_shape, BF, True), (half_rows, F32), (half_rows, BF), ((2, chans), F32)],
            [
                ((J, chans), F32),
                ((all_rows, chans), F32),
                (plane, F32),
                ((rows + 2, pairs, 4 * chans), BF),
                (h4_shape, BF),
            ],
            flops=2 * 1600 * 2304 * 256,
            smem=(0,),
            hbm=(6, 7, 8),
            n_in=9,
            sems=3 * (rows + 2) + 3,
        )(flags, sums, coef, gain, pq, h, pinned(pe), pinned(x), pinned(x_rim))
    with jax.named_scope("input"):
        (input_grad,) = call(
            input_kernel,
            [((rows, cols, chans), BF)],
            [((rows, 2, cols + 8, 128), F32), (h4_shape, BF), (conv_weight.shape, BF)],
            flops=2 * 1024 * 2304 * 256,
            n_in=2,
            hbm=(0, 1),
            sems=2,
        )(pinned(h4), pinned(conv_weight))
    with jax.named_scope("total"):
        whole_rows = (all_rows, chans)
        (mine,) = call(
            join_kernel, [(whole_rows, BF, True)], [(whole_rows, BF)], n_in=4, sems=4
        )(conv_keep, core_swap(conv_send), down_keep, down_other)
        chips = lax.axis_size(NEAR)
        share = all_rows // chips
        got = lax.all_to_all(mine.reshape(chips, share, chans), NEAR, 0, 0, tiled=True)
        got, input_grad = lax.optimization_barrier((got, input_grad))
        piece = jnp.sum(got.astype(F32), axis=0).astype(BF)
        got = lax.all_to_all(
            jnp.broadcast_to(piece[None], (lax.axis_size("z_hi"), share, chans)), "z_hi", 0, 0, tiled=True
        )
        piece = (jnp.sum(got.astype(F32), axis=0) * factor).astype(BF)
        whole = lax.all_to_all(jnp.broadcast_to(piece[None], (chips, share, chans)), NEAR, 0, 0, tiled=True)
        whole = whole.reshape(all_rows, chans)
        other = core_swap(whole)
        flat = (whole_rows, F32, True)
        room = [(whole_rows, F32)]
        conv_grad, down_grad = call(unpack_own, [flat, flat], room, smem=(0,), n_in=2, sems=12)(flags, whole)
        conv_grad, down_grad = call(
            unpack_other, [flat, flat], room, smem=(0,), hbm=(2, 3), n_in=4, sems=12, aliases={2: 0, 3: 1}
        )(flags, other, pinned(conv_grad), pinned(down_grad))
    shape = (3, 3, chans, chans)
    return output, input_grad, conv_grad.reshape(shape), down_grad.reshape(shape), vec[0], vec[1]


SIZES = {64: (4, 4, 2, 2), 2: (1, 1, 2, 1), 4: (2, 1, 2, 1), 8: (1, 2, 2, 2)}


def solution(mesh):
    lon, lat = mesh.devices.shape
    fine = Mesh(mesh.devices.reshape(SIZES[lon] + (lat // 2, 2)), ALL)
    band = P(LAT, LON, None)
    return jax.shard_map(
        local,
        mesh=fine,
        in_specs=(band, P(), P(), P(), P(), band),
        out_specs=(band, band, P(), P(), P(), P()),
        check_vma=False,
    )
```

```python
import functools
import math

import jax
import jax.numpy as jnp
from jax import lax
from jax.experimental import pallas as pl
from jax.experimental.pallas import tpu as pltpu
from jax.sharding import Mesh
from jax.sharding import PartitionSpec as P

EPS = 1e-05
WIDTH = 8
J = 80
LON = ("x", "z_hi", "z_lo", "y_hi")
LAT = ("y_lo", "core")
NEAR = ("x", "z_lo", "y_hi", "y_lo")
FEW = ("x", "core")
REST = ("z_hi", "z_lo", "y_hi", "y_lo")
ALL = LON + LAT
BF = jnp.bfloat16
F32 = jnp.float32


def call(body, outs, scratch=(), flops=0, smem=(), hbm=(), n_in=0, sems=0, aliases=None):
    spaces = [pltpu.SMEM if i in smem else pltpu.HBM if i in hbm else pltpu.VMEM for i in range(n_in)]
    out_spaces = [pltpu.HBM if len(o) > 2 else pltpu.VMEM for o in outs]
    return pl.pallas_call(
        body,
        out_shape=[pltpu.HBM(o[0], o[1]) if len(o) > 2 else jax.ShapeDtypeStruct(o[0], o[1]) for o in outs],
        in_specs=[pl.BlockSpec(memory_space=m) for m in spaces],
        out_specs=[pl.BlockSpec(memory_space=m) for m in out_spaces],
        scratch_shapes=[pltpu.VMEM(s, d) for s, d in scratch]
        + ([pltpu.SemaphoreType.DMA((sems,))] if sems else []),
        input_output_aliases=aliases or {},
        compiler_params=pltpu.CompilerParams(vmem_limit_bytes=24 * 1024 * 1024),
        cost_estimate=pl.CostEstimate(flops=flops, bytes_accessed=1 << 20, transcendentals=0),
    )


def pinned(value):
    return pltpu.with_memory_space_constraint(value, pltpu.HBM)


def dot(a, b):
    return jnp.dot(a, b, preferred_element_type=F32)


def dot_t(a, b):
    return lax.dot_general(a, b, (((1,), (1,)), ((), ())), preferred_element_type=F32)


def t_dot(a, b):
    return lax.dot_general(a, b, (((0,), (0,)), ((), ())), preferred_element_type=F32)


def spread_dot(table, *vectors):
    parts = []
    for v in vectors:
        high = v.astype(BF).astype(F32)
        mid = (v - high).astype(BF).astype(F32)
        parts += [high, mid, v - high - mid]
    parts.append(jnp.zeros((8 - len(parts), vectors[0].shape[1]), F32))
    out = dot(jnp.concatenate(parts, axis=0).astype(BF), table)
    return [out[3 * i : 3 * i + 1] + out[3 * i + 1 : 3 * i + 2] + out[3 * i + 2 : 3 * i + 3] for i in range(len(vectors))]


def table(n, m, row_width, col_width, shift):
    r = lax.broadcasted_iota(jnp.int32, (n, m), 0) // row_width
    c = lax.broadcasted_iota(jnp.int32, (n, m), 1) // col_width
    return jnp.where(r == c + shift, 1.0, 0.0).astype(BF)


def masks():
    j = lax.broadcasted_iota(jnp.int32, (J, 1), 0)
    odd = jnp.where((j >= 1) & (j <= 64), 1.0, 0.0)
    even = jnp.where(j <= 63, 1.0, 0.0)
    return odd, even


def pack_lon(feat_hbm, cot_hbm, out, feat, cot, f32s, sems):
    rows, cols, chans = feat_hbm.shape
    half, pairs, _ = cot_hbm.shape
    copies = []
    for k, (lo_f, lo_c) in enumerate(((cols - 16, pairs - 16), (0, 0))):
        copies.append(pltpu.make_async_copy(feat_hbm.at[:, lo_f : lo_f + 16], feat.at[k], sems.at[2 * k]))
        copies.append(pltpu.make_async_copy(cot_hbm.at[:, lo_c : lo_c + 16], cot.at[k], sems.at[2 * k + 1]))
    for copy in copies:
        copy.start()
    f32s[...] = jnp.zeros(f32s.shape, F32)
    for copy in copies:
        copy.wait()
    for k, (at_f, at_c) in enumerate(((14, 15), (0, 0))):
        for r in range(rows):
            f32s[2 * r : 2 * r + 2] = feat[k, r].astype(F32)[at_f : at_f + 2]
        for i in range(half):
            f32s[2 * rows + i : 2 * rows + i + 1] = cot[k, i].astype(F32)[at_c : at_c + 1]
        out[k] = f32s[...].astype(BF)


def fetch(feat_hbm, cot_hbm, w_hbm, feat, cot, w, sems):
    copies = [
        pltpu.make_async_copy(src, dst, sems.at[i])
        for i, (src, dst) in enumerate(((feat_hbm, feat), (cot_hbm, cot), (w_hbm, w)))
    ]
    for copy in copies:
        copy.start()
    for copy in copies:
        copy.wait()


def columns(flags, pair, next_pair, part=slice(None)):
    low = flags[3] == 0
    west = jnp.where(low, next_pair[0, :, part].astype(F32), pair[0, :, part].astype(F32))
    east = jnp.where(low, pair[1, :, part].astype(F32), next_pair[1, :, part].astype(F32))
    return west, east


def pack_lat(flags, feat, cot, pair, next_pair, near, far, w32, e32, corner):
    rows, cols, _ = feat.shape
    half, pairs, _ = cot.shape
    core = flags[2]
    for dest, last in ((near, 1 - core), (far, core)):
        top, mid = last * (rows - 2), last * (half - 1)
        for k in range(2):
            dest[k * cols : (k + 1) * cols] = feat[top + k]
        dest[2 * cols : 2 * cols + pairs] = cot[mid]
    w32[...], e32[...] = columns(flags, pair, next_pair)
    corner[...] = jnp.zeros(corner.shape, F32)
    for k, (top, mid) in enumerate(((rows - 2, half - 1), (0, 0))):
        corner[k, 0:4] = w32[2 * top : 2 * top + 4]
        corner[k, 4:8] = e32[2 * top : 2 * top + 4]
        corner[k, 8:9] = w32[2 * rows + mid : 2 * rows + mid + 1]
        corner[k, 9:10] = e32[2 * rows + mid : 2 * rows + mid + 1]
    o = 2 * cols + pairs
    near[o : o + 16] = corner[core].astype(BF)
    far[o : o + 16] = corner[1 - core].astype(BF)


def sides(flags, near, far):
    low = flags[2] == 0

    def north(lo, hi, part):
        return jnp.where(low, far[lo:hi, part].astype(F32), near[lo:hi, part].astype(F32))

    def south(lo, hi, part):
        return jnp.where(low, near[lo:hi, part].astype(F32), far[lo:hi, part].astype(F32))

    return north, south


def taps(f32s, x_out, rows, lanes):
    for r in range(rows):
        for v in range(2):
            for k in range(lanes):
                lane = k * 256 + v * 128
                x_out[r, :, lane : lane + 128] = f32s[r, v, pl.ds(14 + k, J, stride=2), :].astype(BF)


def moments(planes, cols):
    chans = planes[0][0].shape[2]
    sums = jnp.zeros((1, chans), F32)
    for (ref, rows), mask in zip(planes, masks()):
        part = jnp.zeros((J, chans), F32)
        for r in rows:
            part = part + ref[r].astype(F32)
        sums = sums + jnp.sum(part * mask, axis=0, keepdims=True)
    (total,) = spread_dot(table(chans, chans, WIDTH, WIDTH, 0), sums)
    mean = total / (len(planes[0][1]) * cols * WIDTH)
    squares = jnp.zeros((1, chans), F32)
    for (ref, rows), mask in zip(planes, masks()):
        part = jnp.zeros((J, chans), F32)
        for r in rows:
            d = ref[r].astype(F32) - mean
            part = part + d * d
        squares = squares + jnp.sum(part * mask, axis=0, keepdims=True)
    return sums, squares


def inner_kernel(
    flags, feat, pair, next_pair, w, x_hbm, rim, hq_out, he_out, vec_out, f32s, edge, x_out, sems
):
    rows, cols, chans = feat.shape
    pairs = cols // 2
    f32s[:, :, 16 + cols : 56 + cols] = jnp.zeros((rows, 2, 40, 128), F32)
    for v in range(2):
        part = slice(v * 128, v * 128 + 128)
        edge[0, v], edge[1, v] = columns(flags, pair, next_pair, part)
        for r in range(rows):
            f32s[r, v, 14:16] = edge[0, v, 2 * r : 2 * r + 2]
            f32s[r, v, 16 + cols : 18 + cols] = edge[1, v, 2 * r : 2 * r + 2]
    for v in range(2):
        f32s[:, v, 16 : 16 + cols] = feat[:, :, v * 128 : v * 128 + 128].astype(F32)
    taps(f32s, x_out, rows, 5)
    keep = pltpu.make_async_copy(x_out.at[:, 0:pairs, chans : 5 * chans], x_hbm, sems.at[0])
    keep.start()
    for i, r in enumerate((0, 1, rows - 2, rows - 1)):
        rim[i] = x_out[r, :, 0 : 4 * chans]
    n = rows - 2
    for out, lo in ((hq_out, 0), (he_out, chans)):
        acc = None
        for a in range(3):
            lhs = x_out[a : a + n, :, lo : lo + 3 * chans].reshape(n * J, 3 * chans)
            term = dot(lhs, w[a])
            acc = term if acc is None else acc + term
        out[...] = acc.astype(BF).reshape(n, J, chans)
    sums, squares = moments(((hq_out, range(n)), (he_out, range(n))), cols)
    vec_out[0:1] = sums
    vec_out[1:2] = squares
    keep.wait()


def outer_kernel(
    cols, flags, near, far, rim, hq_in, he_in, vec, w, x_hbm, hq_out, he_out, stat_out, f32s, edge, x_out, sems
):
    rows = hq_in.shape[0] + 2
    chans = hq_in.shape[2]
    pairs = cols // 2
    f32s[:, :, 16 + cols : 56 + cols] = jnp.zeros((4, 2, 40, 128), F32)
    for v in range(2):
        part = slice(v * 128, v * 128 + 128)
        for k, side in enumerate(sides(flags, near, far)):
            edge[k, v] = side(2 * cols + pairs, 2 * cols + pairs + 16, part)
            for q in range(2):
                row = q + 2 * k
                f32s[row, v, 16 : 16 + cols] = side(q * cols, (q + 1) * cols, part)
                f32s[row, v, 14:16] = edge[k, v, 2 * q : 2 * q + 2]
                f32s[row, v, 16 + cols : 18 + cols] = edge[k, v, 4 + 2 * q : 6 + 2 * q]
    taps(f32s, x_out, 4, 5)
    copies = []
    for i, r in enumerate((1, 2)):
        copies.append(pltpu.make_async_copy(x_out.at[r, 0:pairs, chans : 5 * chans], x_hbm.at[i], sems.at[i]))
        copies[-1].start()
    hq_out[2:rows] = hq_in[...]
    he_out[2:rows] = he_in[...]
    wanted = (
        ((x_out, 0), (x_out, 1), (rim, 2), (rim, 3)),
        ((x_out, 1), (rim, 0), (rim, 3), (x_out, 2)),
        ((rim, 0), (rim, 1), (x_out, 2), (x_out, 3)),
    )
    for k, out in enumerate((hq_out, he_out)):
        lo = k * chans
        acc = None
        for a in range(3):
            lhs = jnp.concatenate([ref[r, :, lo : lo + 3 * chans] for ref, r in wanted[a]], axis=0)
            term = dot(lhs, w[a])
            acc = term if acc is None else acc + term
        value = acc.astype(BF).reshape(4, J, chans)
        out[0:2] = value[0:2]
        out[rows : rows + 2] = value[2:4]
    edges = (1, rows)
    sums, squares = moments(((hq_out, edges), (he_out, edges)), cols)
    n_in = (rows - 2) * cols * WIDTH
    n_out = 2 * cols * WIDTH
    n = n_in + n_out
    gap = vec[0:1] / n_in - sums / n_out
    (means,) = spread_dot(table(chans, 128, WIDTH, 1, 0), vec[0:1] + sums)
    within, gaps = spread_dot(table(chans, 128, WIDTH, 1, -32), vec[1:2] + squares, gap)
    stat = means / n + within + (n_in * n_out / n) * gaps * gaps
    stat_out[...] = jnp.broadcast_to(stat[None], stat_out.shape)
    for copy in copies:
        copy.wait()


def merged_sums(rec, out):
    out[...] = jnp.broadcast_to(jnp.sum(rec[...], axis=0)[None], out.shape)


def back_kernel(flags, cot, pair, next_pair, near, far, dw, hq, he, c_hbm, h_hbm, aq_out, ae_out, f32s, edge, c_out, sems):
    keep_h = [pltpu.make_async_copy(h, h_hbm.at[k], sems.at[1 + k]) for k, h in enumerate((hq, he))]
    for copy in keep_h:
        copy.start()
    half, pairs, chans = cot.shape
    rows = 2 * half
    cols = 2 * pairs
    f32s[:, 16 + pairs :] = jnp.zeros((half + 2, 16, chans), F32)
    edge[0], edge[1] = columns(flags, pair, next_pair)
    every = slice(None)
    for k, side in enumerate(sides(flags, near, far)):
        row = k * (half + 1)
        f32s[row, 16 : 16 + pairs] = side(2 * cols, 2 * cols + pairs, every)
        edge[2 + k, 0:16] = side(2 * cols + pairs, 2 * cols + pairs + 16, every)
        f32s[row, 15:16] = edge[2 + k, 8:9]
        f32s[row, 16 + pairs : 17 + pairs] = edge[2 + k, 9:10]
    f32s[1 : half + 1, 16 : 16 + pairs] = cot[...].astype(F32)
    for i in range(half):
        f32s[1 + i, 15:16] = edge[0, 2 * rows + i : 2 * rows + i + 1]
        f32s[1 + i, 16 + pairs : 17 + pairs] = edge[1, 2 * rows + i : 2 * rows + i + 1]
    for s in range(half + 2):
        c_out[s, :, 0:chans] = f32s[s, 15 : 15 + J].astype(BF)
        c_out[s, :, chans : 2 * chans] = f32s[s, 16 : 16 + J].astype(BF)
    keep = pltpu.make_async_copy(c_out, c_hbm, sems.at[0])
    keep.start()
    n = half + 1
    lo_l = c_out[0:n, :, 0:chans].reshape(n * J, chans)
    lo_r = c_out[0:n, :, chans:].reshape(n * J, chans)
    hi_l = c_out[1 : n + 1, :, 0:chans].reshape(n * J, chans)
    hi_r = c_out[1 : n + 1, :, chans:].reshape(n * J, chans)

    def put(out, k, value):
        value = value.astype(BF).reshape(n, J, chans)
        for i in range(n):
            out[2 * i + k] = value[i]

    put(ae_out, 1, dot_t(hi_r, dw[1, 1]))
    put(aq_out, 1, dot_t(hi_r, dw[1, 0]) + dot_t(hi_l, dw[1, 2]))
    put(ae_out, 0, dot_t(hi_r, dw[0, 1]) + dot_t(lo_r, dw[2, 1]))
    put(
        aq_out,
        0,
        dot_t(hi_r, dw[0, 0]) + dot_t(hi_l, dw[0, 2]) + dot_t(lo_r, dw[2, 0]) + dot_t(lo_l, dw[2, 2]),
    )
    keep.wait()
    for copy in keep_h:
        copy.wait()


def act_kernel(cells, flags, stats, hq, he, aq, ae, gain, bias, t_hbm, pq_hbm, pe_hbm, coef_out, sum_out, f32s, t_out, p_out, sems):
    devices = stats.shape[0]
    rows = hq.shape[0] - 2
    chans = hq.shape[2]
    count = float(cells * WIDTH)
    local_n = count / devices
    rec = stats[...]
    total = jnp.sum(rec, axis=0)
    centre = total / devices
    dev = rec - centre[None]
    between = jnp.sum(dev * dev, axis=0)
    mean, gaps = spread_dot(table(128, chans, 1, WIDTH, 0), centre, between)
    (within,) = spread_dot(table(128, chans, 1, WIDTH, 32), total)
    var = (within + local_n * gaps) / count
    inverse = lax.rsqrt(var + EPS)
    coef_out[0:1] = mean
    coef_out[1:2] = inverse
    g = gain[...]
    b = bias[...]
    odd, even = masks()
    top = jnp.where(flags[0] == 1, 0.0, 1.0)
    bias_sum = jnp.zeros((1, chans), F32)
    gain_sum = jnp.zeros((1, chans), F32)
    copies = []
    accs = [[jnp.zeros((J, chans), F32)] * 2 for _ in range(2)]
    for r in range(rows + 2):
        for k, (h, a) in enumerate(((hq, aq), (he, ae))):
            is_q = k == 0
            normed = (h[r].astype(F32) - mean) * inverse
            shifted = g * normed + b
            sigma = 0.5 + 0.5 * jnp.tanh(0.5 * shifted)
            pre = a[r].astype(F32) * sigma * (1.0 + shifted * (1.0 - sigma))
            p_out[k, r] = pre
            dest = pq_hbm if is_q else pe_hbm
            copies.append(pltpu.make_async_copy(p_out.at[k, r], dest.at[r], sems.at[len(copies)]))
            copies[-1].start()
            if 1 <= r <= rows:
                accs[k] = [accs[k][0] + pre, accs[k][1] + pre * normed]
            if r <= rows:
                active = shifted * sigma
                if r == 0:
                    active = active * top
                if is_q:
                    f32s[...] = active.astype(BF).astype(F32)
                    t_out[r, :, 0:chans] = active[0:64].astype(BF)
                    t_out[r, :, 2 * chans :] = f32s[1:65].astype(BF)
                else:
                    t_out[r, :, chans : 2 * chans] = active[0:64].astype(BF)
                    copies.append(pltpu.make_async_copy(t_out.at[r], t_hbm.at[r], sems.at[len(copies)]))
                    copies[-1].start()
    for (acc_b, acc_g), mask in zip(accs, (odd, even)):
        bias_sum = bias_sum + jnp.sum(acc_b * mask, axis=0, keepdims=True)
        gain_sum = gain_sum + jnp.sum(acc_g * mask, axis=0, keepdims=True)
    payload = jnp.concatenate(
        [bias_sum[:, 0:128], bias_sum[:, 128:256], gain_sum[:, 0:128], gain_sum[:, 128:256]], axis=0
    )
    sum_out[...] = jnp.broadcast_to(payload[None], sum_out.shape)
    for copy in copies:
        copy.wait()


def halves(flags, full, keep, send):
    n = keep.shape[0]
    core = flags[2]
    keep[...] = full[pl.ds(pl.multiple_of(core * n, n), n)]
    send[...] = full[pl.ds(pl.multiple_of((1 - core) * n, n), n)].astype(BF)


def down_kernel(flags, t_hbm, c_hbm, dw_hbm, out, keep, send, t, c, dw, grad, sems):
    half = out.shape[0]
    pairs, chans = out.shape[1:]
    sources = ((t_hbm, t), (c_hbm, c), (dw_hbm, dw))
    loads = [pltpu.make_async_copy(src, dst, sems.at[i]) for i, (src, dst) in enumerate(sources)]
    for load in loads:
        load.start()
    for load in loads:
        load.wait()
    cot = c[1 : half + 1, 0:pairs, chans:].reshape(half * pairs, chans)
    acc = None
    for a in range(3):
        lhs = jnp.concatenate([t[2 * i + a] for i in range(half)], axis=0)
        term = dot(lhs, dw[a])
        acc = term if acc is None else acc + term
        grad[a * 3 * chans : (a + 1) * 3 * chans] = t_dot(lhs, cot)
    out[...] = acc.astype(BF).reshape(out.shape)
    halves(flags, grad, keep, send)


def grad_kernel(
    cells, flags, sums, coef, gain, pq, h_in, pe_hbm, x_hbm, rim_hbm, h4_hbm, keep, send, vec_out, f32s, conv_out, pe, x, h4_out, sems
):
    rows = pq.shape[0] - 2
    chans = pq.shape[2]
    loads = []
    loads.append(pltpu.make_async_copy(pe_hbm, pe, sems.at[0]))
    loads[0].start()
    load_x = []
    for src, dst in ((x_hbm, x.at[1 : rows + 1]), (rim_hbm.at[0], x.at[0]), (rim_hbm.at[1], x.at[rows + 1])):
        load_x.append(pltpu.make_async_copy(src, dst, sems.at[len(loads) + len(load_x)]))
        load_x[-1].start()
    first_out = len(loads) + len(load_x)
    copies = []
    count = float(cells * WIDTH)
    total = jnp.sum(sums[...], axis=0)
    bias_sum = jnp.concatenate([total[0:1], total[1:2]], axis=1)
    gain_sum = jnp.concatenate([total[2:3], total[3:4]], axis=1)
    factor = 1.0 / math.sqrt(cells)
    vec_out[0:1] = gain_sum * factor
    vec_out[1:2] = bias_sum * factor
    g = gain[...]
    first, second = spread_dot(table(chans, chans, WIDTH, WIDTH, 0), g * bias_sum, g * gain_sum)
    first = first / count
    second = second / count
    mean = coef[0:1]
    inverse = coef[1:2]
    top = jnp.where(flags[0] == 1, 0.0, 1.0)
    bottom = jnp.where(flags[1] == 1, 0.0, 1.0)
    for k in range(2):
        is_q = k == 0
        p_in = pq if is_q else pe
        if not is_q:
            loads[0].wait()
        for r in range(rows + 2):
            normed = (h_in[k, r].astype(F32) - mean) * inverse
            value = inverse * (g * p_in[r] - first - normed * second)
            if r == 0:
                value = value * top
            if r == rows + 1:
                value = value * bottom
            rounded = value.astype(BF)
            f32s[...] = rounded.astype(F32)
            moved = f32s[1:65].astype(BF)
            lo = 3 if is_q else 2
            h4_out[r, :, lo * chans : (lo + 1) * chans] = rounded[0:64]
            lo = 1 if is_q else 0
            h4_out[r, :, lo * chans : (lo + 1) * chans] = moved
            if not is_q:
                copies.append(pltpu.make_async_copy(h4_out.at[r], h4_hbm.at[r], sems.at[first_out + r]))
                copies[-1].start()
    for load in load_x:
        load.wait()
    pairs = h4_out.shape[1]
    cells_here = rows * pairs
    odd = h4_out[1 : rows + 1, :, chans : 2 * chans].reshape(cells_here, chans)
    even = h4_out[1 : rows + 1, :, 2 * chans : 3 * chans].reshape(cells_here, chans)
    for a in range(3):
        lhs = x[a : a + rows].reshape(cells_here, 4 * chans)
        part = t_dot(lhs[:, 0 : 3 * chans], even) + t_dot(lhs[:, chans : 4 * chans], odd)
        conv_out[a * 3 * chans : (a + 1) * 3 * chans] = part
    halves(flags, conv_out, keep, send)
    for copy in copies:
        copy.wait()


def input_kernel(h4_hbm, w_hbm, out, f32s, h4, w, sems):
    rows, cols, chans = out.shape
    loads = [pltpu.make_async_copy(h4_hbm, h4, sems.at[0]), pltpu.make_async_copy(w_hbm, w, sems.at[1])]
    for load in loads:
        load.start()
    for load in loads:
        load.wait()
    for k, lo in ((0, 1), (1, 0)):
        acc = None
        for a in range(3):
            for b in range(3):
                lane = (lo + b) * chans
                lhs = h4[2 - a : 2 - a + rows, :, lane : lane + chans].reshape(rows * (cols // 2), chans)
                term = dot_t(lhs, w[a, b])
                acc = term if acc is None else acc + term
        acc = acc.reshape(rows, cols // 2, chans)
        for r in range(rows):
            for v in range(2):
                f32s[r, v, pl.ds(k, cols // 2, stride=2), :] = acc[r, :, v * 128 : v * 128 + 128]
    for v in range(2):
        out[:, :, v * 128 : v * 128 + 128] = f32s[:, v, 0:cols].astype(BF)


def join_rows(keep, other, out, both, sems, base):
    n = keep.shape[0]
    step = n // 2
    copies = []
    for q in range(2):
        part = slice(q * step, (q + 1) * step)
        both[part] = (keep[part] + other[part].astype(F32)).astype(BF)
        copies.append(pltpu.make_async_copy(both.at[part], out.at[base + q * step : base + (q + 1) * step], sems.at[q]))
        copies[-1].start()
    for copy in copies:
        copy.wait()


def join_down(keep, other, out, both, sems):
    join_rows(keep, other, out, both, sems, keep.shape[0])


def join_conv(keep, other, out_in, out, both, sems):
    join_rows(keep, other, out, both, sems, 0)


def unpack_rows(core, rows, conv, down, f32s, sems):
    n = rows.shape[0] // 2
    step = n // 6
    base = pl.multiple_of(core * n, n)
    copies = []
    for k, dst in enumerate((conv, down)):
        for q in range(6):
            o = k * n + q * step
            f32s[o : o + step] = rows[o : o + step].astype(F32)
            part = dst.at[pl.ds(base + q * step, step)]
            copies.append(pltpu.make_async_copy(f32s.at[o : o + step], part, sems.at[k * 6 + q]))
            copies[-1].start()
    for copy in copies:
        copy.wait()


def unpack_own(flags, rows, conv, down, f32s, sems):
    unpack_rows(flags[2], rows, conv, down, f32s, sems)


def unpack_other(flags, rows, conv_in, down_in, conv, down, f32s, sems):
    unpack_rows(1 - flags[2], rows, conv, down, f32s, sems)


def core_swap(value):
    return lax.ppermute(value, "core", [(0, 1), (1, 0)])


def local(features, conv_weight, down_weight, norm_gain, norm_bias, cotangent):
    rows, cols, chans = features.shape
    half, pairs, _ = cotangent.shape
    devices = lax.axis_size(ALL)
    lats = lax.axis_size(LAT)
    cells = rows * cols * devices
    factor = 1.0 / math.sqrt(cells)
    lat = lax.axis_index(LAT)
    odd = lax.axis_index(LON) % 2 == 1
    flags = jnp.stack([lat == 0, lat == lats - 1, lax.axis_index("core") == 1, odd]).astype(jnp.int32)
    gain = norm_gain.reshape(1, chans)
    bias = norm_bias.reshape(1, chans)
    w3 = conv_weight.reshape(3, 3 * chans, chans)
    dw3 = down_weight.reshape(3, 3 * chans, chans)
    all_rows = 9 * chans
    few = lax.axis_size(FEW)
    rest = lax.axis_size(REST)

    with jax.named_scope("halo"):
        slab = (2 * rows + 16, chans)
        (edges,) = call(
            pack_lon,
            [((2,) + slab, BF)],
            [((2, rows, 16, chans), BF), ((2, half, 16, chans), BF), (slab, F32)],
            n_in=2,
            hbm=(0, 1),
            sems=4,
        )(pinned(features), pinned(cotangent))
        lons = lax.axis_size(LON)
        pair = lax.ppermute(edges, LON, [(i, i ^ 1) for i in range(lons)])
        next_pair = lax.ppermute(edges, LON, [(i, (i + 2 * (i % 2) - 1) % lons) for i in range(lons)])
        feat, cot, w_in = call(
            fetch, [(features.shape, BF), (cotangent.shape, BF), (w3.shape, BF)], n_in=3, hbm=(0, 1, 2), sems=3
        )(pinned(features), pinned(cotangent), pinned(w3))
        strip = (2 * cols + pairs + 16, chans)
        to_near, to_far = call(
            pack_lat,
            [(strip, BF)] * 2,
            [(slab, F32), (slab, F32), ((2, 16, chans), F32)],
            n_in=5,
            smem=(0,),
        )(flags, feat, cot, pair, next_pair)
        near = lax.ppermute(to_near, LAT, [(i, i ^ 1) for i in range(lats)])
        gaps = range(1, lats - 1, 2)
        far = lax.ppermute(to_far, LAT, [(i, i + 1) for i in gaps] + [(i + 1, i) for i in gaps])

    plane = (rows + 2, J, chans)
    x_shape = (rows, pairs, 4 * chans)
    rim_shape = (2, pairs, 4 * chans)
    inner_plane = (rows - 2, J, chans)
    with jax.named_scope("conv"):
        x, rim, hq_in, he_in, vec = call(
            inner_kernel,
            [(x_shape, BF, True), ((4, J, 4 * chans), BF), (inner_plane, BF), (inner_plane, BF), ((2, chans), F32)],
            [
                ((rows, 2, cols + 56, 128), F32),
                ((2, 2, slab[0], 128), F32),
                ((rows, J, 5 * chans), BF),
            ],
            flops=2 * 960 * 2304 * 256,
            n_in=5,
            smem=(0,),
            sems=1,
        )(flags, feat, pair, next_pair, w_in)
        x_rim, hq, he, stat = call(
            functools.partial(outer_kernel, cols),
            [(rim_shape, BF, True), (plane, BF), (plane, BF), ((devices, 1, 128), F32)],
            [
                ((4, 2, cols + 56, 128), F32),
                ((2, 2, 16, 128), F32),
                ((4, J, 5 * chans), BF),
            ],
            flops=2 * 640 * 2304 * 256,
            n_in=8,
            smem=(0,),
            sems=2,
        )(flags, near, far, rim, hq_in, he_in, vec, w_in)
        stats = lax.all_to_all(stat, ALL, 0, 0, tiled=True)
    c_shape = (half + 2, J, 2 * chans)
    with jax.named_scope("back"):
        c2, h, aq, ae = call(
            back_kernel,
            [(c_shape, BF, True), ((2,) + plane, BF, True), (plane, BF), (plane, BF)],
            [((half + 2, pairs + 32, chans), F32), ((4,) + slab, F32), (c_shape, BF)],
            flops=2 * 400 * 2304 * 256,
            n_in=9,
            smem=(0,),
            sems=3,
        )(flags, cot, pair, next_pair, near, far, down_weight, hq, he)
    t_shape = (rows + 1, pairs, 3 * chans)
    with jax.named_scope("act"):
        t, pq, pe, coef, sums = call(
            functools.partial(act_kernel, cells),
            [(t_shape, BF, True), (plane, F32, True), (plane, F32, True), ((2, chans), F32), ((few, 4, 128), F32)],
            [((J, chans), F32), (t_shape, BF), ((2,) + plane, F32)],
            flops=1600 * 256 * 20,
            smem=(0,),
            n_in=8,
            sems=3 * rows + 5,
        )(flags, stats, hq, he, aq, ae, gain, bias)
        sums = lax.all_to_all(sums, FEW, 0, 0, tiled=True)
        (sums,) = call(merged_sums, [((rest, 4, 128), F32)], n_in=1)(sums)
        sums, c2 = lax.optimization_barrier((sums, c2))
        sums = lax.all_to_all(sums, REST, 0, 0, tiled=True)
    half_rows = (all_rows // 2, chans)
    with jax.named_scope("down"):
        output, down_keep, down_send = call(
            down_kernel,
            [((half, pairs, chans), BF), (half_rows, F32), (half_rows, BF)],
            [(t_shape, BF), (c_shape, BF), (dw3.shape, BF), ((all_rows, chans), F32)],
            flops=4 * 256 * 2304 * 256,
            smem=(0,),
            hbm=(1, 2, 3),
            n_in=4,
            sems=3,
        )(flags, pinned(t), pinned(c2), pinned(dw3))
        down_other = core_swap(down_send)
    h4_shape = (rows + 2, pairs, 4 * chans)
    with jax.named_scope("grad"):
        h4, conv_keep, conv_send, vec = call(
            functools.partial(grad_kernel, cells),
            [(h4_shape, BF, True), (half_rows, F32), (half_rows, BF), ((2, chans), F32)],
            [
                ((J, chans), F32),
                ((all_rows, chans), F32),
                (plane, F32),
                ((rows + 2, pairs, 4 * chans), BF),
                (h4_shape, BF),
            ],
            flops=2 * 1600 * 2304 * 256,
            smem=(0,),
            hbm=(6, 7, 8),
            n_in=9,
            sems=3 * (rows + 2) + 3,
        )(flags, sums, coef, gain, pq, h, pinned(pe), pinned(x), pinned(x_rim))
    with jax.named_scope("input"):
        (input_grad,) = call(
            input_kernel,
            [((rows, cols, chans), BF)],
            [((rows, 2, cols + 8, 128), F32), (h4_shape, BF), (conv_weight.shape, BF)],
            flops=2 * 1024 * 2304 * 256,
            n_in=2,
            hbm=(0, 1),
            sems=2,
        )(pinned(h4), pinned(conv_weight))
    with jax.named_scope("total"):
        whole_rows = (all_rows, chans)
        mine_out, room = [(whole_rows, BF, True)], [(half_rows, BF)]
        conv_other = core_swap(conv_send)
        (mine,) = call(join_down, mine_out, room, n_in=2, sems=2)(down_keep, down_other)
        (mine,) = call(join_conv, mine_out, room, n_in=3, hbm=(2,), sems=2, aliases={2: 0})(
            conv_keep, conv_other, pinned(mine)
        )
        chips = lax.axis_size(NEAR)
        share = all_rows // chips
        got = lax.all_to_all(mine.reshape(chips, share, chans), NEAR, 0, 0, tiled=True)
        got, input_grad = lax.optimization_barrier((got, input_grad))
        piece = jnp.sum(got.astype(F32), axis=0).astype(BF)
        got = lax.all_to_all(
            jnp.broadcast_to(piece[None], (lax.axis_size("z_hi"), share, chans)), "z_hi", 0, 0, tiled=True
        )
        piece = (jnp.sum(got.astype(F32), axis=0) * factor).astype(BF)
        whole = lax.all_to_all(jnp.broadcast_to(piece[None], (chips, share, chans)), NEAR, 0, 0, tiled=True)
        whole = whole.reshape(all_rows, chans)
        other = core_swap(whole)
        flat = (whole_rows, F32, True)
        room = [(whole_rows, F32)]
        conv_grad, down_grad = call(unpack_own, [flat, flat], room, smem=(0,), n_in=2, sems=12)(flags, whole)
        conv_grad, down_grad = call(
            unpack_other, [flat, flat], room, smem=(0,), hbm=(2, 3), n_in=4, sems=12, aliases={2: 0, 3: 1}
        )(flags, other, pinned(conv_grad), pinned(down_grad))
    shape = (3, 3, chans, chans)
    return output, input_grad, conv_grad.reshape(shape), down_grad.reshape(shape), vec[0], vec[1]


SIZES = {64: (4, 4, 2, 2), 2: (1, 1, 2, 1), 4: (2, 1, 2, 1), 8: (1, 2, 2, 2)}


def solution(mesh):
    lon, lat = mesh.devices.shape
    fine = Mesh(mesh.devices.reshape(SIZES[lon] + (lat // 2, 2)), ALL)
    band = P(LAT, LON, None)
    return jax.shard_map(
        local,
        mesh=fine,
        in_specs=(band, P(), P(), P(), P(), band),
        out_specs=(band, band, P(), P(), P(), P()),
        check_vma=False,
    )
```

```python
import functools
import math

import jax
import jax.numpy as jnp
from jax import lax
from jax.experimental import pallas as pl
from jax.experimental.pallas import tpu as pltpu
from jax.sharding import Mesh
from jax.sharding import PartitionSpec as P

EPS = 1e-05
WIDTH = 8
J = 80
LON = ("x", "z_hi", "z_lo", "y_hi")
LAT = ("y_lo", "core")
NEAR = ("x", "z_lo", "y_hi", "y_lo")
FEW = ("z_hi", "z_lo", "core")
REST = ("x", "y_hi", "y_lo")
ALL = LON + LAT
BF = jnp.bfloat16
F32 = jnp.float32


def call(body, outs, scratch=(), flops=0, smem=(), hbm=(), n_in=0, sems=0, aliases=None):
    spaces = [pltpu.SMEM if i in smem else pltpu.HBM if i in hbm else pltpu.VMEM for i in range(n_in)]
    out_spaces = [pltpu.HBM if len(o) > 2 else pltpu.VMEM for o in outs]
    return pl.pallas_call(
        body,
        out_shape=[pltpu.HBM(o[0], o[1]) if len(o) > 2 else jax.ShapeDtypeStruct(o[0], o[1]) for o in outs],
        in_specs=[pl.BlockSpec(memory_space=m) for m in spaces],
        out_specs=[pl.BlockSpec(memory_space=m) for m in out_spaces],
        scratch_shapes=[pltpu.VMEM(s, d) for s, d in scratch]
        + ([pltpu.SemaphoreType.DMA((sems,))] if sems else []),
        input_output_aliases=aliases or {},
        compiler_params=pltpu.CompilerParams(vmem_limit_bytes=24 * 1024 * 1024),
        cost_estimate=pl.CostEstimate(flops=flops, bytes_accessed=1 << 20, transcendentals=0),
    )


def pinned(value):
    return pltpu.with_memory_space_constraint(value, pltpu.HBM)


def dot(a, b):
    return jnp.dot(a, b, preferred_element_type=F32)


def dot_t(a, b):
    return lax.dot_general(a, b, (((1,), (1,)), ((), ())), preferred_element_type=F32)


def t_dot(a, b):
    return lax.dot_general(a, b, (((0,), (0,)), ((), ())), preferred_element_type=F32)


def spread_dot(table, *vectors):
    parts = []
    for v in vectors:
        high = v.astype(BF).astype(F32)
        mid = (v - high).astype(BF).astype(F32)
        parts += [high, mid, v - high - mid]
    parts.append(jnp.zeros((8 - len(parts), vectors[0].shape[1]), F32))
    out = dot(jnp.concatenate(parts, axis=0).astype(BF), table)
    return [out[3 * i : 3 * i + 1] + out[3 * i + 1 : 3 * i + 2] + out[3 * i + 2 : 3 * i + 3] for i in range(len(vectors))]


def table(n, m, row_width, col_width, shift):
    r = lax.broadcasted_iota(jnp.int32, (n, m), 0) // row_width
    c = lax.broadcasted_iota(jnp.int32, (n, m), 1) // col_width
    return jnp.where(r == c + shift, 1.0, 0.0).astype(BF)


def masks():
    j = lax.broadcasted_iota(jnp.int32, (J, 1), 0)
    odd = jnp.where((j >= 1) & (j <= 64), 1.0, 0.0)
    even = jnp.where(j <= 63, 1.0, 0.0)
    return odd, even


def pack_lon(feat_hbm, cot_hbm, out, feat, cot, f32s, sems):
    rows, cols, chans = feat_hbm.shape
    half, pairs, _ = cot_hbm.shape
    copies = []
    for k, (lo_f, lo_c) in enumerate(((cols - 16, pairs - 16), (0, 0))):
        copies.append(pltpu.make_async_copy(feat_hbm.at[:, lo_f : lo_f + 16], feat.at[k], sems.at[2 * k]))
        copies.append(pltpu.make_async_copy(cot_hbm.at[:, lo_c : lo_c + 16], cot.at[k], sems.at[2 * k + 1]))
    for copy in copies:
        copy.start()
    f32s[...] = jnp.zeros(f32s.shape, F32)
    for copy in copies:
        copy.wait()
    for k, (at_f, at_c) in enumerate(((14, 15), (0, 0))):
        for r in range(rows):
            f32s[2 * r : 2 * r + 2] = feat[k, r].astype(F32)[at_f : at_f + 2]
        for i in range(half):
            f32s[2 * rows + i : 2 * rows + i + 1] = cot[k, i].astype(F32)[at_c : at_c + 1]
        out[k] = f32s[...].astype(BF)


def fetch(feat_hbm, cot_hbm, w_hbm, feat, cot, w, sems):
    copies = [
        pltpu.make_async_copy(src, dst, sems.at[i])
        for i, (src, dst) in enumerate(((feat_hbm, feat), (cot_hbm, cot), (w_hbm, w)))
    ]
    for copy in copies:
        copy.start()
    for copy in copies:
        copy.wait()


def columns(flags, pair, next_pair, part=slice(None)):
    low = flags[3] == 0
    west = jnp.where(low, next_pair[0, :, part].astype(F32), pair[0, :, part].astype(F32))
    east = jnp.where(low, pair[1, :, part].astype(F32), next_pair[1, :, part].astype(F32))
    return west, east


def pack_lat(flags, feat, cot, pair, next_pair, near, far, w32, e32, corner):
    rows, cols, _ = feat.shape
    half, pairs, _ = cot.shape
    core = flags[2]
    for dest, last in ((near, 1 - core), (far, core)):
        top, mid = last * (rows - 2), last * (half - 1)
        for k in range(2):
            dest[k * cols : (k + 1) * cols] = feat[top + k]
        dest[2 * cols : 2 * cols + pairs] = cot[mid]
    w32[...], e32[...] = columns(flags, pair, next_pair)
    corner[...] = jnp.zeros(corner.shape, F32)
    for k, (top, mid) in enumerate(((rows - 2, half - 1), (0, 0))):
        corner[k, 0:4] = w32[2 * top : 2 * top + 4]
        corner[k, 4:8] = e32[2 * top : 2 * top + 4]
        corner[k, 8:9] = w32[2 * rows + mid : 2 * rows + mid + 1]
        corner[k, 9:10] = e32[2 * rows + mid : 2 * rows + mid + 1]
    o = 2 * cols + pairs
    near[o : o + 16] = corner[core].astype(BF)
    far[o : o + 16] = corner[1 - core].astype(BF)


def sides(flags, near, far):
    low = flags[2] == 0

    def north(lo, hi, part):
        return jnp.where(low, far[lo:hi, part].astype(F32), near[lo:hi, part].astype(F32))

    def south(lo, hi, part):
        return jnp.where(low, near[lo:hi, part].astype(F32), far[lo:hi, part].astype(F32))

    return north, south


def taps(f32s, x_out, rows, lanes):
    for r in range(rows):
        for v in range(2):
            for k in range(lanes):
                lane = k * 256 + v * 128
                x_out[r, :, lane : lane + 128] = f32s[r, v, pl.ds(14 + k, J, stride=2), :].astype(BF)


def moments(planes, cols):
    chans = planes[0][0].shape[2]
    sums = jnp.zeros((1, chans), F32)
    for (ref, rows), mask in zip(planes, masks()):
        part = jnp.zeros((J, chans), F32)
        for r in rows:
            part = part + ref[r].astype(F32)
        sums = sums + jnp.sum(part * mask, axis=0, keepdims=True)
    (total,) = spread_dot(table(chans, chans, WIDTH, WIDTH, 0), sums)
    mean = total / (len(planes[0][1]) * cols * WIDTH)
    squares = jnp.zeros((1, chans), F32)
    for (ref, rows), mask in zip(planes, masks()):
        part = jnp.zeros((J, chans), F32)
        for r in rows:
            d = ref[r].astype(F32) - mean
            part = part + d * d
        squares = squares + jnp.sum(part * mask, axis=0, keepdims=True)
    return sums, squares


def inner_kernel(
    flags, feat, pair, next_pair, w, x_hbm, rim, hq_out, he_out, vec_out, f32s, edge, x_out, sems
):
    rows, cols, chans = feat.shape
    pairs = cols // 2
    f32s[:, :, 16 + cols : 56 + cols] = jnp.zeros((rows, 2, 40, 128), F32)
    for v in range(2):
        part = slice(v * 128, v * 128 + 128)
        edge[0, v], edge[1, v] = columns(flags, pair, next_pair, part)
        for r in range(rows):
            f32s[r, v, 14:16] = edge[0, v, 2 * r : 2 * r + 2]
            f32s[r, v, 16 + cols : 18 + cols] = edge[1, v, 2 * r : 2 * r + 2]
    for v in range(2):
        f32s[:, v, 16 : 16 + cols] = feat[:, :, v * 128 : v * 128 + 128].astype(F32)
    taps(f32s, x_out, rows, 5)
    keep = pltpu.make_async_copy(x_out.at[:, 0:pairs, chans : 5 * chans], x_hbm, sems.at[0])
    keep.start()
    for i, r in enumerate((0, 1, rows - 2, rows - 1)):
        rim[i] = x_out[r, :, 0 : 4 * chans]
    n = rows - 2
    for out, lo in ((hq_out, 0), (he_out, chans)):
        acc = None
        for a in range(3):
            lhs = x_out[a : a + n, :, lo : lo + 3 * chans].reshape(n * J, 3 * chans)
            term = dot(lhs, w[a])
            acc = term if acc is None else acc + term
        out[...] = acc.astype(BF).reshape(n, J, chans)
    sums, squares = moments(((hq_out, range(n)), (he_out, range(n))), cols)
    vec_out[0:1] = sums
    vec_out[1:2] = squares
    keep.wait()


def outer_kernel(
    cols, flags, near, far, rim, hq_in, he_in, vec, w, x_hbm, hq_out, he_out, stat_out, f32s, edge, x_out, sems
):
    rows = hq_in.shape[0] + 2
    chans = hq_in.shape[2]
    pairs = cols // 2
    f32s[:, :, 16 + cols : 56 + cols] = jnp.zeros((4, 2, 40, 128), F32)
    for v in range(2):
        part = slice(v * 128, v * 128 + 128)
        for k, side in enumerate(sides(flags, near, far)):
            edge[k, v] = side(2 * cols + pairs, 2 * cols + pairs + 16, part)
            for q in range(2):
                row = q + 2 * k
                f32s[row, v, 16 : 16 + cols] = side(q * cols, (q + 1) * cols, part)
                f32s[row, v, 14:16] = edge[k, v, 2 * q : 2 * q + 2]
                f32s[row, v, 16 + cols : 18 + cols] = edge[k, v, 4 + 2 * q : 6 + 2 * q]
    taps(f32s, x_out, 4, 5)
    copies = []
    for i, r in enumerate((1, 2)):
        copies.append(pltpu.make_async_copy(x_out.at[r, 0:pairs, chans : 5 * chans], x_hbm.at[i], sems.at[i]))
        copies[-1].start()
    hq_out[2:rows] = hq_in[...]
    he_out[2:rows] = he_in[...]
    wanted = (
        ((x_out, 0), (x_out, 1), (rim, 2), (rim, 3)),
        ((x_out, 1), (rim, 0), (rim, 3), (x_out, 2)),
        ((rim, 0), (rim, 1), (x_out, 2), (x_out, 3)),
    )
    for k, out in enumerate((hq_out, he_out)):
        lo = k * chans
        acc = None
        for a in range(3):
            lhs = jnp.concatenate([ref[r, :, lo : lo + 3 * chans] for ref, r in wanted[a]], axis=0)
            term = dot(lhs, w[a])
            acc = term if acc is None else acc + term
        value = acc.astype(BF).reshape(4, J, chans)
        out[0:2] = value[0:2]
        out[rows : rows + 2] = value[2:4]
    edges = (1, rows)
    sums, squares = moments(((hq_out, edges), (he_out, edges)), cols)
    n_in = (rows - 2) * cols * WIDTH
    n_out = 2 * cols * WIDTH
    n = n_in + n_out
    gap = vec[0:1] / n_in - sums / n_out
    (means,) = spread_dot(table(chans, 128, WIDTH, 1, 0), vec[0:1] + sums)
    within, gaps = spread_dot(table(chans, 128, WIDTH, 1, -32), vec[1:2] + squares, gap)
    stat = means / n + within + (n_in * n_out / n) * gaps * gaps
    stat_out[...] = jnp.broadcast_to(stat[None], stat_out.shape)
    for copy in copies:
        copy.wait()


def merged_sums(rec, out):
    out[...] = jnp.broadcast_to(jnp.sum(rec[...], axis=0)[None], out.shape)


def back_kernel(flags, cot, pair, next_pair, near, far, dw, hq, he, c_hbm, h_hbm, aq_out, ae_out, f32s, edge, c_out, sems):
    keep_h = [pltpu.make_async_copy(h, h_hbm.at[k], sems.at[1 + k]) for k, h in enumerate((hq, he))]
    for copy in keep_h:
        copy.start()
    half, pairs, chans = cot.shape
    rows = 2 * half
    cols = 2 * pairs
    f32s[:, 16 + pairs :] = jnp.zeros((half + 2, 16, chans), F32)
    edge[0], edge[1] = columns(flags, pair, next_pair)
    every = slice(None)
    for k, side in enumerate(sides(flags, near, far)):
        row = k * (half + 1)
        f32s[row, 16 : 16 + pairs] = side(2 * cols, 2 * cols + pairs, every)
        edge[2 + k, 0:16] = side(2 * cols + pairs, 2 * cols + pairs + 16, every)
        f32s[row, 15:16] = edge[2 + k, 8:9]
        f32s[row, 16 + pairs : 17 + pairs] = edge[2 + k, 9:10]
    f32s[1 : half + 1, 16 : 16 + pairs] = cot[...].astype(F32)
    for i in range(half):
        f32s[1 + i, 15:16] = edge[0, 2 * rows + i : 2 * rows + i + 1]
        f32s[1 + i, 16 + pairs : 17 + pairs] = edge[1, 2 * rows + i : 2 * rows + i + 1]
    for s in range(half + 2):
        c_out[s, :, 0:chans] = f32s[s, 15 : 15 + J].astype(BF)
        c_out[s, :, chans : 2 * chans] = f32s[s, 16 : 16 + J].astype(BF)
    keep = pltpu.make_async_copy(c_out, c_hbm, sems.at[0])
    keep.start()
    n = half + 1
    lo_l = c_out[0:n, :, 0:chans].reshape(n * J, chans)
    lo_r = c_out[0:n, :, chans:].reshape(n * J, chans)
    hi_l = c_out[1 : n + 1, :, 0:chans].reshape(n * J, chans)
    hi_r = c_out[1 : n + 1, :, chans:].reshape(n * J, chans)

    def put(out, k, value):
        value = value.astype(BF).reshape(n, J, chans)
        for i in range(n):
            out[2 * i + k] = value[i]

    put(ae_out, 1, dot_t(hi_r, dw[1, 1]))
    put(aq_out, 1, dot_t(hi_r, dw[1, 0]) + dot_t(hi_l, dw[1, 2]))
    put(ae_out, 0, dot_t(hi_r, dw[0, 1]) + dot_t(lo_r, dw[2, 1]))
    put(
        aq_out,
        0,
        dot_t(hi_r, dw[0, 0]) + dot_t(hi_l, dw[0, 2]) + dot_t(lo_r, dw[2, 0]) + dot_t(lo_l, dw[2, 2]),
    )
    keep.wait()
    for copy in keep_h:
        copy.wait()


def act_kernel(cells, flags, stats, hq, he, aq, ae, gain, bias, t_hbm, pq_hbm, pe_hbm, coef_out, sum_out, f32s, t_out, p_out, sems):
    devices = stats.shape[0]
    rows = hq.shape[0] - 2
    chans = hq.shape[2]
    count = float(cells * WIDTH)
    local_n = count / devices
    rec = stats[...]
    total = jnp.sum(rec, axis=0)
    centre = total / devices
    dev = rec - centre[None]
    between = jnp.sum(dev * dev, axis=0)
    mean, gaps = spread_dot(table(128, chans, 1, WIDTH, 0), centre, between)
    (within,) = spread_dot(table(128, chans, 1, WIDTH, 32), total)
    var = (within + local_n * gaps) / count
    inverse = lax.rsqrt(var + EPS)
    coef_out[0:1] = mean
    coef_out[1:2] = inverse
    g = gain[...]
    b = bias[...]
    odd, even = masks()
    top = jnp.where(flags[0] == 1, 0.0, 1.0)
    bias_sum = jnp.zeros((1, chans), F32)
    gain_sum = jnp.zeros((1, chans), F32)
    copies = []
    for k, (h, a, mask) in enumerate(((hq, aq, odd), (he, ae, even))):
        is_q = k == 0
        acc_b = jnp.zeros((J, chans), F32)
        acc_g = jnp.zeros((J, chans), F32)
        for r in range(rows + 2):
            normed = (h[r].astype(F32) - mean) * inverse
            shifted = g * normed + b
            sigma = 0.5 + 0.5 * jnp.tanh(0.5 * shifted)
            pre = a[r].astype(F32) * sigma * (1.0 + shifted * (1.0 - sigma))
            p_out[k, r] = pre
            dest = pq_hbm if is_q else pe_hbm
            copies.append(pltpu.make_async_copy(p_out.at[k, r], dest.at[r], sems.at[len(copies)]))
            copies[-1].start()
            if 1 <= r <= rows:
                acc_b = acc_b + pre
                acc_g = acc_g + pre * normed
            if r <= rows:
                active = shifted * sigma
                if r == 0:
                    active = active * top
                if is_q:
                    f32s[...] = active.astype(BF).astype(F32)
                    t_out[r, :, 0:chans] = active[0:64].astype(BF)
                    t_out[r, :, 2 * chans :] = f32s[1:65].astype(BF)
                else:
                    t_out[r, :, chans : 2 * chans] = active[0:64].astype(BF)
                    copies.append(pltpu.make_async_copy(t_out.at[r], t_hbm.at[r], sems.at[len(copies)]))
                    copies[-1].start()
        bias_sum = bias_sum + jnp.sum(acc_b * mask, axis=0, keepdims=True)
        gain_sum = gain_sum + jnp.sum(acc_g * mask, axis=0, keepdims=True)
    payload = jnp.concatenate(
        [bias_sum[:, 0:128], bias_sum[:, 128:256], gain_sum[:, 0:128], gain_sum[:, 128:256]], axis=0
    )
    sum_out[...] = jnp.broadcast_to(payload[None], sum_out.shape)
    for copy in copies:
        copy.wait()


def halves(flags, full, keep, send):
    n = keep.shape[0]
    core = flags[2]
    keep[...] = full[pl.ds(pl.multiple_of(core * n, n), n)]
    send[...] = full[pl.ds(pl.multiple_of((1 - core) * n, n), n)].astype(BF)


def down_kernel(flags, t_hbm, c_hbm, dw_hbm, out, keep, send, t, c, dw, grad, sems):
    half = out.shape[0]
    pairs, chans = out.shape[1:]
    sources = ((t_hbm, t), (c_hbm, c), (dw_hbm, dw))
    loads = [pltpu.make_async_copy(src, dst, sems.at[i]) for i, (src, dst) in enumerate(sources)]
    for load in loads:
        load.start()
    for load in loads:
        load.wait()
    cot = c[1 : half + 1, 0:pairs, chans:].reshape(half * pairs, chans)
    acc = None
    for a in range(3):
        lhs = jnp.concatenate([t[2 * i + a] for i in range(half)], axis=0)
        term = dot(lhs, dw[a])
        acc = term if acc is None else acc + term
        grad[a * 3 * chans : (a + 1) * 3 * chans] = t_dot(lhs, cot)
    out[...] = acc.astype(BF).reshape(out.shape)
    halves(flags, grad, keep, send)


def grad_kernel(
    cells, flags, sums, coef, gain, pq, h_in, pe_hbm, x_hbm, rim_hbm, h4_hbm, keep, send, vec_out, f32s, conv_out, pe, x, h4_out, sems
):
    rows = pq.shape[0] - 2
    chans = pq.shape[2]
    loads = []
    loads.append(pltpu.make_async_copy(pe_hbm, pe, sems.at[0]))
    loads[0].start()
    load_x = []
    for src, dst in ((x_hbm, x.at[1 : rows + 1]), (rim_hbm.at[0], x.at[0]), (rim_hbm.at[1], x.at[rows + 1])):
        load_x.append(pltpu.make_async_copy(src, dst, sems.at[len(loads) + len(load_x)]))
        load_x[-1].start()
    first_out = len(loads) + len(load_x)
    copies = []
    count = float(cells * WIDTH)
    total = jnp.sum(sums[...], axis=0)
    bias_sum = jnp.concatenate([total[0:1], total[1:2]], axis=1)
    gain_sum = jnp.concatenate([total[2:3], total[3:4]], axis=1)
    factor = 1.0 / math.sqrt(cells)
    vec_out[0:1] = gain_sum * factor
    vec_out[1:2] = bias_sum * factor
    g = gain[...]
    first, second = spread_dot(table(chans, chans, WIDTH, WIDTH, 0), g * bias_sum, g * gain_sum)
    first = first / count
    second = second / count
    mean = coef[0:1]
    inverse = coef[1:2]
    top = jnp.where(flags[0] == 1, 0.0, 1.0)
    bottom = jnp.where(flags[1] == 1, 0.0, 1.0)
    for k in range(2):
        is_q = k == 0
        p_in = pq if is_q else pe
        if not is_q:
            loads[0].wait()
        for r in range(rows + 2):
            normed = (h_in[k, r].astype(F32) - mean) * inverse
            value = inverse * (g * p_in[r] - first - normed * second)
            if r == 0:
                value = value * top
            if r == rows + 1:
                value = value * bottom
            rounded = value.astype(BF)
            f32s[...] = rounded.astype(F32)
            moved = f32s[1:65].astype(BF)
            lo = 3 if is_q else 2
            h4_out[r, :, lo * chans : (lo + 1) * chans] = rounded[0:64]
            lo = 1 if is_q else 0
            h4_out[r, :, lo * chans : (lo + 1) * chans] = moved
            if not is_q:
                copies.append(pltpu.make_async_copy(h4_out.at[r], h4_hbm.at[r], sems.at[first_out + r]))
                copies[-1].start()
    for load in load_x:
        load.wait()
    pairs = h4_out.shape[1]
    cells_here = rows * pairs
    odd = h4_out[1 : rows + 1, :, chans : 2 * chans].reshape(cells_here, chans)
    even = h4_out[1 : rows + 1, :, 2 * chans : 3 * chans].reshape(cells_here, chans)
    for a in range(3):
        lhs = x[a : a + rows].reshape(cells_here, 4 * chans)
        part = t_dot(lhs[:, 0 : 3 * chans], even) + t_dot(lhs[:, chans : 4 * chans], odd)
        conv_out[a * 3 * chans : (a + 1) * 3 * chans] = part
    halves(flags, conv_out, keep, send)
    for copy in copies:
        copy.wait()


def input_kernel(h4_hbm, w_hbm, out, f32s, h4, w, sems):
    rows, cols, chans = out.shape
    loads = [pltpu.make_async_copy(h4_hbm, h4, sems.at[0]), pltpu.make_async_copy(w_hbm, w, sems.at[1])]
    for load in loads:
        load.start()
    for load in loads:
        load.wait()
    for k, lo in ((0, 1), (1, 0)):
        acc = None
        for a in range(3):
            for b in range(3):
                lane = (lo + b) * chans
                lhs = h4[2 - a : 2 - a + rows, :, lane : lane + chans].reshape(rows * (cols // 2), chans)
                term = dot_t(lhs, w[a, b])
                acc = term if acc is None else acc + term
        acc = acc.reshape(rows, cols // 2, chans)
        for r in range(rows):
            for v in range(2):
                f32s[r, v, pl.ds(k, cols // 2, stride=2), :] = acc[r, :, v * 128 : v * 128 + 128]
    for v in range(2):
        out[:, :, v * 128 : v * 128 + 128] = f32s[:, v, 0:cols].astype(BF)


def join_kernel(conv_keep, conv_other, down_keep, down_other, out, both, sems):
    n = conv_keep.shape[0]
    step = n // 2
    copies = []
    for k, (keep, other) in enumerate(((down_keep, down_other), (conv_keep, conv_other))):
        for q in range(2):
            part = slice(q * step, (q + 1) * step)
            o = (1 - k) * n + q * step
            both[o : o + step] = (keep[part] + other[part].astype(F32)).astype(BF)
            copies.append(pltpu.make_async_copy(both.at[o : o + step], out.at[o : o + step], sems.at[2 * k + q]))
            copies[-1].start()
    for copy in copies:
        copy.wait()


def unpack_rows(core, rows, conv, down, f32s, sems):
    n = rows.shape[0] // 2
    step = n // 6
    base = pl.multiple_of(core * n, n)
    copies = []
    for k, dst in enumerate((conv, down)):
        for q in range(6):
            o = k * n + q * step
            f32s[o : o + step] = rows[o : o + step].astype(F32)
            part = dst.at[pl.ds(base + q * step, step)]
            copies.append(pltpu.make_async_copy(f32s.at[o : o + step], part, sems.at[k * 6 + q]))
            copies[-1].start()
    for copy in copies:
        copy.wait()


def unpack_own(flags, rows, conv, down, f32s, sems):
    unpack_rows(flags[2], rows, conv, down, f32s, sems)


def unpack_other(flags, rows, conv_in, down_in, conv, down, f32s, sems):
    unpack_rows(1 - flags[2], rows, conv, down, f32s, sems)


def core_swap(value):
    return lax.ppermute(value, "core", [(0, 1), (1, 0)])


def local(features, conv_weight, down_weight, norm_gain, norm_bias, cotangent):
    rows, cols, chans = features.shape
    half, pairs, _ = cotangent.shape
    devices = lax.axis_size(ALL)
    lats = lax.axis_size(LAT)
    cells = rows * cols * devices
    factor = 1.0 / math.sqrt(cells)
    lat = lax.axis_index(LAT)
    odd = lax.axis_index(LON) % 2 == 1
    flags = jnp.stack([lat == 0, lat == lats - 1, lax.axis_index("core") == 1, odd]).astype(jnp.int32)
    gain = norm_gain.reshape(1, chans)
    bias = norm_bias.reshape(1, chans)
    w3 = conv_weight.reshape(3, 3 * chans, chans)
    dw3 = down_weight.reshape(3, 3 * chans, chans)
    all_rows = 9 * chans
    few = lax.axis_size(FEW)
    rest = lax.axis_size(REST)

    with jax.named_scope("halo"):
        slab = (2 * rows + 16, chans)
        (edges,) = call(
            pack_lon,
            [((2,) + slab, BF)],
            [((2, rows, 16, chans), BF), ((2, half, 16, chans), BF), (slab, F32)],
            n_in=2,
            hbm=(0, 1),
            sems=4,
        )(pinned(features), pinned(cotangent))
        lons = lax.axis_size(LON)
        pair = lax.ppermute(edges, LON, [(i, i ^ 1) for i in range(lons)])
        next_pair = lax.ppermute(edges, LON, [(i, (i + 2 * (i % 2) - 1) % lons) for i in range(lons)])
        feat, cot, w_in = call(
            fetch, [(features.shape, BF), (cotangent.shape, BF), (w3.shape, BF)], n_in=3, hbm=(0, 1, 2), sems=3
        )(pinned(features), pinned(cotangent), pinned(w3))
        strip = (2 * cols + pairs + 16, chans)
        to_near, to_far = call(
            pack_lat,
            [(strip, BF)] * 2,
            [(slab, F32), (slab, F32), ((2, 16, chans), F32)],
            n_in=5,
            smem=(0,),
        )(flags, feat, cot, pair, next_pair)
        near = lax.ppermute(to_near, LAT, [(i, i ^ 1) for i in range(lats)])
        gaps = range(1, lats - 1, 2)
        far = lax.ppermute(to_far, LAT, [(i, i + 1) for i in gaps] + [(i + 1, i) for i in gaps])

    plane = (rows + 2, J, chans)
    x_shape = (rows, pairs, 4 * chans)
    rim_shape = (2, pairs, 4 * chans)
    inner_plane = (rows - 2, J, chans)
    with jax.named_scope("conv"):
        x, rim, hq_in, he_in, vec = call(
            inner_kernel,
            [(x_shape, BF, True), ((4, J, 4 * chans), BF), (inner_plane, BF), (inner_plane, BF), ((2, chans), F32)],
            [
                ((rows, 2, cols + 56, 128), F32),
                ((2, 2, slab[0], 128), F32),
                ((rows, J, 5 * chans), BF),
            ],
            flops=2 * 960 * 2304 * 256,
            n_in=5,
            smem=(0,),
            sems=1,
        )(flags, feat, pair, next_pair, w_in)
        x_rim, hq, he, stat = call(
            functools.partial(outer_kernel, cols),
            [(rim_shape, BF, True), (plane, BF), (plane, BF), ((devices, 1, 128), F32)],
            [
                ((4, 2, cols + 56, 128), F32),
                ((2, 2, 16, 128), F32),
                ((4, J, 5 * chans), BF),
            ],
            flops=2 * 640 * 2304 * 256,
            n_in=8,
            smem=(0,),
            sems=2,
        )(flags, near, far, rim, hq_in, he_in, vec, w_in)
        stats = lax.all_to_all(stat, ALL, 0, 0, tiled=True)
    c_shape = (half + 2, J, 2 * chans)
    with jax.named_scope("back"):
        c2, h, aq, ae = call(
            back_kernel,
            [(c_shape, BF, True), ((2,) + plane, BF, True), (plane, BF), (plane, BF)],
            [((half + 2, pairs + 32, chans), F32), ((4,) + slab, F32), (c_shape, BF)],
            flops=2 * 400 * 2304 * 256,
            n_in=9,
            smem=(0,),
            sems=3,
        )(flags, cot, pair, next_pair, near, far, down_weight, hq, he)
    t_shape = (rows + 1, pairs, 3 * chans)
    with jax.named_scope("act"):
        t, pq, pe, coef, sums = call(
            functools.partial(act_kernel, cells),
            [(t_shape, BF, True), (plane, F32, True), (plane, F32, True), ((2, chans), F32), ((few, 4, 128), F32)],
            [((J, chans), F32), (t_shape, BF), ((2,) + plane, F32)],
            flops=1600 * 256 * 20,
            smem=(0,),
            n_in=8,
            sems=3 * rows + 5,
        )(flags, stats, hq, he, aq, ae, gain, bias)
        sums = lax.all_to_all(sums, FEW, 0, 0, tiled=True)
        (sums,) = call(merged_sums, [((rest, 4, 128), F32)], n_in=1)(sums)
        sums, c2 = lax.optimization_barrier((sums, c2))
        sums = lax.all_to_all(sums, REST, 0, 0, tiled=True)
    half_rows = (all_rows // 2, chans)
    with jax.named_scope("down"):
        output, down_keep, down_send = call(
            down_kernel,
            [((half, pairs, chans), BF), (half_rows, F32), (half_rows, BF)],
            [(t_shape, BF), (c_shape, BF), (dw3.shape, BF), ((all_rows, chans), F32)],
            flops=4 * 256 * 2304 * 256,
            smem=(0,),
            hbm=(1, 2, 3),
            n_in=4,
            sems=3,
        )(flags, pinned(t), pinned(c2), pinned(dw3))
        down_other = core_swap(down_send)
    h4_shape = (rows + 2, pairs, 4 * chans)
    with jax.named_scope("grad"):
        h4, conv_keep, conv_send, vec = call(
            functools.partial(grad_kernel, cells),
            [(h4_shape, BF, True), (half_rows, F32), (half_rows, BF), ((2, chans), F32)],
            [
                ((J, chans), F32),
                ((all_rows, chans), F32),
                (plane, F32),
                ((rows + 2, pairs, 4 * chans), BF),
                (h4_shape, BF),
            ],
            flops=2 * 1600 * 2304 * 256,
            smem=(0,),
            hbm=(6, 7, 8),
            n_in=9,
            sems=3 * (rows + 2) + 3,
        )(flags, sums, coef, gain, pq, h, pinned(pe), pinned(x), pinned(x_rim))
    with jax.named_scope("input"):
        (input_grad,) = call(
            input_kernel,
            [((rows, cols, chans), BF)],
            [((rows, 2, cols + 8, 128), F32), (h4_shape, BF), (conv_weight.shape, BF)],
            flops=2 * 1024 * 2304 * 256,
            n_in=2,
            hbm=(0, 1),
            sems=2,
        )(pinned(h4), pinned(conv_weight))
    with jax.named_scope("total"):
        whole_rows = (all_rows, chans)
        (mine,) = call(
            join_kernel, [(whole_rows, BF, True)], [(whole_rows, BF)], n_in=4, sems=4
        )(conv_keep, core_swap(conv_send), down_keep, down_other)
        chips = lax.axis_size(NEAR)
        share = all_rows // chips
        got = lax.all_to_all(mine.reshape(chips, share, chans), NEAR, 0, 0, tiled=True)
        got, input_grad = lax.optimization_barrier((got, input_grad))
        piece = jnp.sum(got.astype(F32), axis=0).astype(BF)
        got = lax.all_to_all(
            jnp.broadcast_to(piece[None], (lax.axis_size("z_hi"), share, chans)), "z_hi", 0, 0, tiled=True
        )
        piece = (jnp.sum(got.astype(F32), axis=0) * factor).astype(BF)
        whole = lax.all_to_all(jnp.broadcast_to(piece[None], (chips, share, chans)), NEAR, 0, 0, tiled=True)
        whole = whole.reshape(all_rows, chans)
        other = core_swap(whole)
        flat = (whole_rows, F32, True)
        room = [(whole_rows, F32)]
        conv_grad, down_grad = call(unpack_own, [flat, flat], room, smem=(0,), n_in=2, sems=12)(flags, whole)
        conv_grad, down_grad = call(
            unpack_other, [flat, flat], room, smem=(0,), hbm=(2, 3), n_in=4, sems=12, aliases={2: 0, 3: 1}
        )(flags, other, pinned(conv_grad), pinned(down_grad))
    shape = (3, 3, chans, chans)
    return output, input_grad, conv_grad.reshape(shape), down_grad.reshape(shape), vec[0], vec[1]


SIZES = {64: (4, 4, 2, 2), 2: (1, 1, 2, 1), 4: (2, 1, 2, 1), 8: (1, 2, 2, 2)}


def solution(mesh):
    lon, lat = mesh.devices.shape
    fine = Mesh(mesh.devices.reshape(SIZES[lon] + (lat // 2, 2)), ALL)
    band = P(LAT, LON, None)
    return jax.shard_map(
        local,
        mesh=fine,
        in_specs=(band, P(), P(), P(), P(), band),
        out_specs=(band, band, P(), P(), P(), P()),
        check_vma=False,
    )
```
